32 devices in a mesh: tile: 8 (over z, y), flow: 4 (over x, core).
Axes of the slice: x: 2, y: 2, z: 4, core: 2. Of those that a mesh axis runs over, the one named last changes fastest.
Arguments:
- density: float32 [64, 1024, 512], P(None, 'tile', 'flow'), may hold values from 0 to 2
- habitat_class: int32 [1024, 512], P('tile', 'flow'), may hold values from 0 to 15
- suitability: float32 [16], replicated, may hold values from 0.2 to 1
- dispersal_draw: bfloat16 [64, 1024, 512], P(None, 'tile', 'flow'), may hold values from 0 to 1
- threshold: float32 [1024, 512], P('tile', 'flow'), may hold values from 0.2 to 0.8
- hub_row: int32 [4, 128], P('flow', 'tile'), may hold values from 0 to 127
- dest_tile: int32 [4, 128, 1], P('flow', 'tile'), may hold values from 0 to 7; in each aligned block of 16 rows (0 to 15, 16 to 31, ..., all dimensions but the last counted through in order) at most 4 rows name the same one
- dest_row: int32 [4, 128], P('flow', 'tile'), may hold values from 0 to 127
- county_id: int32 [4, 128], P('flow', 'tile'), may hold values from 0 to 15
- jump_share: float32 [4, 128], P('flow', 'tile'), may hold values from 0.1 to 0.4
- flow_tiles: bfloat16 [16, 128, 128], P('flow'), may hold values from 0 to 0.019897461
- flow_scale: bfloat16 [16], P('flow'), may hold values from 0.5 to 2
Outputs:
- density_next: float32 [64, 1024, 512], P(None, 'tile', 'flow')
The draws below stay inside these ranges and needn't reach their ends.
Inputs may be any that keep to these rules, and one draw needn't show every extreme that they name: `dest_tile`: among the 16 hubs of one device, at most 4 reach the same band, and in every draw some band gets exactly 4 of them.
All inputs are finite; a program needn't handle non-finite values.
Results may differ from the reference program's by a relative error of at most 0.00043.
Values may be sent and summed in bfloat16 or wider, within the bound.
No kernel may reach another device: no remote copies, remote signals or barrier semaphores. Data moves between devices by JAX's collectives and lax.ppermute only.
A program may use at most 64 MiB of HBM per device.

```python
import math
import jax
import jax.numpy as jnp
import numpy as np

MEMBERS = 64
CC = 128
CR = 128
STEPS = 2
CAP = 4
CLASSES = 16
HUBS = 16
COUNTIES = 16
NR = 1024
NC = 512
N_TILE = 8
N_FLOW = 4


def place_ends(result, key, least, top_value):
    extent = result.shape
    index_at = [jax.random.randint(jax.random.fold_in(key, axis), (), 0, extent[axis]) for axis in range(len(extent))]
    result = result.at[tuple(index_at)].set(least)
    longest = extent.index(max(extent))
    index_at[longest] = (index_at[longest] + 1) % extent[longest]
    return result.at[tuple(index_at)].set(top_value)


def steps_of(own_key, dims, split, smallest, top_value):
    def one(dim, parts):
        steps = jax.random.uniform(jax.random.fold_in(jax.random.fold_in(own_key, 6), dim), (parts,), jnp.float32, smallest / len(split), top_value / len(split))
        return jnp.repeat(jnp.exp(steps), dims[dim] // parts).reshape((-1,) + (1,) * (len(dims) - dim - 1))

    loudness = one(*split[0])
    for cut in split[1:]:
        loudness = loudness * one(*cut)
    return loudness


def deal_out(stream_key, own, number, rows, number_of, top, most, skew):
    order = jax.random.permutation(stream_key, number_of)
    crowded, usual = shares(number_of, rows * top, most, skew, True), shares(number_of, rows * top, most, skew, False)
    places = jnp.arange(number_of)

    def named(tallies, turn):
        used = int((tallies > 0).sum())
        fixed = max(1, used // 4)
        shifted = fixed + (places - fixed + turn * (used - fixed)) % max(1, number_of - fixed)
        return jnp.zeros((number_of,), jnp.int32).at[order[jnp.where(places < fixed, places, shifted)]].set(jnp.asarray(tallies, jnp.int32))

    tallies = jnp.where(number % 4 == 0, named(crowded, number // 4), named(usual, number - number // 4 - 1))
    mixed = jax.random.permutation(jax.random.fold_in(own, 3), number_of)
    donor, sink = mixed[0:number_of // 2 * 2:2], mixed[1:number_of // 2 * 2:2]
    slack = jnp.minimum(tallies[donor] - 1, most - tallies[sink]) // 2
    slack = jnp.where((donor == order[0]) | (sink == order[0]) | (tallies[sink] == 0), 0, jnp.maximum(slack, 0))
    shifted = jax.random.randint(jax.random.fold_in(own, 4), (number_of // 2,), 0, 1 << 20) % (slack + 1)
    tallies = tallies.at[donor].add(-shifted).at[sink].add(shifted)
    members = jnp.searchsorted(jnp.cumsum(tallies), jnp.arange(rows * top), side="right").astype(jnp.int32)
    table = members.reshape(top, rows).T
    table = table[jax.random.permutation(jax.random.fold_in(own, 1), rows)]
    turn = jax.random.randint(jax.random.fold_in(own, 2), (rows, 1), 0, top)
    return jnp.take_along_axis(table, (jnp.arange(top)[None, :] + turn) % top, axis=1)


def shares(number_of, total, limit, skew, full):
    portions = [(1 << 20) // math.isqrt(rank ** skew) + 1 for rank in range(1, number_of + 1)]
    largest = limit if full else min(limit, max(-(-total // number_of), total * portions[0] // sum(portions)))
    least = 1 if total - largest >= number_of - 1 else 0
    counts, surplus = [largest] + [least] * (number_of - 1), total - largest - least * (number_of - 1)
    while surplus > 0:
        free = [i for i in range(1, number_of) if counts[i] < largest] or [i for i in range(1, number_of) if counts[i] < limit]
        whole, left = sum([portions[i] for i in free]), surplus
        for i in free:
            extra = min(limit - counts[i], max(1, left * portions[i] // whole), surplus)
            counts[i] = counts[i] + extra
            surplus = surplus - extra
    return np.array(counts)


def setup_inputs(seed: int = 0) -> dict:
    splits = jax.random.split(jax.random.key(seed), 13)
    density = jnp.clip(2.0 * jax.random.uniform(splits[0], (MEMBERS, NR, NC), jnp.float32) ** steps_of(splits[0], (MEMBERS, NR, NC), ((1, 8), (2, 4)), -0.2, 0.2), 0.0, 2.0)
    habitat_class = place_ends(jax.random.randint(splits[1], (NR, NC), 0, CLASSES), jax.random.fold_in(splits[1], 1), 0, CLASSES - 1).astype(jnp.int32)
    suitability = jnp.clip(jnp.exp(jax.random.uniform(splits[2], (CLASSES,), jnp.float32, math.log(0.2), math.log(1.0))), 0.2, 1.0)
    dispersal_draw = jnp.clip(1.0 * jax.random.uniform(splits[3], (MEMBERS, NR, NC), jnp.float32) ** steps_of(splits[3], (MEMBERS, NR, NC), ((1, 8), (2, 4)), -0.2, 0.2), 0.0, 1.0).astype(jnp.bfloat16)
    threshold = jnp.clip(0.2 + 0.6 * jax.random.uniform(splits[4], (NR, NC), jnp.float32) ** steps_of(splits[4], (NR, NC), ((0, 8), (1, 4)), -0.2, 0.2), 0.2, 0.8)
    hub_row = place_ends(jax.random.randint(splits[5], (N_FLOW, N_TILE * HUBS), 0, CR), jax.random.fold_in(splits[5], 1), 0, CR - 1).astype(jnp.int32)
    dest_tile_keys = jax.random.split(jax.random.fold_in(splits[6], 1), N_FLOW * (N_TILE * HUBS) // HUBS)
    dest_tile_turns = jax.random.permutation(jax.random.fold_in(splits[6], 3), N_FLOW * (N_TILE * HUBS) // HUBS)
    dest_tile = jax.vmap(lambda own, number: deal_out(jax.random.fold_in(splits[6], 2), own, number, HUBS, N_TILE, 1, CAP, 2))(dest_tile_keys, dest_tile_turns).reshape((N_FLOW, N_TILE * HUBS, 1))
    dest_row = place_ends(jax.random.randint(splits[7], (N_FLOW, N_TILE * HUBS), 0, CR), jax.random.fold_in(splits[7], 1), 0, CR - 1).astype(jnp.int32)
    county_id = place_ends(jax.random.randint(splits[8], (N_FLOW, N_TILE * HUBS), 0, COUNTIES), jax.random.fold_in(splits[8], 1), 0, COUNTIES - 1).astype(jnp.int32)
    jump_share = jnp.clip(0.1 + 0.3 * jax.random.uniform(splits[9], (N_FLOW, N_TILE * HUBS), jnp.float32) ** steps_of(splits[9], (N_FLOW, N_TILE * HUBS), ((0, 4), (1, 8)), -0.2, 0.2), 0.1, 0.4)
    flow_tiles = jnp.clip(0.019897461 * jax.random.uniform(splits[10], (COUNTIES, CC, CC), jnp.float32) ** steps_of(splits[10], (COUNTIES, CC, CC), ((0, 4),), -0.2, 0.2), 0.0, 0.019897461).astype(jnp.bfloat16)
    flow_scale = jnp.clip(jnp.exp(math.log(2.0) - 1.3862944 * jax.random.uniform(splits[11], (COUNTIES,), jnp.float32) ** steps_of(splits[11], (COUNTIES,), ((0, 4),), -0.2, 0.2)), 0.5, 2.0).astype(jnp.bfloat16)
    return {"density": density, "habitat_class": habitat_class, "suitability": suitability, "dispersal_draw": dispersal_draw, "threshold": threshold, "hub_row": hub_row, "dest_tile": dest_tile, "dest_row": dest_row, "county_id": county_id, "jump_share": jump_share, "flow_tiles": flow_tiles, "flow_scale": flow_scale}


KAPPA = 0.24
SHARPNESS = 8.0


def relax(padded, centre_weight):
    centre = padded[:, 1:-1, 1:-1]
    beside_all = padded[:, 2:, 1:-1] + padded[:, :-2, 1:-1] + padded[:, 1:-1, 2:] + padded[:, 1:-1, :-2]
    return centre + KAPPA * centre_weight * (beside_all - 4.0 * centre)


def reference(density, habitat_class, suitability, dispersal_draw, threshold, hub_row, dest_tile, dest_row, county_id, jump_share, flow_tiles, flow_scale):
    weight = jnp.take(suitability, habitat_class, axis=0)
    field = density
    for step in range(STEPS):
        padded = jnp.pad(field, ((0, 0), (1, 1), (1, 1)))
        field = relax(padded, weight)
    strips = []
    index = jnp.arange(N_TILE * HUBS, dtype=jnp.int32)
    for column in range(N_FLOW):
        strip = field[:, :, column * CC:(column + 1) * CC]
        source = (index // HUBS) * CR + hub_row[column]
        target = dest_tile[column, :, 0] * CR + dest_row[column]
        picked = strip[:, source, :]
        moved = jump_share[column][None, :, None] * picked
        outgoing = moved.astype(jnp.bfloat16)
        county = county_id[column]
        tiles = jnp.take(flow_tiles, county, axis=0).astype(jnp.float32)
        scales = jnp.take(flow_scale, county, axis=0).astype(jnp.float32)
        carried = jnp.einsum("mhk,hkj->mhj", outgoing.astype(jnp.float32), tiles) * scales[None, :, None]
        carried = carried.astype(jnp.bfloat16)
        strip = strip.at[:, source, :].add(-moved)
        strip = strip.at[:, target, :].add(carried.astype(jnp.float32))
        strips.append(strip)
    jumped = jnp.concatenate(strips, axis=2)
    grow = jax.nn.sigmoid(SHARPNESS * (dispersal_draw.astype(jnp.float32) - threshold))
    return jumped * grow[:, :, :] if grow.ndim == 3 else jumped * grow
```

```python
import jax
import jax.numpy as jnp
from jax import lax
from jax.experimental import pallas as pl
from jax.experimental.pallas import tpu as pltpu
from jax.sharding import PartitionSpec as P

CAP = 4
KAPPA = 0.24
SHARPNESS = 8.0
PAD = 8
TAIL = 8
TAGS = 16
VMEM_BYTES = 24 * 1024 * 1024
F32 = jnp.float32
BF16 = jnp.bfloat16


def lanes(shape):
    return lax.broadcasted_iota(jnp.int32, shape, 1)


def sublanes(shape):
    return lax.broadcasted_iota(jnp.int32, shape, 0)


def column_to_row(column, shape):
    return jnp.sum(jnp.where(lanes(shape) == sublanes(shape), column, 0.0), axis=0, keepdims=True)


def row_to_column(row, shape):
    return jnp.sum(jnp.where(lanes(shape) == sublanes(shape), row, 0.0), axis=1, keepdims=True)


def edges_kernel(
    place, suit, density, habitat, tiles, scale,
    cols_a, cols_b, rows_a, rows_b, own, weight_out, tiles_out, acc_e, acc_o,
):
    step = pl.program_id(0)
    block, rows, cols = density.shape
    members = block * pl.num_programs(0)
    t_even = place[0] == 0
    f_even = place[1] == 0

    quad = lanes((8, cols)) // 4
    for k in range(rows // 8):
        at = pl.ds(8 * k, 8)
        even, odd = acc_e[at, :], acc_o[at, :]
        for j in range(block // 2):
            q = step * (block // 2) + j
            shift = 4 * q + 2
            hit = quad == q
            even = jnp.where(hit, pltpu.roll(density[2 * j, at, :], shift, 1), even)
            odd = jnp.where(hit, pltpu.roll(density[2 * j + 1, at, :], shift, 1), odd)
        acc_e[at, :] = even
        acc_o[at, :] = odd

    def copy_rows(out, start):
        for k in range(2):
            for j in range(block):
                out[pl.ds(k * members + step * block + j, 1), :] = density[j, pl.ds(start + k, 1), :]

    copy_rows(rows_a, jnp.where(t_even, rows - 2, 0))
    copy_rows(rows_b, jnp.where(t_even, 0, rows - 2))

    @pl.when(step == pl.num_programs(0) - 1)
    def _():
        shape = (rows, cols)
        low = lanes(shape) % 4 < 2
        even, odd = acc_e[...], acc_o[...]
        right = jnp.where(low, even, pltpu.roll(odd, 2, 1))
        left = jnp.where(low, pltpu.roll(even, cols - 2, 1), odd)
        own[...] = jnp.where(lanes(shape) % 2 == 0, pltpu.roll(right, cols - 1, 1), pltpu.roll(left, 1, 1))
        label = habitat[...]
        weight = jnp.zeros(shape, F32)
        for c in range(suit.shape[0]):
            weight = jnp.where(label == c, suit[c], weight)
        weight_out[...] = weight
        w_right = jnp.broadcast_to(column_to_row(weight[:, cols - 1:], shape), (TAIL, cols))
        w_left = jnp.broadcast_to(column_to_row(weight[:, :1], shape), (TAIL, cols))
        cols_a[:rows, :] = jnp.where(f_even, right, left)
        cols_b[:rows, :] = jnp.where(f_even, left, right)
        cols_a[rows:, :] = jnp.where(f_even, w_right, w_left)
        cols_b[rows:, :] = jnp.where(f_even, w_left, w_right)
        w_top = jnp.broadcast_to(weight[:1, :], (TAIL, cols))
        w_bottom = jnp.broadcast_to(weight[rows - 1:, :], (TAIL, cols))
        rows_a[2 * members:, :] = jnp.where(t_even, w_bottom, w_top)
        rows_b[2 * members:, :] = jnp.where(t_even, w_top, w_bottom)
        depth = tiles.shape[1]
        for c in range(tiles.shape[0]):
            tiles_out[c, :depth, :] = tiles[c]
            tiles_out[c, depth:, :] = jnp.broadcast_to(scale[:, c:c + 1].astype(F32), (TAGS, cols)).astype(BF16)


def corners_kernel(place, rows_a, rows_b, got_a, got_b, out_a, out_b):
    rows = got_a.shape[0] - TAIL
    cols = got_a.shape[1]
    messages = rows_a.shape[0] - TAIL
    t_even = place[0] == 0
    f_even = place[1] == 0
    odd_lane = lanes((8, cols)) % 2 == 1
    swap = odd_lane == f_even
    top = jnp.where(swap, got_b[:8, :], got_a[:8, :])[:1]
    bottom = jnp.where(swap, got_b[rows - 8:rows, :], got_a[rows - 8:rows, :])[7:]
    out_a[...] = rows_a[...]
    out_b[...] = rows_b[...]
    out_a[messages + 1:messages + 2, :] = jnp.where(t_even, bottom, top)
    out_b[messages + 1:messages + 2, :] = jnp.where(t_even, top, bottom)


def stencil_kernel(
    place, hub_row, dest_tile, dest_row, county, share,
    density, weight, own, cols_a, cols_b, rows_a, rows_b,
    diffused, sent, field, inner, halo0, halo1, edge_n, edge_s, counts, sem,
):
    members, rows, cols = density.shape
    high = field.shape[0] // members
    bands = counts.shape[0]
    copy = pltpu.make_async_copy(density, field.reshape(members, high, cols).at[:, PAD:PAD + rows, :], sem)
    copy.start()
    t_even = place[0] == 0
    f_even = place[1] == 0
    band = place[2]

    shape = (rows, cols)
    even_lane = lanes(shape) % 2 == 0
    a, b = cols_a[:rows, :], cols_b[:rows, :]
    from_e = jnp.where(f_even, a, b)
    from_w = jnp.where(f_even, b, a)
    near = jnp.where(even_lane, from_e, from_w)
    far = jnp.where(even_lane, pltpu.roll(from_e, cols - 1, 1), pltpu.roll(from_w, 1, 1))
    halo0[PAD:PAD + rows, :] = near
    tail_n = jnp.where(t_even, rows_b[2 * members:, :], rows_a[2 * members:, :])
    tail_s = jnp.where(t_even, rows_a[2 * members:, :], rows_b[2 * members:, :])
    halo0[PAD - 1:PAD, :] = tail_n[1:2]
    halo0[PAD + rows:PAD + rows + 1, :] = tail_s[1:2]
    wa = row_to_column(cols_a[rows:rows + 1, :], shape)
    wb = row_to_column(cols_b[rows:rows + 1, :], shape)
    w_e = jnp.where(f_even, wa, wb)
    w_w = jnp.where(f_even, wb, wa)
    w_packed = jnp.where(even_lane, w_e, w_w)
    around = halo0[PAD - 1:PAD + rows - 1, :] + halo0[PAD + 1:PAD + rows + 1, :] + far + own[...]
    halo1[...] = near + KAPPA * w_packed * (around - 4.0 * near)

    copy.wait()
    side = (members, cols)
    lane = lanes(side)
    twice = 2 * sublanes(side)

    def edge(tail, outer, centre, beyond, into):
        corner = jnp.broadcast_to(tail[1:2, :], side)
        east = jnp.sum(jnp.where(lane == twice, corner, 0.0), axis=1, keepdims=True)
        west = jnp.sum(jnp.where(lane == twice + 1, corner, 0.0), axis=1, keepdims=True)
        w = jnp.where(lane == 0, west, pltpu.roll(centre, 1, 1))
        e = jnp.where(lane == cols - 1, east, pltpu.roll(centre, cols - 1, 1))
        into[...] = centre + KAPPA * tail[0:1, :] * (outer + beyond + w + e - 4.0 * centre)

    n0 = jnp.where(t_even, rows_b[:members, :], rows_a[:members, :])
    n1 = jnp.where(t_even, rows_b[members:2 * members, :], rows_a[members:2 * members, :])
    s0 = jnp.where(t_even, rows_a[:members, :], rows_b[:members, :])
    s1 = jnp.where(t_even, rows_a[members:2 * members, :], rows_b[members:2 * members, :])
    field[pl.ds(PAD - 1, members, stride=high), :] = n1
    field[pl.ds(PAD + rows, members, stride=high), :] = s0
    edge(tail_n, n0, n1, field[pl.ds(PAD, members, stride=high), :], edge_n)
    edge(tail_s, s1, s0, field[pl.ds(PAD + rows - 1, members, stride=high), :], edge_s)

    lane8 = lanes((8, cols))
    first, last = lane8 == 0, lane8 == cols - 1

    def relax(ref, base, k, halo, shift, coef):
        start = base + PAD + 8 * k
        centre = ref[pl.ds(start, 8), :]
        n = ref[pl.ds(start - 1, 8), :]
        s = ref[pl.ds(start + 1, 8), :]
        h = pltpu.roll(halo, shift, 1)
        w = jnp.where(first, h, pltpu.roll(centre, 1, 1))
        e = jnp.where(last, h, pltpu.roll(centre, cols - 1, 1))
        return centre + coef * ((n + s) + (w + e) - 4.0 * centre)

    def one(m, slot):
        shift = cols - 1 - 2 * m
        base = pl.multiple_of(m * high, 8)
        low = slot * high
        inner[low + PAD - 1:low + PAD, :] = edge_n[pl.ds(m, 1), :]
        inner[low + PAD + rows:low + PAD + rows + 1, :] = edge_s[pl.ds(m, 1), :]
        for k in range(rows // 8):
            coef = KAPPA * weight[8 * k:8 * k + 8, :]
            inner[low + PAD + 8 * k:low + PAD + 8 * k + 8, :] = relax(
                field, base, k, halo0[PAD + 8 * k:PAD + 8 * k + 8, :], shift, coef)
        to = pl.multiple_of(m * rows, 8)
        for k in range(rows // 8):
            coef = KAPPA * weight[8 * k:8 * k + 8, :]
            diffused[pl.ds(to + 8 * k, 8), :] = relax(
                inner, low, k, halo1[8 * k:8 * k + 8, :], shift, coef)

    def pair(i, carry):
        one(2 * i, 0)
        one(2 * i + 1, 1)
        return carry

    lax.fori_loop(0, members // 2, pair, 0)

    stride = CAP * members + TAGS
    for t in range(bands):
        counts[t] = 0
    tag_lane = lanes((TAGS, cols))
    for t in range(bands):
        sent[t * stride + CAP * members:(t + 1) * stride, :] = jnp.full((TAGS, cols), -1.0, BF16)
    for h in range(hub_row.shape[0]):
        to = dest_tile[h]
        n = counts[to]
        counts[to] = n + 1
        moved = share[h] * diffused[pl.ds(hub_row[h], members, stride=rows), :]
        base = pl.multiple_of(to * stride, 16)
        sent[pl.ds(pl.multiple_of(base + n * members, 16), members), :] = moved.astype(BF16)
        at = pl.ds(pl.multiple_of(base + CAP * members, 16), TAGS)
        tags = sent[at, :].astype(F32)
        tags = jnp.where(tag_lane == n, dest_row[h].astype(F32), tags)
        tags = jnp.where(tag_lane == CAP + n, county[h].astype(F32), tags)
        sent[at, :] = tags.astype(BF16)


def grow_kernel(hub_row, share, diffused, draw, threshold, kept, grow, factor):
    step = pl.program_id(0)
    block, rows, cols = diffused.shape

    @pl.when(step == 0)
    def _():
        row = sublanes((rows, cols))
        left = jnp.ones((rows, cols), F32)
        for h in range(hub_row.shape[0]):
            left = left - jnp.where(row == hub_row[h], share[h], 0.0)
        factor[...] = left

    for j in range(block):
        x = 0.5 * SHARPNESS * (draw[j].astype(F32) - threshold[...])
        g = 0.5 * jnp.tanh(x) + 0.5
        grow[j] = g
        kept[j] = diffused[j] * factor[...] * g


def land_kernel(place, landed, kept, grow, *rest):
    blocks, (out, tags_v, tags_s, sem) = rest[:-4], rest[-4:]
    flow = place[3]
    per = blocks[0].shape[0]
    bands = tags_v.shape[0]
    cols = tags_v.shape[1]
    stride = landed.shape[0] // bands
    members = (stride - TAGS) // CAP
    rows = kept.shape[0] // members
    depth = blocks[0].shape[1] - TAGS
    for t in range(bands):
        tags = landed[t * stride + CAP * members:(t + 1) * stride, :].astype(F32)
        tags_v[t:t + 1, :] = tags[:1].astype(jnp.int32)
    copy = pltpu.make_async_copy(tags_v, tags_s, sem)
    copy.start()
    copy.wait()
    out[...] = kept[...]
    for t in range(bands):
        for n in range(CAP):
            row = tags_s[t, n]

            @pl.when(row >= 0)
            def _():
                c = tags_s[t, CAP + n]
                block = jnp.bitwise_xor(c // per, flow)
                c = c % per
                x = landed[t * stride + n * members:t * stride + (n + 1) * members, :]
                at = pl.ds(row, members, stride=rows)

                for i, ref in enumerate(blocks):
                    @pl.when(block == i)
                    def _():
                        product = jnp.dot(x, ref[c, :depth, :], preferred_element_type=F32)
                        scale = ref[c, depth:, :].astype(F32)[:1]
                        carried = (product * scale).astype(BF16).astype(F32)
                        out[at, :] = out[at, :] + carried * grow[at, :]


def smem():
    return pl.BlockSpec(memory_space=pltpu.SMEM)


def vmem():
    return pl.BlockSpec(memory_space=pltpu.VMEM)


def anywhere():
    return pl.BlockSpec(memory_space=pl.ANY)


def params():
    return pltpu.CompilerParams(vmem_limit_bytes=VMEM_BYTES)


def near_pairs(count):
    return [(i, i ^ 1) for i in range(count)]


def far_pairs(count):
    return [(i, j) for k in range(1, count - 1, 2) for i, j in ((k, k + 1), (k + 1, k))]


def local(
    density,
    habitat_class,
    suitability,
    dispersal_draw,
    threshold,
    hub_row,
    dest_tile,
    dest_row,
    county_id,
    jump_share,
    flow_tiles,
    flow_scale,
):
    members, rows, cols = density.shape
    bands, flows = lax.axis_size("tile"), lax.axis_size("flow")
    t, f = lax.axis_index("tile"), lax.axis_index("flow")
    place = jnp.stack([t % 2, f % 2, t, f]).astype(jnp.int32)
    hubs, share = hub_row.reshape(-1), jump_share.reshape(-1)
    sds = jax.ShapeDtypeStruct
    block = 8
    per = flow_tiles.shape[0]
    message = sds((rows + TAIL, cols), F32)
    strip = sds((2 * members + TAIL, cols), F32)
    whole = lambda *shape: pl.BlockSpec(shape, lambda i: (0,) * len(shape))
    cols_a, cols_b, rows_a, rows_b, own, weight, tiles = pl.pallas_call(
        edges_kernel,
        grid=(members // block,),
        out_shape=(message, message, strip, strip, sds((rows, cols), F32), sds((rows, cols), F32),
                   sds((per, flow_tiles.shape[1] + TAGS, cols), BF16)),
        in_specs=[smem(), smem(), pl.BlockSpec((block, rows, cols), lambda i: (i, 0, 0)), whole(rows, cols),
                  whole(*flow_tiles.shape), whole(1, per)],
        out_specs=(whole(*message.shape), whole(*message.shape), whole(*strip.shape), whole(*strip.shape),
                   whole(rows, cols), whole(rows, cols), whole(per, flow_tiles.shape[1] + TAGS, cols)),
        scratch_shapes=[pltpu.VMEM((rows, cols), F32), pltpu.VMEM((rows, cols), F32)],
        compiler_params=params(),
        name="edges",
    )(place, suitability, density, habitat_class, flow_tiles, flow_scale.reshape(1, -1))

    got_a = lax.ppermute(cols_a, "flow", near_pairs(flows))
    got_b = lax.ppermute(cols_b, "flow", far_pairs(flows))
    rows_a, rows_b = pl.pallas_call(
        corners_kernel,
        out_shape=(strip, strip),
        in_specs=[smem()] + [vmem()] * 4,
        out_specs=(vmem(), vmem()),
        compiler_params=params(),
        name="corners",
    )(place, rows_a, rows_b, got_a, got_b)
    strip_a = lax.ppermute(rows_a, "tile", near_pairs(bands))
    strip_b = lax.ppermute(rows_b, "tile", far_pairs(bands))

    stride = CAP * members + TAGS
    high = rows + 2 * PAD
    diffused, sent = pl.pallas_call(
        stencil_kernel,
        out_shape=(sds((members * rows, cols), F32), sds((bands * stride, cols), BF16)),
        in_specs=[smem()] * 6 + [anywhere()] + [vmem()] * 6,
        out_specs=(vmem(), vmem()),
        scratch_shapes=[
            pltpu.VMEM((members * high, cols), F32),
            pltpu.VMEM((2 * high, cols), F32),
            pltpu.VMEM((high, cols), F32),
            pltpu.VMEM((rows, cols), F32),
            pltpu.VMEM((members, cols), F32),
            pltpu.VMEM((members, cols), F32),
            pltpu.SMEM((bands,), jnp.int32),
            pltpu.SemaphoreType.DMA,
        ],
        compiler_params=params(),
        name="stencil",
    )(place, hubs, dest_tile.reshape(-1), dest_row.reshape(-1), county_id.reshape(-1), share,
      density, weight, own, got_a, got_b, strip_a, strip_b)

    landed = lax.all_to_all(sent, "tile", split_axis=0, concat_axis=0, tiled=True)
    tiles, diffused = lax.optimization_barrier((tiles, diffused))
    blocks = [tiles]
    bit = flows // 2
    offsets = [0]
    while bit:
        blocks += [lax.ppermute(x, "flow", [(i, i ^ bit) for i in range(flows)]) for x in blocks]
        offsets += [o ^ bit for o in offsets]
        bit //= 2
    blocks = [x for _, x in sorted(zip(offsets, blocks), key=lambda p: p[0])]

    cut = lambda: pl.BlockSpec((block, rows, cols), lambda i: (i, 0, 0))
    kept, grow = pl.pallas_call(
        grow_kernel,
        grid=(members // block,),
        out_shape=(sds(density.shape, F32), sds(density.shape, F32)),
        in_specs=[smem(), smem(), cut(), cut(), whole(rows, cols)],
        out_specs=(cut(), cut()),
        scratch_shapes=[pltpu.VMEM((rows, cols), F32)],
        compiler_params=params(),
        name="grow",
    )(hubs, share, diffused.reshape(density.shape), dispersal_draw, threshold)

    out = pl.pallas_call(
        land_kernel,
        out_shape=sds((members * rows, cols), F32),
        in_specs=[smem()] + [vmem()] * (3 + flows),
        out_specs=vmem(),
        scratch_shapes=[
            pltpu.VMEM((bands, cols), jnp.int32),
            pltpu.SMEM((bands, cols), jnp.int32),
            pltpu.SemaphoreType.DMA,
        ],
        compiler_params=params(),
        name="land",
    )(place, landed, kept.reshape(-1, cols), grow.reshape(-1, cols), *blocks)
    return out.reshape(density.shape)


def solution(mesh):
    in_specs = (
        P(None, "tile", "flow"),
        P("tile", "flow"),
        P(),
        P(None, "tile", "flow"),
        P("tile", "flow"),
        P("flow", "tile"),
        P("flow", "tile", None),
        P("flow", "tile"),
        P("flow", "tile"),
        P("flow", "tile"),
        P("flow", None, None),
        P("flow"),
    )
    out_specs = P(None, "tile", "flow")
    return jax.shard_map(local, mesh=mesh, in_specs=in_specs, out_specs=out_specs, check_vma=False)
```

```python
import jax
import jax.numpy as jnp
from jax import lax
from jax.experimental import pallas as pl
from jax.experimental.pallas import tpu as pltpu
from jax.sharding import PartitionSpec as P

CAP = 4
KAPPA = 0.24
SHARPNESS = 8.0
TAIL = 8
TAGS = 16
CHUNK = 16
UNROLL = 4
STEP = 16
GROW = 16
MIB = 1024 * 1024
F32 = jnp.float32
BF16 = jnp.bfloat16


def lanes(shape):
    return lax.broadcasted_iota(jnp.int32, shape, 1)


def sublanes(shape):
    return lax.broadcasted_iota(jnp.int32, shape, 0)


def edges_kernel(
    place, density, habitat, suit, tiles, scale,
    cols_a, cols_b, rows_a, rows_b, own, weight_out, tiles_out, turned,
    acc_e, acc_o, label_v, suit_v, scale_v, row_sems, sems,
):
    rows, members, cols = turned.shape
    half = rows // 2
    chunk = CHUNK
    t_even = place[0] == 0
    f_even = place[1] == 0
    depth = tiles.shape[1]
    small = [
        pltpu.make_async_copy(suit, suit_v, sems.at[0]),
        pltpu.make_async_copy(habitat, label_v, sems.at[1]),
        pltpu.make_async_copy(scale, scale_v, sems.at[2]),
        pltpu.make_async_copy(tiles, tiles_out.at[:, :depth, :], sems.at[3]),
    ]
    for copy in small:
        copy.start()

    def fetch(i, carry):
        for k in range(8):
            r = i * 8 + k
            pltpu.make_async_copy(density.at[:, r, :], turned.at[r], row_sems.at[i * 8 // chunk]).start()
        return carry

    lax.fori_loop(0, rows // 8, fetch, 0)
    for copy in small:
        copy.wait()

    shape = (rows, cols)
    label = label_v[...]
    weight = jnp.zeros(shape, F32)
    for c in range(suit_v.shape[0]):
        weight = jnp.where(label == c, suit_v[c], weight)
    weight_out[...] = weight
    pair_lane = lanes((half, cols)) // 2 == sublanes((half, cols))

    def spread(column):
        return jnp.sum(jnp.where(pair_lane, column, 0.0), axis=0, keepdims=True)

    row8 = sublanes((TAIL, cols))

    def side_weight(column):
        return jnp.where(row8 == 0, spread(column[:half]), spread(column[half:]))

    w_right = side_weight(weight[:, cols - 1:])
    w_left = side_weight(weight[:, :1])
    cols_a[2 * members:, :] = jnp.where(f_even, w_right, w_left)
    cols_b[2 * members:, :] = jnp.where(f_even, w_left, w_right)
    w_top = jnp.broadcast_to(weight[:1, :], (TAIL, cols))
    w_bottom = jnp.broadcast_to(weight[rows - 1:, :], (TAIL, cols))
    rows_a[2 * members:, :] = jnp.where(t_even, w_bottom, w_top)
    rows_b[2 * members:, :] = jnp.where(t_even, w_top, w_bottom)
    for c in range(tiles.shape[0]):
        value = scale_v[:, c:c + 1].astype(F32)
        tiles_out[c, depth:, :] = jnp.broadcast_to(value, (TAGS, cols)).astype(BF16)

    quad = lanes((8, cols)) // 4

    def pack(i, carry):
        ready = turned.at[pl.ds(i * chunk, chunk)]
        pltpu.make_async_copy(ready, ready, row_sems.at[i]).wait()
        part = i // (half // chunk)
        first = (i - part * (half // chunk)) * (chunk // 2)
        for g in range(members // 8):
            to = pl.ds(pl.multiple_of(part * members + 8 * g, 8), 8)
            even, odd = acc_e[to, :], acc_o[to, :]
            for j in range(chunk // 2):
                r = i * chunk + 2 * j
                q = first + j
                shift = 4 * q + 2
                hit = quad == q
                even = jnp.where(hit, pltpu.roll(turned[r, 8 * g:8 * g + 8, :], shift, 1), even)
                odd = jnp.where(hit, pltpu.roll(turned[r + 1, 8 * g:8 * g + 8, :], shift, 1), odd)
            acc_e[to, :] = even
            acc_o[to, :] = odd
        return carry

    lax.fori_loop(0, rows // chunk, pack, 0)

    wide = (2 * members, cols)
    low = lanes(wide) % 4 < 2
    even, odd = acc_e[...], acc_o[...]
    right = jnp.where(low, even, pltpu.roll(odd, 2, 1))
    left = jnp.where(low, pltpu.roll(even, cols - 2, 1), odd)
    own[...] = jnp.where(lanes(wide) % 2 == 0, pltpu.roll(right, cols - 1, 1), pltpu.roll(left, 1, 1))
    cols_a[:2 * members, :] = jnp.where(f_even, right, left)
    cols_b[:2 * members, :] = jnp.where(f_even, left, right)
    for k in range(2):
        to = pl.ds(k * members, members)
        rows_a[to, :] = turned[jnp.where(t_even, rows - 2, 0) + k]
        rows_b[to, :] = turned[jnp.where(t_even, 0, rows - 2) + k]


def corners_kernel(place, rows_a, rows_b, got_a, got_b, out_a, out_b):
    cols = got_a.shape[1]
    members = (got_a.shape[0] - TAIL) // 2
    t_even = place[0] == 0
    f_even = place[1] == 0
    side = (members, cols)
    swap = (lanes(side) % 2 == 1) == f_even
    top = jnp.where(swap, got_b[:members, :], got_a[:members, :])
    bottom = jnp.where(swap, got_b[members:2 * members, :], got_a[members:2 * members, :])

    def to_row(pair, first):
        east = jnp.where(lanes(side) == 2 * sublanes(side), pair[:, first:first + 1], 0.0)
        west = jnp.where(lanes(side) == 2 * sublanes(side) + 1, pair[:, first + 1:first + 2], 0.0)
        return jnp.sum(east + west, axis=0, keepdims=True)

    top_row = to_row(top, 0)
    bottom_row = to_row(bottom, cols - 2)
    out_a[...] = rows_a[...]
    out_b[...] = rows_b[...]
    at = 2 * members + 1
    out_a[at:at + 1, :] = jnp.where(t_even, bottom_row, top_row)
    out_b[at:at + 1, :] = jnp.where(t_even, top_row, bottom_row)


def hubs_kernel(
    place, hub_row, dest_tile, dest_row, county, share,
    turned, weight, own, cols_a, cols_b, rows_a, rows_b,
    sent, near, halo1, beside, coef, strips, counts,
):
    rows, members, cols = turned.shape
    bands = counts.shape[0]
    t_even = place[0] == 0
    f_even = place[1] == 0
    side = (members, cols)
    lane = lanes(side)
    even_lane = lane % 2 == 0

    tail_n = jnp.where(t_even, rows_b[2 * members:, :], rows_a[2 * members:, :])
    tail_s = jnp.where(t_even, rows_a[2 * members:, :], rows_b[2 * members:, :])
    for k in range(2):
        at = slice(k * members, (k + 1) * members)
        strips[k] = jnp.where(t_even, rows_b[at, :], rows_a[at, :])
        strips[2 + k] = jnp.where(t_even, rows_a[at, :], rows_b[at, :])
    coef[0:8, :] = KAPPA * tail_n
    coef[8:8 + rows, :] = KAPPA * weight[...]
    coef[8 + rows:, :] = KAPPA * tail_s

    def corner(tail):
        row = jnp.broadcast_to(tail[1:2, :], side)
        east = jnp.sum(jnp.where(lane == 2 * sublanes(side), row, 0.0), axis=1, keepdims=True)
        west = jnp.sum(jnp.where(lane == 2 * sublanes(side) + 1, row, 0.0), axis=1, keepdims=True)
        return east, west

    east_n, west_n = corner(tail_n)
    east_s, west_s = corner(tail_s)
    halves = []
    for k in range(2):
        at = slice(k * members, (k + 1) * members)
        a, b = cols_a[at, :], cols_b[at, :]
        from_e = jnp.where(f_even, a, b)
        from_w = jnp.where(f_even, b, a)
        close = jnp.where(even_lane, from_e, from_w)
        far = jnp.where(even_lane, pltpu.roll(from_e, cols - 1, 1), pltpu.roll(from_w, 1, 1))
        near[at, :] = close
        halves.append((close, far))
    wa, wb = cols_a[2 * members:, :], cols_b[2 * members:, :]
    w_e = jnp.where(f_even, wa, wb)
    w_w = jnp.where(f_even, wb, wa)
    w_packed = jnp.where(lanes((TAIL, cols)) % 2 == 0, w_e, w_w)
    near0, near1 = halves[0][0], halves[1][0]
    down0, down1 = pltpu.roll(near0, 2, 1), pltpu.roll(near1, 2, 1)
    up0, up1 = pltpu.roll(near0, cols - 2, 1), pltpu.roll(near1, cols - 2, 1)
    n0 = jnp.where(lane < 2, jnp.where(even_lane, east_n, west_n), down0)
    n1 = jnp.where(lane < 2, down0, down1)
    s0 = jnp.where(lane >= cols - 2, up1, up0)
    s1 = jnp.where(lane >= cols - 2, jnp.where(even_lane, east_s, west_s), up1)
    for k, (n, s) in enumerate(((n0, s0), (n1, s1))):
        at = slice(k * members, (k + 1) * members)
        close, far = halves[k]
        around = (n + s) + (far + own[at, :])
        halo1[at, :] = close + KAPPA * w_packed[k:k + 1, :] * (around - 4.0 * close)
    beside[0:members, :] = jnp.where(lane == 0, west_n, east_n)
    beside[members:2 * members, :] = pltpu.roll(near1, cols - 1, 1)
    beside[2 * members:3 * members, :] = pltpu.roll(near0, 1, 1)
    beside[3 * members:, :] = jnp.where(lane == 0, west_s, east_s)

    stride = CAP * members + TAGS
    tag_lane = lanes((TAGS, cols))
    for t in range(bands):
        counts[t] = 0
        sent[t * stride + CAP * members:(t + 1) * stride, :] = jnp.full((TAGS, cols), -1.0, BF16)
    half = rows // 2
    first, last = lane == 0, lane == cols - 1

    def field_row(r):
        inside = turned[jnp.clip(r, 0, rows - 1)]
        outside = strips[jnp.clip(jnp.where(r < 0, r + 2, r - rows + 2), 0, 3)]
        return jnp.where(jnp.logical_and(r >= 0, r < rows), inside, outside)

    def halo_row(ref, r):
        k = jnp.where(r >= half, 1, 0)
        at = pl.ds(pl.multiple_of(k * members, 8), members)
        return pltpu.roll(ref[at, :], cols - 1 - 2 * (r - k * half), 1)

    def side_row(r):
        edge = jnp.where(r < 0, beside[0:members, :], beside[3 * members:, :])
        inside = halo_row(near, jnp.clip(r, 0, rows - 1))
        return jnp.where(jnp.logical_and(r >= 0, r < rows), inside, edge)

    def relax(c, n, s, h, w):
        west = jnp.where(first, h, pltpu.roll(c, 1, 1))
        east = jnp.where(last, h, pltpu.roll(c, cols - 1, 1))
        return c + w * ((n + s) + (west + east) - 4.0 * c)

    def coef_row(r):
        at = jnp.where(r < 0, 0, r + 8)
        return coef[pl.ds(at, 1), :]

    def one(h):
        r = hub_row[h]
        u = [field_row(r + k) for k in range(-2, 3)]
        v = [relax(u[k + 2], u[k + 1], u[k + 3], side_row(r + k), coef_row(r + k)) for k in range(-1, 2)]
        moved = share[h] * relax(v[1], v[0], v[2], halo_row(halo1, r), coef_row(r))
        to = dest_tile[h]
        n = counts[to]
        counts[to] = n + 1
        base = pl.multiple_of(to * stride, 16)
        sent[pl.ds(pl.multiple_of(base + n * members, 16), members), :] = moved.astype(BF16)
        at = pl.ds(pl.multiple_of(base + CAP * members, 16), TAGS)
        tags = sent[at, :].astype(F32)
        tags = jnp.where(tag_lane == n, dest_row[h].astype(F32), tags)
        tags = jnp.where(tag_lane == CAP + n, county[h].astype(F32), tags)
        sent[at, :] = tags.astype(BF16)

    def several(i, carry):
        for k in range(UNROLL):
            one(i * UNROLL + k)
        return carry

    lax.fori_loop(0, hub_row.shape[0] // UNROLL, several, 0)


def grow_kernel(draw, threshold, grow, draw_v, grow_v, limit_v, in_sem, out_sem, sem):
    chunk = draw.shape[0] // GROW
    limit = pltpu.make_async_copy(threshold, limit_v, sem)
    limit.start()

    def fetch(i, carry):
        at = pl.ds(i * chunk, chunk)
        pltpu.make_async_copy(draw.at[at], draw_v.at[at], in_sem.at[i]).start()
        return carry

    lax.fori_loop(0, GROW, fetch, 0)
    limit.wait()

    def work(i, carry):
        at = pl.ds(i * chunk, chunk)
        pltpu.make_async_copy(draw.at[at], draw_v.at[at], in_sem.at[i]).wait()
        for k in range(chunk):
            x = 0.5 * SHARPNESS * (draw_v[i * chunk + k].astype(F32) - limit_v[...])
            grow_v[i * chunk + k] = 0.5 * jnp.tanh(x) + 0.5
        pltpu.make_async_copy(grow_v.at[at], grow.at[at], out_sem).start()
        return carry

    lax.fori_loop(0, GROW, work, 0)
    pltpu.make_async_copy(grow_v, grow, out_sem).wait()


def bulk_kernel(
    hub_row, share, density, grow, coef, strips, near, halo1, beside,
    kept, field, inner, gate, factor, in_sem, gate_sem, out_sem,
):
    members, rows, cols = density.shape
    half = rows // 2
    step = STEP
    blocks = rows // step

    def fetch(i, carry):
        for k in range(step):
            r = i * step + k
            pltpu.make_async_copy(density.at[:, r, :], field.at[r + 2], in_sem.at[i]).start()
        return carry

    def fetch_gate(i, carry):
        for k in range(step):
            r = i * step + k
            pltpu.make_async_copy(grow.at[:, r, :], gate.at[r], gate_sem.at[i]).start()
        return carry

    lax.fori_loop(0, blocks, fetch, 0)
    lax.fori_loop(0, blocks, fetch_gate, 0)
    for k in range(2):
        field[k] = strips[k]
        field[rows + 2 + k] = strips[2 + k]

    def clear(i, carry):
        for k in range(8):
            factor[i * 8 + k] = 1.0
        return carry

    lax.fori_loop(0, rows // 8, clear, 0)

    def leave(h, carry):
        r = hub_row[h]
        factor[r] = factor[r] - share[h]
        return carry

    lax.fori_loop(0, hub_row.shape[0], leave, 0)

    side = (members, cols)
    lane = lanes(side)
    first, last = lane == 0, lane == cols - 1

    edge = jnp.logical_or(first, last)
    band = (cols, cols)
    beside_mask = (jnp.abs(lanes(band) - sublanes(band)) == 1).astype(BF16)

    def lateral(c):
        flat = c.reshape(-1, cols)
        high = flat.astype(BF16)
        low = (flat - high.astype(F32)).astype(BF16)
        both = jnp.dot(high, beside_mask, preferred_element_type=F32)
        return (both + jnp.dot(low, beside_mask, preferred_element_type=F32)).reshape(c.shape)

    def relax(c, n, s, h, w, across):
        return c + w * ((n + s) + (across + jnp.where(edge, h, 0.0)) - 4.0 * c)

    def halo_row(ref, part, r):
        at = pl.ds(pl.multiple_of(part * members, 8), members)
        return pltpu.roll(ref[at, :], cols - 1 - 2 * (r - part * half), 1)

    def landed(i):
        ready = field.at[pl.ds(i * step + 2, step)]
        pltpu.make_async_copy(ready, ready, in_sem.at[i]).wait()

    landed(0)
    inner[0] = relax(field[1], field[0], field[2], beside[:members, :], coef[0:1, :], lateral(field[1]))

    def early(i, carry):
        @pl.when(i < blocks - 1)
        def _():
            landed(i + 1)

        part = i // (half // step)
        across = lateral(field[pl.ds(i * step + 2, step)])
        for k in range(step):
            r = i * step + k
            inner[r + 1] = relax(
                field[r + 2], field[r + 1], field[r + 3], halo_row(near, part, r), coef[pl.ds(r + 8, 1), :], across[k])
        return carry

    lax.fori_loop(0, blocks, early, 0)
    inner[rows + 1] = relax(
        field[rows + 2], field[rows + 1], field[rows + 3], beside[3 * members:, :], coef[rows + 8:rows + 9, :],
        lateral(field[rows + 2]))

    def late(i, carry):
        ready = gate.at[pl.ds(i * step, step)]
        pltpu.make_async_copy(ready, ready, gate_sem.at[i]).wait()
        part = i // (half // step)
        across = lateral(inner[pl.ds(i * step + 1, step)])
        for k in range(step):
            r = i * step + k
            d = relax(
                inner[r + 1], inner[r], inner[r + 2], halo_row(halo1, part, r), coef[pl.ds(r + 8, 1), :], across[k])
            gate[r] = d * factor[r] * gate[r]
        for k in range(step):
            r = i * step + k
            pltpu.make_async_copy(gate.at[r], kept.at[:, r, :], out_sem).start()
        return carry

    lax.fori_loop(0, blocks, late, 0)
    pltpu.make_async_copy(gate, gate, out_sem).wait()


def table_kernel(place, *refs):
    blocks, (table, sem) = refs[:-2], refs[-2:]
    flow = place[3]
    per = blocks[0].shape[0]
    copies = []
    for i, ref in enumerate(blocks):
        at = jnp.bitwise_xor(flow, i) * per
        copies.append(pltpu.make_async_copy(ref, table.at[pl.ds(at, per)], sem))
    for copy in copies:
        copy.start()
    for copy in copies:
        copy.wait()


def land_kernel(
    landed, table, kept, grow, out,
    base, gate, carried, tags_v, tags_s, owner, lead, tag_sem, row_sem, out_sem,
):
    bands, cols = tags_v.shape
    stride = landed.shape[0] // bands
    members, rows, _ = kept.shape
    depth = table.shape[1] - TAGS
    slots = bands * CAP
    for t in range(bands):
        tags = landed[t * stride + CAP * members:(t + 1) * stride, :].astype(F32)
        tags_v[t:t + 1, :] = tags[:1].astype(jnp.int32)
    copy = pltpu.make_async_copy(tags_v, tags_s, tag_sem)
    copy.start()

    def clear(r, carry):
        owner[r] = -1
        return carry

    lax.fori_loop(0, rows, clear, 0, unroll=8)
    copy.wait()

    def fetch(row, s):
        return (pltpu.make_async_copy(out.at[:, row, :], base.at[s], row_sem),
                pltpu.make_async_copy(grow.at[:, row, :], gate.at[s], row_sem))

    def store(row, s):
        return pltpu.make_async_copy(base.at[s], out.at[:, row, :], out_sem)

    def claim(s, carry):
        row = tags_s[s // CAP, s % CAP]
        at = jnp.maximum(row, 0)
        mine = owner[at]
        fresh = jnp.logical_and(row >= 0, mine < 0)
        lead[s] = jnp.where(row < 0, -1, jnp.where(mine < 0, s, mine))

        @pl.when(fresh)
        def _():
            owner[at] = s
            for c in fetch(at, s):
                c.start()

        return carry

    lax.fori_loop(0, slots, claim, 0)

    def product(t, carry):
        for n in range(CAP):
            c = jnp.maximum(tags_s[t, CAP + n], 0)
            at = pl.ds(pl.multiple_of(t * stride + n * members, 16), members)
            x = jnp.dot(landed[at, :], table[c, :depth, :], preferred_element_type=F32)
            scale = table[c, depth:, :].astype(F32)[:1]
            carried[t * CAP + n] = (x * scale).astype(BF16).astype(F32)
        return carry

    lax.fori_loop(0, bands, product, 0, unroll=8)

    def arrive(s, carry):
        @pl.when(lead[s] == s)
        def _():
            for c in fetch(tags_s[s // CAP, s % CAP], s):
                c.wait()
        return carry

    lax.fori_loop(0, slots, arrive, 0)

    def add(s, carry):
        @pl.when(lead[s] >= 0)
        def _():
            to = lead[s]
            base[to] = base[to] + carried[s] * gate[to]
        return carry

    lax.fori_loop(0, slots, add, 0)

    def send(s, carry):
        @pl.when(lead[s] == s)
        def _():
            store(tags_s[s // CAP, s % CAP], s).start()
        return carry

    def sent(s, carry):
        @pl.when(lead[s] == s)
        def _():
            store(tags_s[s // CAP, s % CAP], s).wait()
        return carry

    lax.fori_loop(0, slots, send, 0)
    lax.fori_loop(0, slots, sent, 0)


def smem():
    return pl.BlockSpec(memory_space=pltpu.SMEM)


def vmem():
    return pl.BlockSpec(memory_space=pltpu.VMEM)


def anywhere():
    return pl.BlockSpec(memory_space=pl.ANY)


def hbm():
    return pl.BlockSpec(memory_space=pltpu.HBM)


def params(mib):
    return pltpu.CompilerParams(vmem_limit_bytes=int(mib * MIB))


def near_pairs(count):
    return [(i, i ^ 1) for i in range(count)]


def far_pairs(count):
    return [(i, j) for k in range(1, count - 1, 2) for i, j in ((k, k + 1), (k + 1, k))]


def local(
    density,
    habitat_class,
    suitability,
    dispersal_draw,
    threshold,
    hub_row,
    dest_tile,
    dest_row,
    county_id,
    jump_share,
    flow_tiles,
    flow_scale,
):
    members, rows, cols = density.shape
    bands, flows = lax.axis_size("tile"), lax.axis_size("flow")
    density, dispersal_draw, habitat_class, flow_tiles = (
        pltpu.with_memory_space_constraint(x, pltpu.HBM)
        for x in (density, dispersal_draw, habitat_class, flow_tiles))
    t, f = lax.axis_index("tile"), lax.axis_index("flow")
    place = jnp.stack([t % 2, f % 2, t, f]).astype(jnp.int32)
    hubs, share = hub_row.reshape(-1), jump_share.reshape(-1)
    sds = jax.ShapeDtypeStruct
    per, depth = flow_tiles.shape[:2]
    message = sds((2 * members + TAIL, cols), F32)
    pack = sds((2 * members, cols), F32)
    cols_a, cols_b, rows_a, rows_b, own, weight, tiles, turned = pl.pallas_call(
        edges_kernel,
        out_shape=(message, message, message, message, pack, sds((rows, cols), F32),
                   sds((per, depth + TAGS, cols), BF16), sds((rows, members, cols), F32)),
        in_specs=[smem()] + [hbm()] * 5,
        out_specs=(vmem(),) * 8,
        scratch_shapes=[
            pltpu.VMEM(pack.shape, F32),
            pltpu.VMEM(pack.shape, F32),
            pltpu.VMEM((rows, cols), jnp.int32),
            pltpu.SMEM(suitability.shape, F32),
            pltpu.VMEM((1, per), BF16),
            pltpu.SemaphoreType.DMA((rows // CHUNK,)),
            pltpu.SemaphoreType.DMA((4,)),
        ],
        compiler_params=params(24),
        name="edges",
    )(place, density, habitat_class, suitability, flow_tiles, flow_scale.reshape(1, -1))

    got_a = lax.ppermute(cols_a, "flow", near_pairs(flows))
    got_b = lax.ppermute(cols_b, "flow", far_pairs(flows))
    rows_a, rows_b = pl.pallas_call(
        corners_kernel,
        out_shape=(message, message),
        in_specs=[smem()] + [vmem()] * 4,
        out_specs=(vmem(), vmem()),
        compiler_params=params(24),
        name="corners",
    )(place, rows_a, rows_b, got_a, got_b)
    strip_a = lax.ppermute(rows_a, "tile", near_pairs(bands))
    strip_b = lax.ppermute(rows_b, "tile", far_pairs(bands))

    stride = CAP * members + TAGS
    sent, near, halo1, beside, coef, strips = pl.pallas_call(
        hubs_kernel,
        out_shape=(sds((bands * stride, cols), BF16), pack, pack, sds((4 * members, cols), F32),
                   sds((rows + 16, cols), F32), sds((4, members, cols), F32)),
        in_specs=[smem()] * 6 + [vmem()] * 7,
        out_specs=(vmem(),) * 6,
        scratch_shapes=[pltpu.SMEM((bands,), jnp.int32)],
        compiler_params=params(24),
        name="hubs",
    )(place, hubs, dest_tile.reshape(-1), dest_row.reshape(-1), county_id.reshape(-1), share,
      turned, weight, own, got_a, got_b, strip_a, strip_b)

    landed = lax.all_to_all(sent, "tile", split_axis=0, concat_axis=0, tiled=True)
    dispersal_draw, near = lax.optimization_barrier((dispersal_draw, near))
    blocks = [tiles]
    bit = flows // 2
    offsets = [0]
    while bit:
        blocks += [lax.ppermute(x, "flow", [(i, i ^ bit) for i in range(flows)]) for x in blocks]
        offsets += [o ^ bit for o in offsets]
        bit //= 2
    blocks = [x for _, x in sorted(zip(offsets, blocks), key=lambda p: p[0])]
    table = pl.pallas_call(
        table_kernel,
        out_shape=sds((flows * per, depth + TAGS, cols), BF16),
        in_specs=[smem()] + [vmem()] * flows,
        out_specs=vmem(),
        scratch_shapes=[pltpu.SemaphoreType.DMA],
        compiler_params=params(24),
        name="table",
    )(place, *blocks)

    grow = pl.pallas_call(
        grow_kernel,
        out_shape=sds(density.shape, F32),
        in_specs=[hbm(), hbm()],
        out_specs=hbm(),
        scratch_shapes=[
            pltpu.VMEM(density.shape, BF16),
            pltpu.VMEM(density.shape, F32),
            pltpu.VMEM((rows, cols), F32),
            pltpu.SemaphoreType.DMA((GROW,)),
            pltpu.SemaphoreType.DMA,
            pltpu.SemaphoreType.DMA,
        ],
        compiler_params=params(24),
        name="grow",
    )(dispersal_draw, threshold)
    grow = pltpu.with_memory_space_constraint(grow, pltpu.HBM)

    kept = pl.pallas_call(
        bulk_kernel,
        out_shape=sds(density.shape, F32),
        in_specs=[smem(), smem(), hbm(), hbm()] + [vmem()] * 5,
        out_specs=hbm(),
        scratch_shapes=[
            pltpu.VMEM((rows + 4, members, cols), F32),
            pltpu.VMEM((rows + 2, members, cols), F32),
            pltpu.VMEM((rows, members, cols), F32),
            pltpu.SMEM((rows,), F32),
            pltpu.SemaphoreType.DMA((rows // STEP,)),
            pltpu.SemaphoreType.DMA((rows // STEP,)),
            pltpu.SemaphoreType.DMA,
        ],
        compiler_params=params(24),
        name="bulk",
    )(hubs, share, density, grow, coef, strips, near, halo1, beside)

    slots = bands * CAP
    out = pl.pallas_call(
        land_kernel,
        out_shape=sds(density.shape, F32),
        in_specs=[vmem(), vmem(), hbm(), hbm()],
        out_specs=hbm(),
        input_output_aliases={2: 0},
        scratch_shapes=[
            pltpu.VMEM((slots, members, cols), F32),
            pltpu.VMEM((slots, members, cols), F32),
            pltpu.VMEM((slots, members, cols), F32),
            pltpu.VMEM((bands, cols), jnp.int32),
            pltpu.SMEM((bands, cols), jnp.int32),
            pltpu.SMEM((rows,), jnp.int32),
            pltpu.SMEM((slots,), jnp.int32),
            pltpu.SemaphoreType.DMA,
            pltpu.SemaphoreType.DMA,
            pltpu.SemaphoreType.DMA,
        ],
        compiler_params=params(24),
        name="land",
    )(landed, table, kept, grow)
    return out


def solution(mesh):
    in_specs = (
        P(None, "tile", "flow"),
        P("tile", "flow"),
        P(),
        P(None, "tile", "flow"),
        P("tile", "flow"),
        P("flow", "tile"),
        P("flow", "tile", None),
        P("flow", "tile"),
        P("flow", "tile"),
        P("flow", "tile"),
        P("flow", None, None),
        P("flow"),
    )
    out_specs = P(None, "tile", "flow")
    return jax.shard_map(local, mesh=mesh, in_specs=in_specs, out_specs=out_specs, check_vma=False)
```

```python
import jax
import jax.numpy as jnp
from jax import lax
from jax.experimental import pallas as pl
from jax.experimental.pallas import tpu as pltpu
from jax.sharding import PartitionSpec as P

CAP = 4
KAPPA = 0.24
SHARPNESS = 8.0
TAIL = 8
TAGS = 16
CHUNK = 16
UNROLL = 4
STEP = 16
GROW = 16
MIB = 1024 * 1024
F32 = jnp.float32
BF16 = jnp.bfloat16


def lanes(shape):
    return lax.broadcasted_iota(jnp.int32, shape, 1)


def sublanes(shape):
    return lax.broadcasted_iota(jnp.int32, shape, 0)


def edges_kernel(
    place, density, habitat, suit, tiles, scale,
    cols_a, cols_b, rows_a, rows_b, own, weight_out, tiles_out, turned,
    acc_e, acc_o, label_v, suit_v, scale_v, row_sems, sems,
):
    rows, members, cols = turned.shape
    half = rows // 2
    chunk = CHUNK
    t_even = place[0] == 0
    f_even = place[1] == 0
    depth = tiles.shape[1]
    small = [
        pltpu.make_async_copy(suit, suit_v, sems.at[0]),
        pltpu.make_async_copy(habitat, label_v, sems.at[1]),
        pltpu.make_async_copy(scale, scale_v, sems.at[2]),
        pltpu.make_async_copy(tiles, tiles_out.at[:, :depth, :], sems.at[3]),
    ]
    for copy in small:
        copy.start()

    def fetch(i, carry):
        for k in range(8):
            r = i * 8 + k
            pltpu.make_async_copy(density.at[:, r, :], turned.at[r], row_sems.at[i * 8 // chunk]).start()
        return carry

    lax.fori_loop(0, rows // 8, fetch, 0)
    for copy in small:
        copy.wait()

    shape = (rows, cols)
    label = label_v[...]
    weight = jnp.zeros(shape, F32)
    for c in range(suit_v.shape[0]):
        weight = jnp.where(label == c, suit_v[c], weight)
    weight_out[...] = weight
    pair_lane = lanes((half, cols)) // 2 == sublanes((half, cols))

    def spread(column):
        return jnp.sum(jnp.where(pair_lane, column, 0.0), axis=0, keepdims=True)

    row8 = sublanes((TAIL, cols))

    def side_weight(column):
        return jnp.where(row8 == 0, spread(column[:half]), spread(column[half:]))

    w_right = side_weight(weight[:, cols - 1:])
    w_left = side_weight(weight[:, :1])
    cols_a[2 * members:, :] = jnp.where(f_even, w_right, w_left)
    cols_b[2 * members:, :] = jnp.where(f_even, w_left, w_right)
    w_top = jnp.broadcast_to(weight[:1, :], (TAIL, cols))
    w_bottom = jnp.broadcast_to(weight[rows - 1:, :], (TAIL, cols))
    rows_a[2 * members:, :] = jnp.where(t_even, w_bottom, w_top)
    rows_b[2 * members:, :] = jnp.where(t_even, w_top, w_bottom)
    for c in range(tiles.shape[0]):
        value = scale_v[:, c:c + 1].astype(F32)
        tiles_out[c, depth:, :] = jnp.broadcast_to(value, (TAGS, cols)).astype(BF16)

    quad = lanes((8, cols)) // 4

    def pack(i, carry):
        ready = turned.at[pl.ds(i * chunk, chunk)]
        pltpu.make_async_copy(ready, ready, row_sems.at[i]).wait()
        part = i // (half // chunk)
        first = (i - part * (half // chunk)) * (chunk // 2)
        for g in range(members // 8):
            to = pl.ds(pl.multiple_of(part * members + 8 * g, 8), 8)
            even, odd = acc_e[to, :], acc_o[to, :]
            for j in range(chunk // 2):
                r = i * chunk + 2 * j
                q = first + j
                shift = 4 * q + 2
                hit = quad == q
                even = jnp.where(hit, pltpu.roll(turned[r, 8 * g:8 * g + 8, :], shift, 1), even)
                odd = jnp.where(hit, pltpu.roll(turned[r + 1, 8 * g:8 * g + 8, :], shift, 1), odd)
            acc_e[to, :] = even
            acc_o[to, :] = odd
        return carry

    lax.fori_loop(0, rows // chunk, pack, 0)

    wide = (2 * members, cols)
    low = lanes(wide) % 4 < 2
    even, odd = acc_e[...], acc_o[...]
    right = jnp.where(low, even, pltpu.roll(odd, 2, 1))
    left = jnp.where(low, pltpu.roll(even, cols - 2, 1), odd)
    own[...] = jnp.where(lanes(wide) % 2 == 0, pltpu.roll(right, cols - 1, 1), pltpu.roll(left, 1, 1))
    cols_a[:2 * members, :] = jnp.where(f_even, right, left)
    cols_b[:2 * members, :] = jnp.where(f_even, left, right)
    for k in range(2):
        to = pl.ds(k * members, members)
        rows_a[to, :] = turned[jnp.where(t_even, rows - 2, 0) + k]
        rows_b[to, :] = turned[jnp.where(t_even, 0, rows - 2) + k]


def corners_kernel(place, rows_a, rows_b, got_a, got_b, out_a, out_b):
    cols = got_a.shape[1]
    members = (got_a.shape[0] - TAIL) // 2
    t_even = place[0] == 0
    f_even = place[1] == 0
    side = (members, cols)
    swap = (lanes(side) % 2 == 1) == f_even
    top = jnp.where(swap, got_b[:members, :], got_a[:members, :])
    bottom = jnp.where(swap, got_b[members:2 * members, :], got_a[members:2 * members, :])

    def to_row(pair, first):
        east = jnp.where(lanes(side) == 2 * sublanes(side), pair[:, first:first + 1], 0.0)
        west = jnp.where(lanes(side) == 2 * sublanes(side) + 1, pair[:, first + 1:first + 2], 0.0)
        return jnp.sum(east + west, axis=0, keepdims=True)

    top_row = to_row(top, 0)
    bottom_row = to_row(bottom, cols - 2)
    out_a[...] = rows_a[...]
    out_b[...] = rows_b[...]
    at = 2 * members + 1
    out_a[at:at + 1, :] = jnp.where(t_even, bottom_row, top_row)
    out_b[at:at + 1, :] = jnp.where(t_even, top_row, bottom_row)


def hubs_kernel(
    place, hub_row, dest_tile, dest_row, county, share,
    turned, weight, own, cols_a, cols_b, rows_a, rows_b,
    sent, near, halo1, beside, coef, strips, counts,
):
    rows, members, cols = turned.shape
    bands = counts.shape[0]
    t_even = place[0] == 0
    f_even = place[1] == 0
    side = (members, cols)
    lane = lanes(side)
    even_lane = lane % 2 == 0

    tail_n = jnp.where(t_even, rows_b[2 * members:, :], rows_a[2 * members:, :])
    tail_s = jnp.where(t_even, rows_a[2 * members:, :], rows_b[2 * members:, :])
    for k in range(2):
        at = slice(k * members, (k + 1) * members)
        strips[k] = jnp.where(t_even, rows_b[at, :], rows_a[at, :])
        strips[2 + k] = jnp.where(t_even, rows_a[at, :], rows_b[at, :])
    coef[0:8, :] = KAPPA * tail_n
    coef[8:8 + rows, :] = KAPPA * weight[...]
    coef[8 + rows:, :] = KAPPA * tail_s

    def corner(tail):
        row = jnp.broadcast_to(tail[1:2, :], side)
        east = jnp.sum(jnp.where(lane == 2 * sublanes(side), row, 0.0), axis=1, keepdims=True)
        west = jnp.sum(jnp.where(lane == 2 * sublanes(side) + 1, row, 0.0), axis=1, keepdims=True)
        return east, west

    east_n, west_n = corner(tail_n)
    east_s, west_s = corner(tail_s)
    halves = []
    for k in range(2):
        at = slice(k * members, (k + 1) * members)
        a, b = cols_a[at, :], cols_b[at, :]
        from_e = jnp.where(f_even, a, b)
        from_w = jnp.where(f_even, b, a)
        close = jnp.where(even_lane, from_e, from_w)
        far = jnp.where(even_lane, pltpu.roll(from_e, cols - 1, 1), pltpu.roll(from_w, 1, 1))
        near[at, :] = close
        halves.append((close, far))
    wa, wb = cols_a[2 * members:, :], cols_b[2 * members:, :]
    w_e = jnp.where(f_even, wa, wb)
    w_w = jnp.where(f_even, wb, wa)
    w_packed = jnp.where(lanes((TAIL, cols)) % 2 == 0, w_e, w_w)
    near0, near1 = halves[0][0], halves[1][0]
    down0, down1 = pltpu.roll(near0, 2, 1), pltpu.roll(near1, 2, 1)
    up0, up1 = pltpu.roll(near0, cols - 2, 1), pltpu.roll(near1, cols - 2, 1)
    n0 = jnp.where(lane < 2, jnp.where(even_lane, east_n, west_n), down0)
    n1 = jnp.where(lane < 2, down0, down1)
    s0 = jnp.where(lane >= cols - 2, up1, up0)
    s1 = jnp.where(lane >= cols - 2, jnp.where(even_lane, east_s, west_s), up1)
    for k, (n, s) in enumerate(((n0, s0), (n1, s1))):
        at = slice(k * members, (k + 1) * members)
        close, far = halves[k]
        around = (n + s) + (far + own[at, :])
        halo1[at, :] = close + KAPPA * w_packed[k:k + 1, :] * (around - 4.0 * close)
    beside[0:members, :] = jnp.where(lane == 0, west_n, east_n)
    beside[members:2 * members, :] = pltpu.roll(near1, cols - 1, 1)
    beside[2 * members:3 * members, :] = pltpu.roll(near0, 1, 1)
    beside[3 * members:, :] = jnp.where(lane == 0, west_s, east_s)

    stride = CAP * members + TAGS
    tag_lane = lanes((TAGS, cols))
    for t in range(bands):
        counts[t] = 0
        sent[t * stride + CAP * members:(t + 1) * stride, :] = jnp.full((TAGS, cols), -1.0, BF16)
    half = rows // 2
    first, last = lane == 0, lane == cols - 1

    def field_row(r):
        inside = turned[jnp.clip(r, 0, rows - 1)]
        outside = strips[jnp.clip(jnp.where(r < 0, r + 2, r - rows + 2), 0, 3)]
        return jnp.where(jnp.logical_and(r >= 0, r < rows), inside, outside)

    def halo_row(ref, r):
        k = jnp.where(r >= half, 1, 0)
        at = pl.ds(pl.multiple_of(k * members, 8), members)
        return pltpu.roll(ref[at, :], cols - 1 - 2 * (r - k * half), 1)

    def side_row(r):
        edge = jnp.where(r < 0, beside[0:members, :], beside[3 * members:, :])
        inside = halo_row(near, jnp.clip(r, 0, rows - 1))
        return jnp.where(jnp.logical_and(r >= 0, r < rows), inside, edge)

    edge = jnp.logical_or(first, last)
    band = (cols, cols)
    mask = (jnp.abs(lanes(band) - sublanes(band)) == 1).astype(BF16)

    def lateral(rows_in):
        flat = jnp.concatenate(rows_in, axis=0)
        high = flat.astype(BF16)
        low = (flat - high.astype(F32)).astype(BF16)
        both = jnp.dot(high, mask, preferred_element_type=F32) + jnp.dot(low, mask, preferred_element_type=F32)
        return [both[k * members:(k + 1) * members] for k in range(len(rows_in))]

    def relax(c, n, s, h, w, across):
        return c + w * ((n + s) + (across + jnp.where(edge, h, 0.0)) - 4.0 * c)

    def coef_row(r):
        at = jnp.where(r < 0, 0, r + 8)
        return coef[pl.ds(at, 1), :]

    def several(i, carry):
        chosen = [i * UNROLL + k for k in range(UNROLL)]
        spot = [hub_row[h] for h in chosen]
        u = [[field_row(r + k) for k in range(-2, 3)] for r in spot]
        across = lateral([u[k][c] for k in range(UNROLL) for c in (1, 2, 3)])
        v = []
        for k, r in enumerate(spot):
            v.append([
                relax(u[k][c + 2], u[k][c + 1], u[k][c + 3], side_row(r + c), coef_row(r + c), across[3 * k + c + 1])
                for c in range(-1, 2)])
        across = lateral([x[1] for x in v])
        for k, (h, r) in enumerate(zip(chosen, spot)):
            moved = share[h] * relax(v[k][1], v[k][0], v[k][2], halo_row(halo1, r), coef_row(r), across[k])
            to = dest_tile[h]
            n = counts[to]
            counts[to] = n + 1
            base = pl.multiple_of(to * stride, 16)
            sent[pl.ds(pl.multiple_of(base + n * members, 16), members), :] = moved.astype(BF16)
            at = pl.ds(pl.multiple_of(base + CAP * members, 16), TAGS)
            tags = sent[at, :].astype(F32)
            tags = jnp.where(tag_lane == n, dest_row[h].astype(F32), tags)
            tags = jnp.where(tag_lane == CAP + n, county[h].astype(F32), tags)
            sent[at, :] = tags.astype(BF16)
        return carry

    lax.fori_loop(0, hub_row.shape[0] // UNROLL, several, 0)


def grow_kernel(draw, threshold, grow, draw_v, grow_v, limit_v, in_sem, out_sem, sem):
    chunk = draw.shape[0] // GROW
    limit = pltpu.make_async_copy(threshold, limit_v, sem)
    limit.start()

    def fetch(i, carry):
        at = pl.ds(i * chunk, chunk)
        pltpu.make_async_copy(draw.at[at], draw_v.at[at], in_sem.at[i]).start()
        return carry

    lax.fori_loop(0, GROW, fetch, 0)
    limit.wait()

    def work(i, carry):
        at = pl.ds(i * chunk, chunk)
        pltpu.make_async_copy(draw.at[at], draw_v.at[at], in_sem.at[i]).wait()
        for k in range(chunk):
            x = 0.5 * SHARPNESS * (draw_v[i * chunk + k].astype(F32) - limit_v[...])
            grow_v[i * chunk + k] = 0.5 * jnp.tanh(x) + 0.5
        pltpu.make_async_copy(grow_v.at[at], grow.at[at], out_sem).start()
        return carry

    lax.fori_loop(0, GROW, work, 0)
    pltpu.make_async_copy(grow_v, grow, out_sem).wait()


def bulk_kernel(
    hub_row, share, density, grow, coef, strips, near, halo1, beside,
    kept, field, inner, gate, factor, in_sem, gate_sem, out_sem,
):
    members, rows, cols = density.shape
    half = rows // 2
    step = STEP
    blocks = rows // step

    def fetch(i, carry):
        for k in range(step):
            r = i * step + k
            pltpu.make_async_copy(density.at[:, r, :], field.at[r + 2], in_sem.at[i]).start()
        return carry

    def fetch_gate(i, carry):
        for k in range(step):
            r = i * step + k
            pltpu.make_async_copy(grow.at[:, r, :], gate.at[r], gate_sem.at[i]).start()
        return carry

    lax.fori_loop(0, blocks, fetch, 0)
    lax.fori_loop(0, blocks, fetch_gate, 0)
    for k in range(2):
        field[k] = strips[k]
        field[rows + 2 + k] = strips[2 + k]

    def clear(i, carry):
        for k in range(8):
            factor[i * 8 + k] = 1.0
        return carry

    lax.fori_loop(0, rows // 8, clear, 0)

    def leave(h, carry):
        r = hub_row[h]
        factor[r] = factor[r] - share[h]
        return carry

    lax.fori_loop(0, hub_row.shape[0], leave, 0)

    side = (members, cols)
    lane = lanes(side)
    first, last = lane == 0, lane == cols - 1

    edge = jnp.logical_or(first, last)
    band = (cols, cols)
    beside_mask = (jnp.abs(lanes(band) - sublanes(band)) == 1).astype(BF16)

    def lateral(c):
        flat = c.reshape(-1, cols)
        high = flat.astype(BF16)
        low = (flat - high.astype(F32)).astype(BF16)
        both = jnp.dot(high, beside_mask, preferred_element_type=F32)
        return (both + jnp.dot(low, beside_mask, preferred_element_type=F32)).reshape(c.shape)

    def relax(c, n, s, h, w, across):
        return c + w * ((n + s) + (across + jnp.where(edge, h, 0.0)) - 4.0 * c)

    def halo_row(ref, part, r):
        at = pl.ds(pl.multiple_of(part * members, 8), members)
        return pltpu.roll(ref[at, :], cols - 1 - 2 * (r - part * half), 1)

    def landed(i):
        ready = field.at[pl.ds(i * step + 2, step)]
        pltpu.make_async_copy(ready, ready, in_sem.at[i]).wait()

    landed(0)
    inner[0] = relax(field[1], field[0], field[2], beside[:members, :], coef[0:1, :], lateral(field[1]))

    def early(i, carry):
        @pl.when(i < blocks - 1)
        def _():
            landed(i + 1)

        part = i // (half // step)
        across = lateral(field[pl.ds(i * step + 2, step)])
        for k in range(step):
            r = i * step + k
            inner[r + 1] = relax(
                field[r + 2], field[r + 1], field[r + 3], halo_row(near, part, r), coef[pl.ds(r + 8, 1), :], across[k])
        return carry

    lax.fori_loop(0, blocks, early, 0)
    inner[rows + 1] = relax(
        field[rows + 2], field[rows + 1], field[rows + 3], beside[3 * members:, :], coef[rows + 8:rows + 9, :],
        lateral(field[rows + 2]))

    def late(i, carry):
        ready = gate.at[pl.ds(i * step, step)]
        pltpu.make_async_copy(ready, ready, gate_sem.at[i]).wait()
        part = i // (half // step)
        across = lateral(inner[pl.ds(i * step + 1, step)])
        for k in range(step):
            r = i * step + k
            d = relax(
                inner[r + 1], inner[r], inner[r + 2], halo_row(halo1, part, r), coef[pl.ds(r + 8, 1), :], across[k])
            gate[r] = d * factor[r] * gate[r]
        for k in range(step):
            r = i * step + k
            pltpu.make_async_copy(gate.at[r], kept.at[:, r, :], out_sem).start()
        return carry

    lax.fori_loop(0, blocks, late, 0)
    pltpu.make_async_copy(gate, gate, out_sem).wait()


def land_kernel(place, landed, kept, grow, *rest):
    blocks, rest = rest[:-12], rest[-12:]
    out, table, base, gate, carried, tags_v, tags_s, owner, lead, tag_sem, row_sem, out_sem = rest
    per = blocks[0].shape[0]
    bands, cols = tags_v.shape
    stride = landed.shape[0] // bands
    members, rows, _ = kept.shape
    depth = table.shape[1] - TAGS
    slots = bands * CAP
    for t in range(bands):
        tags = landed[t * stride + CAP * members:(t + 1) * stride, :].astype(F32)
        tags_v[t:t + 1, :] = tags[:1].astype(jnp.int32)
    copy = pltpu.make_async_copy(tags_v, tags_s, tag_sem)
    copy.start()
    for d, ref in enumerate(blocks):
        at = jnp.bitwise_xor(place[3], d) * per
        for c in range(per):
            table[at + c] = ref[c]

    def clear(r, carry):
        for k in range(8):
            owner[r * 8 + k] = -1
        return carry

    lax.fori_loop(0, rows // 8, clear, 0)
    copy.wait()

    def fetch(row, s):
        return (pltpu.make_async_copy(out.at[:, row, :], base.at[s], row_sem),
                pltpu.make_async_copy(grow.at[:, row, :], gate.at[s], row_sem))

    def store(row, s):
        return pltpu.make_async_copy(base.at[s], out.at[:, row, :], out_sem)

    def claim(s, count):
        row = tags_s[s // CAP, s % CAP]
        at = jnp.maximum(row, 0)
        mine = owner[at]
        fresh = jnp.logical_and(row >= 0, mine < 0)
        lead[s] = jnp.where(row < 0, slots, jnp.where(mine < 0, s, mine))

        @pl.when(fresh)
        def _():
            owner[at] = s
            for c in fetch(at, s):
                c.start()

        return count + jnp.where(fresh, 1, 0)

    count = lax.fori_loop(0, slots, claim, 0)

    def product(t, carry):
        for n in range(CAP):
            c = jnp.maximum(tags_s[t, CAP + n], 0)
            at = pl.ds(pl.multiple_of(t * stride + n * members, 16), members)
            x = jnp.dot(landed[at, :], table[c, :depth, :], preferred_element_type=F32)
            scale = table[c, depth:, :].astype(F32)[:1]
            carried[t * CAP + n] = (x * scale).astype(BF16).astype(F32)
        return carry

    lax.fori_loop(0, bands, product, 0, unroll=8)

    def arrive(s, carry):
        for c in fetch(0, 0):
            c.wait()
        return carry

    lax.fori_loop(0, count, arrive, 0)

    def add(t, carry):
        for n in range(CAP):
            to = lead[t * CAP + n]
            base[to] = base[to] + carried[t * CAP + n] * gate[to]
        return carry

    lax.fori_loop(0, bands, add, 0)

    def send(s, carry):
        @pl.when(lead[s] == s)
        def _():
            store(tags_s[s // CAP, s % CAP], s).start()
        return carry

    def finish(s, carry):
        store(0, 0).wait()
        return carry

    lax.fori_loop(0, slots, send, 0)
    lax.fori_loop(0, count, finish, 0)


def smem():
    return pl.BlockSpec(memory_space=pltpu.SMEM)


def vmem():
    return pl.BlockSpec(memory_space=pltpu.VMEM)


def anywhere():
    return pl.BlockSpec(memory_space=pl.ANY)


def hbm():
    return pl.BlockSpec(memory_space=pltpu.HBM)


def params(mib):
    return pltpu.CompilerParams(vmem_limit_bytes=int(mib * MIB))


def near_pairs(count):
    return [(i, i ^ 1) for i in range(count)]


def far_pairs(count):
    return [(i, j) for k in range(1, count - 1, 2) for i, j in ((k, k + 1), (k + 1, k))]


def local(
    density,
    habitat_class,
    suitability,
    dispersal_draw,
    threshold,
    hub_row,
    dest_tile,
    dest_row,
    county_id,
    jump_share,
    flow_tiles,
    flow_scale,
):
    members, rows, cols = density.shape
    bands, flows = lax.axis_size("tile"), lax.axis_size("flow")
    flow_scale = flow_scale.reshape(1, -1)
    density, dispersal_draw, habitat_class, flow_tiles, suitability, flow_scale, threshold = (
        pltpu.with_memory_space_constraint(x, pltpu.HBM)
        for x in (density, dispersal_draw, habitat_class, flow_tiles, suitability, flow_scale, threshold))
    t, f = lax.axis_index("tile"), lax.axis_index("flow")
    place = jnp.stack([t % 2, f % 2, t, f]).astype(jnp.int32)
    hubs, share = hub_row.reshape(-1), jump_share.reshape(-1)
    sds = jax.ShapeDtypeStruct
    per, depth = flow_tiles.shape[:2]
    message = sds((2 * members + TAIL, cols), F32)
    pack = sds((2 * members, cols), F32)
    cols_a, cols_b, rows_a, rows_b, own, weight, tiles, turned = pl.pallas_call(
        edges_kernel,
        out_shape=(message, message, message, message, pack, sds((rows, cols), F32),
                   sds((per, depth + TAGS, cols), BF16), sds((rows, members, cols), F32)),
        in_specs=[smem()] + [hbm()] * 5,
        out_specs=(vmem(),) * 8,
        scratch_shapes=[
            pltpu.VMEM(pack.shape, F32),
            pltpu.VMEM(pack.shape, F32),
            pltpu.VMEM((rows, cols), jnp.int32),
            pltpu.SMEM(suitability.shape, F32),
            pltpu.VMEM((1, per), BF16),
            pltpu.SemaphoreType.DMA((rows // CHUNK,)),
            pltpu.SemaphoreType.DMA((4,)),
        ],
        compiler_params=params(24),
        name="edges",
    )(place, density, habitat_class, suitability, flow_tiles, flow_scale)

    got_a = lax.ppermute(cols_a, "flow", near_pairs(flows))
    got_b = lax.ppermute(cols_b, "flow", far_pairs(flows))
    rows_a, rows_b = pl.pallas_call(
        corners_kernel,
        out_shape=(message, message),
        in_specs=[smem()] + [vmem()] * 4,
        out_specs=(vmem(), vmem()),
        compiler_params=params(24),
        name="corners",
    )(place, rows_a, rows_b, got_a, got_b)
    rows_a, rows_b, tiles, dispersal_draw = lax.optimization_barrier((rows_a, rows_b, tiles, dispersal_draw))
    strip_a = lax.ppermute(rows_a, "tile", near_pairs(bands))
    strip_b = lax.ppermute(rows_b, "tile", far_pairs(bands))

    def swap(x, bit):
        return lax.ppermute(x, "flow", [(i, i ^ bit) for i in range(flows)])

    grow = pl.pallas_call(
        grow_kernel,
        out_shape=pltpu.HBM(density.shape, F32),
        in_specs=[hbm(), hbm()],
        out_specs=hbm(),
        scratch_shapes=[
            pltpu.VMEM(density.shape, BF16),
            pltpu.VMEM(density.shape, F32),
            pltpu.VMEM((rows, cols), F32),
            pltpu.SemaphoreType.DMA((GROW,)),
            pltpu.SemaphoreType.DMA,
            pltpu.SemaphoreType.DMA,
        ],
        compiler_params=params(24),
        name="grow",
    )(dispersal_draw, threshold)
    grow = pltpu.with_memory_space_constraint(grow, pltpu.HBM)

    blocks = [tiles] + [None] * (flows - 1)
    bits = [1 << k for k in reversed(range((flows - 1).bit_length()))]
    for bit in bits:
        blocks[bit] = swap(tiles, bit)
    turned, grow, *early = lax.optimization_barrier([turned, grow] + [blocks[bit] for bit in bits])
    for bit, x in zip(bits, early):
        blocks[bit] = x
    for d in range(flows):
        if blocks[d] is None:
            blocks[d] = swap(blocks[d & (d - 1)], d & -d)

    stride = CAP * members + TAGS
    sent, near, halo1, beside, coef, strips = pl.pallas_call(
        hubs_kernel,
        out_shape=(sds((bands * stride, cols), BF16), pack, pack, sds((4 * members, cols), F32),
                   sds((rows + 16, cols), F32), sds((4, members, cols), F32)),
        in_specs=[smem()] * 6 + [vmem()] * 7,
        out_specs=(vmem(),) * 6,
        scratch_shapes=[pltpu.SMEM((bands,), jnp.int32)],
        compiler_params=params(24),
        name="hubs",
    )(place, hubs, dest_tile.reshape(-1), dest_row.reshape(-1), county_id.reshape(-1), share,
      turned, weight, own, got_a, got_b, strip_a, strip_b)

    landed = lax.all_to_all(sent, "tile", split_axis=0, concat_axis=0, tiled=True)
    kept = pl.pallas_call(
        bulk_kernel,
        out_shape=sds(density.shape, F32),
        in_specs=[smem(), smem(), hbm(), hbm()] + [vmem()] * 5,
        out_specs=hbm(),
        scratch_shapes=[
            pltpu.VMEM((rows + 4, members, cols), F32),
            pltpu.VMEM((rows + 2, members, cols), F32),
            pltpu.VMEM((rows, members, cols), F32),
            pltpu.SMEM((rows,), F32),
            pltpu.SemaphoreType.DMA((rows // STEP,)),
            pltpu.SemaphoreType.DMA((rows // STEP,)),
            pltpu.SemaphoreType.DMA,
        ],
        compiler_params=params(24),
        name="bulk",
    )(hubs, share, density, grow, coef, strips, near, halo1, beside)

    slots = bands * CAP
    out = pl.pallas_call(
        land_kernel,
        out_shape=sds(density.shape, F32),
        in_specs=[smem(), vmem(), hbm(), hbm()] + [vmem()] * flows,
        out_specs=hbm(),
        input_output_aliases={2: 0},
        scratch_shapes=[
            pltpu.VMEM((flows * per, depth + TAGS, cols), BF16),
            pltpu.VMEM((slots + 1, members, cols), F32),
            pltpu.VMEM((slots + 1, members, cols), F32),
            pltpu.VMEM((slots, members, cols), F32),
            pltpu.VMEM((bands, cols), jnp.int32),
            pltpu.SMEM((bands, cols), jnp.int32),
            pltpu.SMEM((rows,), jnp.int32),
            pltpu.SMEM((slots,), jnp.int32),
            pltpu.SemaphoreType.DMA,
            pltpu.SemaphoreType.DMA,
            pltpu.SemaphoreType.DMA,
        ],
        compiler_params=params(24),
        name="land",
    )(place, landed, kept, grow, *blocks)
    return out


def solution(mesh):
    in_specs = (
        P(None, "tile", "flow"),
        P("tile", "flow"),
        P(),
        P(None, "tile", "flow"),
        P("tile", "flow"),
        P("flow", "tile"),
        P("flow", "tile", None),
        P("flow", "tile"),
        P("flow", "tile"),
        P("flow", "tile"),
        P("flow", None, None),
        P("flow"),
    )
    out_specs = P(None, "tile", "flow")
    return jax.shard_map(local, mesh=mesh, in_specs=in_specs, out_specs=out_specs, check_vma=False)
```

```python
import jax
import jax.numpy as jnp
from jax import lax
from jax.experimental import pallas as pl
from jax.experimental.pallas import tpu as pltpu
from jax.sharding import PartitionSpec as P

CAP = 4
KAPPA = 0.24
SHARPNESS = 8.0
TAIL = 8
TAGS = 16
CHUNK = 16
UNROLL = 8
STEP = 16
GROW = 16
MIB = 1024 * 1024
F32 = jnp.float32
BF16 = jnp.bfloat16


def lanes(shape):
    return lax.broadcasted_iota(jnp.int32, shape, 1)


def sublanes(shape):
    return lax.broadcasted_iota(jnp.int32, shape, 0)


def edges_kernel(
    place, density, habitat, suit, tiles, scale,
    cols_a, cols_b, rows_a, rows_b, own, weight_out, tiles_out, turned,
    acc_e, acc_o, label_v, suit_v, scale_v, row_sems, sems,
):
    rows, members, cols = turned.shape
    half = rows // 2
    chunk = CHUNK
    t_even = place[0] == 0
    f_even = place[1] == 0
    depth = tiles.shape[1]
    small = [
        pltpu.make_async_copy(suit, suit_v, sems.at[0]),
        pltpu.make_async_copy(habitat, label_v, sems.at[1]),
        pltpu.make_async_copy(scale, scale_v, sems.at[2]),
        pltpu.make_async_copy(tiles, tiles_out.at[:, :depth, :], sems.at[3]),
    ]
    for copy in small:
        copy.start()

    def fetch(i, carry):
        for k in range(8):
            r = i * 8 + k
            pltpu.make_async_copy(density.at[:, r, :], turned.at[r], row_sems.at[i * 8 // chunk]).start()
        return carry

    lax.fori_loop(0, rows // 8, fetch, 0)
    for copy in small:
        copy.wait()

    shape = (rows, cols)
    label = label_v[...]
    weight = jnp.zeros(shape, F32)
    for c in range(suit_v.shape[0]):
        weight = jnp.where(label == c, suit_v[c], weight)
    weight_out[...] = weight
    pair_lane = lanes((half, cols)) // 2 == sublanes((half, cols))

    def spread(column):
        return jnp.sum(jnp.where(pair_lane, column, 0.0), axis=0, keepdims=True)

    row8 = sublanes((TAIL, cols))

    def side_weight(column):
        return jnp.where(row8 == 0, spread(column[:half]), spread(column[half:]))

    w_right = side_weight(weight[:, cols - 1:])
    w_left = side_weight(weight[:, :1])
    cols_a[2 * members:, :] = jnp.where(f_even, w_right, w_left)
    cols_b[2 * members:, :] = jnp.where(f_even, w_left, w_right)
    w_top = jnp.broadcast_to(weight[:1, :], (TAIL, cols))
    w_bottom = jnp.broadcast_to(weight[rows - 1:, :], (TAIL, cols))
    rows_a[2 * members:, :] = jnp.where(t_even, w_bottom, w_top)
    rows_b[2 * members:, :] = jnp.where(t_even, w_top, w_bottom)
    for c in range(tiles.shape[0]):
        value = scale_v[:, c:c + 1].astype(F32)
        tiles_out[c, depth:, :] = jnp.broadcast_to(value, (TAGS, cols)).astype(BF16)

    quad = lanes((8, cols)) // 4

    def pack(i, carry):
        ready = turned.at[pl.ds(i * chunk, chunk)]
        pltpu.make_async_copy(ready, ready, row_sems.at[i]).wait()
        part = i // (half // chunk)
        first = (i - part * (half // chunk)) * (chunk // 2)
        for g in range(members // 8):
            to = pl.ds(pl.multiple_of(part * members + 8 * g, 8), 8)
            even, odd = acc_e[to, :], acc_o[to, :]
            for j in range(chunk // 2):
                r = i * chunk + 2 * j
                q = first + j
                shift = 4 * q + 2
                hit = quad == q
                even = jnp.where(hit, pltpu.roll(turned[r, 8 * g:8 * g + 8, :], shift, 1), even)
                odd = jnp.where(hit, pltpu.roll(turned[r + 1, 8 * g:8 * g + 8, :], shift, 1), odd)
            acc_e[to, :] = even
            acc_o[to, :] = odd
        return carry

    lax.fori_loop(0, rows // chunk, pack, 0)

    wide = (2 * members, cols)
    low = lanes(wide) % 4 < 2
    even, odd = acc_e[...], acc_o[...]
    right = jnp.where(low, even, pltpu.roll(odd, 2, 1))
    left = jnp.where(low, pltpu.roll(even, cols - 2, 1), odd)
    own[...] = jnp.where(lanes(wide) % 2 == 0, pltpu.roll(right, cols - 1, 1), pltpu.roll(left, 1, 1))
    cols_a[:2 * members, :] = jnp.where(f_even, right, left)
    cols_b[:2 * members, :] = jnp.where(f_even, left, right)
    for k in range(2):
        to = pl.ds(k * members, members)
        rows_a[to, :] = turned[jnp.where(t_even, rows - 2, 0) + k]
        rows_b[to, :] = turned[jnp.where(t_even, 0, rows - 2) + k]


def corners_kernel(place, rows_a, rows_b, got_a, got_b, out_a, out_b):
    cols = got_a.shape[1]
    members = (got_a.shape[0] - TAIL) // 2
    t_even = place[0] == 0
    f_even = place[1] == 0
    side = (members, cols)
    swap = (lanes(side) % 2 == 1) == f_even
    top = jnp.where(swap, got_b[:members, :], got_a[:members, :])
    bottom = jnp.where(swap, got_b[members:2 * members, :], got_a[members:2 * members, :])

    def to_row(pair, first):
        east = jnp.where(lanes(side) == 2 * sublanes(side), pair[:, first:first + 1], 0.0)
        west = jnp.where(lanes(side) == 2 * sublanes(side) + 1, pair[:, first + 1:first + 2], 0.0)
        return jnp.sum(east + west, axis=0, keepdims=True)

    top_row = to_row(top, 0)
    bottom_row = to_row(bottom, cols - 2)
    out_a[...] = rows_a[...]
    out_b[...] = rows_b[...]
    at = 2 * members + 1
    out_a[at:at + 1, :] = jnp.where(t_even, bottom_row, top_row)
    out_b[at:at + 1, :] = jnp.where(t_even, top_row, bottom_row)


def hubs_kernel(
    place, hub_row, dest_tile, dest_row, county, share,
    turned, weight, own, cols_a, cols_b, rows_a, rows_b,
    sent, near, halo1, beside, coef, strips, counts,
):
    rows, members, cols = turned.shape
    bands = counts.shape[0]
    t_even = place[0] == 0
    f_even = place[1] == 0
    side = (members, cols)
    lane = lanes(side)
    even_lane = lane % 2 == 0

    tail_n = jnp.where(t_even, rows_b[2 * members:, :], rows_a[2 * members:, :])
    tail_s = jnp.where(t_even, rows_a[2 * members:, :], rows_b[2 * members:, :])
    for k in range(2):
        at = slice(k * members, (k + 1) * members)
        strips[k] = jnp.where(t_even, rows_b[at, :], rows_a[at, :])
        strips[2 + k] = jnp.where(t_even, rows_a[at, :], rows_b[at, :])
    coef[0:8, :] = KAPPA * tail_n
    coef[8:8 + rows, :] = KAPPA * weight[...]
    coef[8 + rows:, :] = KAPPA * tail_s

    def corner(tail):
        row = jnp.broadcast_to(tail[1:2, :], side)
        east = jnp.sum(jnp.where(lane == 2 * sublanes(side), row, 0.0), axis=1, keepdims=True)
        west = jnp.sum(jnp.where(lane == 2 * sublanes(side) + 1, row, 0.0), axis=1, keepdims=True)
        return east, west

    east_n, west_n = corner(tail_n)
    east_s, west_s = corner(tail_s)
    halves = []
    for k in range(2):
        at = slice(k * members, (k + 1) * members)
        a, b = cols_a[at, :], cols_b[at, :]
        from_e = jnp.where(f_even, a, b)
        from_w = jnp.where(f_even, b, a)
        close = jnp.where(even_lane, from_e, from_w)
        far = jnp.where(even_lane, pltpu.roll(from_e, cols - 1, 1), pltpu.roll(from_w, 1, 1))
        near[at, :] = close
        halves.append((close, far))
    wa, wb = cols_a[2 * members:, :], cols_b[2 * members:, :]
    w_e = jnp.where(f_even, wa, wb)
    w_w = jnp.where(f_even, wb, wa)
    w_packed = jnp.where(lanes((TAIL, cols)) % 2 == 0, w_e, w_w)
    near0, near1 = halves[0][0], halves[1][0]
    down0, down1 = pltpu.roll(near0, 2, 1), pltpu.roll(near1, 2, 1)
    up0, up1 = pltpu.roll(near0, cols - 2, 1), pltpu.roll(near1, cols - 2, 1)
    n0 = jnp.where(lane < 2, jnp.where(even_lane, east_n, west_n), down0)
    n1 = jnp.where(lane < 2, down0, down1)
    s0 = jnp.where(lane >= cols - 2, up1, up0)
    s1 = jnp.where(lane >= cols - 2, jnp.where(even_lane, east_s, west_s), up1)
    for k, (n, s) in enumerate(((n0, s0), (n1, s1))):
        at = slice(k * members, (k + 1) * members)
        close, far = halves[k]
        around = (n + s) + (far + own[at, :])
        halo1[at, :] = close + KAPPA * w_packed[k:k + 1, :] * (around - 4.0 * close)
    beside[0:members, :] = jnp.where(lane == 0, west_n, east_n)
    beside[members:2 * members, :] = pltpu.roll(near1, cols - 1, 1)
    beside[2 * members:3 * members, :] = pltpu.roll(near0, 1, 1)
    beside[3 * members:, :] = jnp.where(lane == 0, west_s, east_s)

    stride = CAP * members + TAGS
    tag_lane = lanes((TAGS, cols))
    for t in range(bands):
        counts[t] = 0
        sent[t * stride + CAP * members:(t + 1) * stride, :] = jnp.full((TAGS, cols), -1.0, BF16)
    half = rows // 2
    first, last = lane == 0, lane == cols - 1

    def field_row(r):
        inside = turned[jnp.clip(r, 0, rows - 1)]
        outside = strips[jnp.clip(jnp.where(r < 0, r + 2, r - rows + 2), 0, 3)]
        return jnp.where(jnp.logical_and(r >= 0, r < rows), inside, outside)

    def halo_row(ref, r):
        k = jnp.where(r >= half, 1, 0)
        at = pl.ds(pl.multiple_of(k * members, 8), members)
        return pltpu.roll(ref[at, :], cols - 1 - 2 * (r - k * half), 1)

    def side_row(r):
        edge = jnp.where(r < 0, beside[0:members, :], beside[3 * members:, :])
        inside = halo_row(near, jnp.clip(r, 0, rows - 1))
        return jnp.where(jnp.logical_and(r >= 0, r < rows), inside, edge)

    edge = jnp.logical_or(first, last)
    band = (cols, cols)
    mask = (jnp.abs(lanes(band) - sublanes(band)) == 1).astype(BF16)
    mask = jnp.concatenate([mask, mask], axis=0)

    def lateral(rows_in):
        flat = jnp.concatenate(rows_in, axis=0)
        high = flat.astype(BF16)
        low = (flat - high.astype(F32)).astype(BF16)
        both = jnp.dot(jnp.concatenate([high, low], axis=1), mask, preferred_element_type=F32)
        return [both[k * members:(k + 1) * members] for k in range(len(rows_in))]

    def relax(c, n, s, h, w, across):
        return c + w * ((n + s) + (across + jnp.where(edge, h, 0.0)) - 4.0 * c)

    def coef_row(r):
        at = jnp.where(r < 0, 0, r + 8)
        return coef[pl.ds(at, 1), :]

    def several(i, carry):
        chosen = [i * UNROLL + k for k in range(UNROLL)]
        spot = [hub_row[h] for h in chosen]
        u = [[field_row(r + k) for k in range(-2, 3)] for r in spot]
        across = lateral([u[k][c] for k in range(UNROLL) for c in (1, 2, 3)])
        v = []
        for k, r in enumerate(spot):
            v.append([
                relax(u[k][c + 2], u[k][c + 1], u[k][c + 3], side_row(r + c), coef_row(r + c), across[3 * k + c + 1])
                for c in range(-1, 2)])
        across = lateral([x[1] for x in v])
        for k, (h, r) in enumerate(zip(chosen, spot)):
            moved = share[h] * relax(v[k][1], v[k][0], v[k][2], halo_row(halo1, r), coef_row(r), across[k])
            to = dest_tile[h]
            n = counts[to]
            counts[to] = n + 1
            base = pl.multiple_of(to * stride, 16)
            sent[pl.ds(pl.multiple_of(base + n * members, 16), members), :] = moved.astype(BF16)
            at = pl.ds(pl.multiple_of(base + CAP * members, 16), TAGS)
            tags = sent[at, :].astype(F32)
            tags = jnp.where(tag_lane == n, dest_row[h].astype(F32), tags)
            tags = jnp.where(tag_lane == CAP + n, county[h].astype(F32), tags)
            sent[at, :] = tags.astype(BF16)
        return carry

    lax.fori_loop(0, hub_row.shape[0] // UNROLL, several, 0)


def grow_kernel(draw, threshold, grow, draw_v, grow_v, limit_v, in_sem, out_sem, sem):
    chunk = draw.shape[0] // GROW
    limit = pltpu.make_async_copy(threshold, limit_v, sem)
    limit.start()

    def fetch(i, carry):
        at = pl.ds(i * chunk, chunk)
        pltpu.make_async_copy(draw.at[at], draw_v.at[at], in_sem.at[i]).start()
        return carry

    lax.fori_loop(0, GROW, fetch, 0)
    limit.wait()

    def work(i, carry):
        at = pl.ds(i * chunk, chunk)
        pltpu.make_async_copy(draw.at[at], draw_v.at[at], in_sem.at[i]).wait()
        for k in range(chunk):
            x = 0.5 * SHARPNESS * (draw_v[i * chunk + k].astype(F32) - limit_v[...])
            grow_v[i * chunk + k] = 0.5 * jnp.tanh(x) + 0.5
        pltpu.make_async_copy(grow_v.at[at], grow.at[at], out_sem).start()
        return carry

    lax.fori_loop(0, GROW, work, 0)
    pltpu.make_async_copy(grow_v, grow, out_sem).wait()


def bulk_kernel(
    hub_row, share, density, grow, coef, strips, near, halo1, beside,
    kept, field, inner, gate, factor, in_sem, gate_sem, out_sem,
):
    members, rows, cols = density.shape
    half = rows // 2
    step = STEP
    blocks = rows // step

    def fetch(i, carry):
        for k in range(step):
            r = i * step + k
            pltpu.make_async_copy(density.at[:, r, :], field.at[r + 2], in_sem.at[i]).start()
        return carry

    def fetch_gate(i, carry):
        for k in range(step):
            r = i * step + k
            pltpu.make_async_copy(grow.at[:, r, :], gate.at[r], gate_sem.at[i]).start()
        return carry

    lax.fori_loop(0, blocks, fetch, 0)
    lax.fori_loop(0, blocks, fetch_gate, 0)
    for k in range(2):
        field[k] = strips[k]
        field[rows + 2 + k] = strips[2 + k]

    def clear(i, carry):
        for k in range(8):
            factor[i * 8 + k] = 1.0
        return carry

    lax.fori_loop(0, rows // 8, clear, 0)

    def leave(h, carry):
        r = hub_row[h]
        factor[r] = factor[r] - share[h]
        return carry

    lax.fori_loop(0, hub_row.shape[0], leave, 0)

    side = (members, cols)
    lane = lanes(side)
    first, last = lane == 0, lane == cols - 1

    edge = jnp.logical_or(first, last)
    band = (cols, cols)
    beside_mask = (jnp.abs(lanes(band) - sublanes(band)) == 1).astype(BF16)
    beside_mask = jnp.concatenate([beside_mask, beside_mask], axis=0)

    def lateral(c):
        flat = c.reshape(-1, cols)
        high = flat.astype(BF16)
        low = (flat - high.astype(F32)).astype(BF16)
        parts = jnp.concatenate([high, low], axis=1)
        return jnp.dot(parts, beside_mask, preferred_element_type=F32).reshape(c.shape)

    def relax(c, n, s, h, w, across):
        return c + w * ((n + s) + (across + jnp.where(edge, h, 0.0)) - 4.0 * c)

    def halo_row(ref, part, r):
        at = pl.ds(pl.multiple_of(part * members, 8), members)
        return pltpu.roll(ref[at, :], cols - 1 - 2 * (r - part * half), 1)

    def landed(i):
        ready = field.at[pl.ds(i * step + 2, step)]
        pltpu.make_async_copy(ready, ready, in_sem.at[i]).wait()

    landed(0)
    inner[0] = relax(field[1], field[0], field[2], beside[:members, :], coef[0:1, :], lateral(field[1]))

    def early(i, carry):
        @pl.when(i < blocks - 1)
        def _():
            landed(i + 1)

        part = i // (half // step)
        across = lateral(field[pl.ds(i * step + 2, step)])
        for k in range(step):
            r = i * step + k
            inner[r + 1] = relax(
                field[r + 2], field[r + 1], field[r + 3], halo_row(near, part, r), coef[pl.ds(r + 8, 1), :], across[k])
        return carry

    lax.fori_loop(0, blocks, early, 0)
    inner[rows + 1] = relax(
        field[rows + 2], field[rows + 1], field[rows + 3], beside[3 * members:, :], coef[rows + 8:rows + 9, :],
        lateral(field[rows + 2]))

    def late(i, carry):
        ready = gate.at[pl.ds(i * step, step)]
        pltpu.make_async_copy(ready, ready, gate_sem.at[i]).wait()
        part = i // (half // step)
        across = lateral(inner[pl.ds(i * step + 1, step)])
        for k in range(step):
            r = i * step + k
            d = relax(
                inner[r + 1], inner[r], inner[r + 2], halo_row(halo1, part, r), coef[pl.ds(r + 8, 1), :], across[k])
            gate[r] = d * factor[r] * gate[r]
        for k in range(step):
            r = i * step + k
            pltpu.make_async_copy(gate.at[r], kept.at[:, r, :], out_sem).start()
        return carry

    lax.fori_loop(0, blocks, late, 0)
    pltpu.make_async_copy(gate, gate, out_sem).wait()


def land_kernel(place, landed, kept, grow, *rest):
    blocks, rest = rest[:-12], rest[-12:]
    out, table, base, gate, carried, tags_v, tags_s, owner, lead, tag_sem, row_sem, out_sem = rest
    per = blocks[0].shape[0]
    bands, cols = tags_v.shape
    stride = landed.shape[0] // bands
    members, rows, _ = kept.shape
    depth = table.shape[1] - TAGS
    slots = bands * CAP
    for t in range(bands):
        tags = landed[t * stride + CAP * members:(t + 1) * stride, :].astype(F32)
        tags_v[t:t + 1, :] = tags[:1].astype(jnp.int32)
    copy = pltpu.make_async_copy(tags_v, tags_s, tag_sem)
    copy.start()
    for d, ref in enumerate(blocks):
        at = jnp.bitwise_xor(place[3], d) * per
        for c in range(per):
            table[at + c] = ref[c]

    def clear(r, carry):
        for k in range(8):
            owner[r * 8 + k] = -1
        return carry

    lax.fori_loop(0, rows // 8, clear, 0)
    copy.wait()

    def fetch(row, s):
        return (pltpu.make_async_copy(out.at[:, row, :], base.at[s], row_sem),
                pltpu.make_async_copy(grow.at[:, row, :], gate.at[s], row_sem))

    def store(row, s):
        return pltpu.make_async_copy(base.at[s], out.at[:, row, :], out_sem)

    def claim(s, count):
        row = tags_s[s // CAP, s % CAP]
        at = jnp.maximum(row, 0)
        mine = owner[at]
        fresh = jnp.logical_and(row >= 0, mine < 0)
        lead[s] = jnp.where(row < 0, slots, jnp.where(mine < 0, s, mine))

        @pl.when(fresh)
        def _():
            owner[at] = s
            for c in fetch(at, s):
                c.start()

        return count + jnp.where(fresh, 1, 0)

    count = lax.fori_loop(0, slots, claim, 0)

    def product(t, carry):
        for n in range(CAP):
            c = jnp.maximum(tags_s[t, CAP + n], 0)
            at = pl.ds(pl.multiple_of(t * stride + n * members, 16), members)
            x = jnp.dot(landed[at, :], table[c, :depth, :], preferred_element_type=F32)
            scale = table[c, depth:, :].astype(F32)[:1]
            carried[t * CAP + n] = (x * scale).astype(BF16).astype(F32)
        return carry

    lax.fori_loop(0, bands, product, 0, unroll=8)

    def arrive(s, carry):
        for c in fetch(0, 0):
            c.wait()
        return carry

    lax.fori_loop(0, count, arrive, 0)

    def add(t, carry):
        for n in range(CAP):
            to = lead[t * CAP + n]
            base[to] = base[to] + carried[t * CAP + n] * gate[to]
        return carry

    lax.fori_loop(0, bands, add, 0)

    def send(s, carry):
        @pl.when(lead[s] == s)
        def _():
            store(tags_s[s // CAP, s % CAP], s).start()
        return carry

    def finish(s, carry):
        store(0, 0).wait()
        return carry

    lax.fori_loop(0, slots, send, 0)
    lax.fori_loop(0, count, finish, 0)


def smem():
    return pl.BlockSpec(memory_space=pltpu.SMEM)


def vmem():
    return pl.BlockSpec(memory_space=pltpu.VMEM)


def anywhere():
    return pl.BlockSpec(memory_space=pl.ANY)


def hbm():
    return pl.BlockSpec(memory_space=pltpu.HBM)


def params(mib):
    return pltpu.CompilerParams(vmem_limit_bytes=int(mib * MIB))


def near_pairs(count):
    return [(i, i ^ 1) for i in range(count)]


def far_pairs(count):
    return [(i, j) for k in range(1, count - 1, 2) for i, j in ((k, k + 1), (k + 1, k))]


def local(
    density,
    habitat_class,
    suitability,
    dispersal_draw,
    threshold,
    hub_row,
    dest_tile,
    dest_row,
    county_id,
    jump_share,
    flow_tiles,
    flow_scale,
):
    members, rows, cols = density.shape
    bands, flows = lax.axis_size("tile"), lax.axis_size("flow")
    flow_scale = flow_scale.reshape(1, -1)
    density, dispersal_draw, habitat_class, flow_tiles, suitability, flow_scale, threshold = (
        pltpu.with_memory_space_constraint(x, pltpu.HBM)
        for x in (density, dispersal_draw, habitat_class, flow_tiles, suitability, flow_scale, threshold))
    t, f = lax.axis_index("tile"), lax.axis_index("flow")
    place = jnp.stack([t % 2, f % 2, t, f]).astype(jnp.int32)
    hubs, share = hub_row.reshape(-1), jump_share.reshape(-1)
    sds = jax.ShapeDtypeStruct
    per, depth = flow_tiles.shape[:2]
    message = sds((2 * members + TAIL, cols), F32)
    pack = sds((2 * members, cols), F32)
    cols_a, cols_b, rows_a, rows_b, own, weight, tiles, turned = pl.pallas_call(
        edges_kernel,
        out_shape=(message, message, message, message, pack, sds((rows, cols), F32),
                   sds((per, depth + TAGS, cols), BF16), sds((rows, members, cols), F32)),
        in_specs=[smem()] + [hbm()] * 5,
        out_specs=(vmem(),) * 8,
        scratch_shapes=[
            pltpu.VMEM(pack.shape, F32),
            pltpu.VMEM(pack.shape, F32),
            pltpu.VMEM((rows, cols), jnp.int32),
            pltpu.SMEM(suitability.shape, F32),
            pltpu.VMEM((1, per), BF16),
            pltpu.SemaphoreType.DMA((rows // CHUNK,)),
            pltpu.SemaphoreType.DMA((4,)),
        ],
        compiler_params=params(24),
        name="edges",
    )(place, density, habitat_class, suitability, flow_tiles, flow_scale)

    got_a = lax.ppermute(cols_a, "flow", near_pairs(flows))
    got_b = lax.ppermute(cols_b, "flow", far_pairs(flows))
    rows_a, rows_b = pl.pallas_call(
        corners_kernel,
        out_shape=(message, message),
        in_specs=[smem()] + [vmem()] * 4,
        out_specs=(vmem(), vmem()),
        compiler_params=params(24),
        name="corners",
    )(place, rows_a, rows_b, got_a, got_b)
    rows_a, rows_b, dispersal_draw = lax.optimization_barrier((rows_a, rows_b, dispersal_draw))
    strip_a = lax.ppermute(rows_a, "tile", near_pairs(bands))
    strip_b = lax.ppermute(rows_b, "tile", far_pairs(bands))

    def swap(x, bit):
        return lax.ppermute(x, "flow", [(i, i ^ bit) for i in range(flows)])

    grow = pl.pallas_call(
        grow_kernel,
        out_shape=pltpu.HBM(density.shape, F32),
        in_specs=[hbm(), hbm()],
        out_specs=hbm(),
        scratch_shapes=[
            pltpu.VMEM(density.shape, BF16),
            pltpu.VMEM(density.shape, F32),
            pltpu.VMEM((rows, cols), F32),
            pltpu.SemaphoreType.DMA((GROW,)),
            pltpu.SemaphoreType.DMA,
            pltpu.SemaphoreType.DMA,
        ],
        compiler_params=params(24),
        name="grow",
    )(dispersal_draw, threshold)
    grow = pltpu.with_memory_space_constraint(grow, pltpu.HBM)

    blocks = [tiles] + [swap(tiles, d) for d in range(1, flows)]
    turned, grow = lax.optimization_barrier((turned, grow))

    stride = CAP * members + TAGS
    sent, near, halo1, beside, coef, strips = pl.pallas_call(
        hubs_kernel,
        out_shape=(sds((bands * stride, cols), BF16), pack, pack, sds((4 * members, cols), F32),
                   sds((rows + 16, cols), F32), sds((4, members, cols), F32)),
        in_specs=[smem()] * 6 + [vmem()] * 7,
        out_specs=(vmem(),) * 6,
        scratch_shapes=[pltpu.SMEM((bands,), jnp.int32)],
        compiler_params=params(24),
        name="hubs",
    )(place, hubs, dest_tile.reshape(-1), dest_row.reshape(-1), county_id.reshape(-1), share,
      turned, weight, own, got_a, got_b, strip_a, strip_b)

    landed = lax.all_to_all(sent, "tile", split_axis=0, concat_axis=0, tiled=True)
    kept = pl.pallas_call(
        bulk_kernel,
        out_shape=sds(density.shape, F32),
        in_specs=[smem(), smem(), hbm(), hbm()] + [vmem()] * 5,
        out_specs=hbm(),
        scratch_shapes=[
            pltpu.VMEM((rows + 4, members, cols), F32),
            pltpu.VMEM((rows + 2, members, cols), F32),
            pltpu.VMEM((rows, members, cols), F32),
            pltpu.SMEM((rows,), F32),
            pltpu.SemaphoreType.DMA((rows // STEP,)),
            pltpu.SemaphoreType.DMA((rows // STEP,)),
            pltpu.SemaphoreType.DMA,
        ],
        compiler_params=params(24),
        name="bulk",
    )(hubs, share, density, grow, coef, strips, near, halo1, beside)

    slots = bands * CAP
    out = pl.pallas_call(
        land_kernel,
        out_shape=sds(density.shape, F32),
        in_specs=[smem(), vmem(), hbm(), hbm()] + [vmem()] * flows,
        out_specs=hbm(),
        input_output_aliases={2: 0},
        scratch_shapes=[
            pltpu.VMEM((flows * per, depth + TAGS, cols), BF16),
            pltpu.VMEM((slots + 1, members, cols), F32),
            pltpu.VMEM((slots + 1, members, cols), F32),
            pltpu.VMEM((slots, members, cols), F32),
            pltpu.VMEM((bands, cols), jnp.int32),
            pltpu.SMEM((bands, cols), jnp.int32),
            pltpu.SMEM((rows,), jnp.int32),
            pltpu.SMEM((slots,), jnp.int32),
            pltpu.SemaphoreType.DMA,
            pltpu.SemaphoreType.DMA,
            pltpu.SemaphoreType.DMA,
        ],
        compiler_params=params(24),
        name="land",
    )(place, landed, kept, grow, *blocks)
    return out


def solution(mesh):
    in_specs = (
        P(None, "tile", "flow"),
        P("tile", "flow"),
        P(),
        P(None, "tile", "flow"),
        P("tile", "flow"),
        P("flow", "tile"),
        P("flow", "tile", None),
        P("flow", "tile"),
        P("flow", "tile"),
        P("flow", "tile"),
        P("flow", None, None),
        P("flow"),
    )
    out_specs = P(None, "tile", "flow")
    return jax.shard_map(local, mesh=mesh, in_specs=in_specs, out_specs=out_specs, check_vma=False)
```

```python
import jax
import jax.numpy as jnp
from jax import lax
from jax.experimental import pallas as pl
from jax.experimental.pallas import tpu as pltpu
from jax.sharding import PartitionSpec as P

CAP = 4
KAPPA = 0.24
SHARPNESS = 8.0
TAIL = 16
TAGS = 16
CHUNK = 16
UNROLL = 8
STEP = 16
GROW = 16
MIB = 1024 * 1024
F32 = jnp.float32
BF16 = jnp.bfloat16


def lanes(shape):
    return lax.broadcasted_iota(jnp.int32, shape, 1)


def sublanes(shape):
    return lax.broadcasted_iota(jnp.int32, shape, 0)


def edges_kernel(
    place, density, habitat, suit, tiles, scale,
    cols_a, cols_b, rows_a, rows_b, own, weight_out, tiles_out, turned,
    acc_e, acc_o, label_v, suit_v, scale_v, row_sems, sems,
):
    rows, members, cols = turned.shape
    half = rows // 2
    chunk = CHUNK
    t_even = place[0] == 0
    f_even = place[1] == 0
    depth = tiles.shape[1]
    small = [
        pltpu.make_async_copy(suit, suit_v, sems.at[0]),
        pltpu.make_async_copy(habitat, label_v, sems.at[1]),
        pltpu.make_async_copy(scale, scale_v, sems.at[2]),
        pltpu.make_async_copy(tiles, tiles_out.at[:, :depth, :], sems.at[3]),
    ]
    for copy in small:
        copy.start()

    def fetch(i, carry):
        for k in range(8):
            r = i * 8 + k
            pltpu.make_async_copy(density.at[:, r, :], turned.at[r], row_sems.at[i * 8 // chunk]).start()
        return carry

    lax.fori_loop(0, rows // 8, fetch, 0)
    for copy in small:
        copy.wait()

    shape = (rows, cols)
    label = label_v[...]
    weight = jnp.zeros(shape, F32)
    for c in range(suit_v.shape[0]):
        weight = jnp.where(label == c, suit_v[c], weight)
    weight_out[...] = weight
    pair_lane = lanes((half, cols)) // 2 == sublanes((half, cols))

    def spread(column):
        return jnp.sum(jnp.where(pair_lane, column, 0.0), axis=0, keepdims=True)

    row8 = sublanes((TAIL, cols))

    def split(value):
        high = value.astype(BF16).astype(F32)
        return high, value - high

    def side_weight(column):
        high0, low0 = split(spread(column[:half]))
        high1, low1 = split(spread(column[half:]))
        lows = jnp.where(row8 == 2, low0, low1)
        return jnp.where(row8 == 0, high0, jnp.where(row8 == 1, high1, lows))

    w_right = side_weight(weight[:, cols - 1:])
    w_left = side_weight(weight[:, :1])
    cols_a[2 * members:, :] = jnp.where(f_even, w_right, w_left).astype(BF16)
    cols_b[2 * members:, :] = jnp.where(f_even, w_left, w_right).astype(BF16)

    def rim_weight(row):
        high, low = split(row)
        return jnp.where(row8 == 0, high, low)

    w_top = rim_weight(weight[:1, :])
    w_bottom = rim_weight(weight[rows - 1:, :])
    rows_a[2 * members:, :] = jnp.where(t_even, w_bottom, w_top).astype(BF16)
    rows_b[2 * members:, :] = jnp.where(t_even, w_top, w_bottom).astype(BF16)
    for c in range(tiles.shape[0]):
        value = scale_v[:, c:c + 1].astype(F32)
        tiles_out[c, depth:, :] = jnp.broadcast_to(value, (TAGS, cols)).astype(BF16)

    quad = lanes((8, cols)) // 4

    def pack(i, carry):
        ready = turned.at[pl.ds(i * chunk, chunk)]
        pltpu.make_async_copy(ready, ready, row_sems.at[i]).wait()
        part = i // (half // chunk)
        first = (i - part * (half // chunk)) * (chunk // 2)
        for g in range(members // 8):
            to = pl.ds(pl.multiple_of(part * members + 8 * g, 8), 8)
            even, odd = acc_e[to, :], acc_o[to, :]
            for j in range(chunk // 2):
                r = i * chunk + 2 * j
                q = first + j
                shift = 4 * q + 2
                hit = quad == q
                even = jnp.where(hit, pltpu.roll(turned[r, 8 * g:8 * g + 8, :], shift, 1), even)
                odd = jnp.where(hit, pltpu.roll(turned[r + 1, 8 * g:8 * g + 8, :], shift, 1), odd)
            acc_e[to, :] = even
            acc_o[to, :] = odd
        return carry

    lax.fori_loop(0, rows // chunk, pack, 0)

    wide = (2 * members, cols)
    low = lanes(wide) % 4 < 2
    even, odd = acc_e[...], acc_o[...]
    right = jnp.where(low, even, pltpu.roll(odd, 2, 1))
    left = jnp.where(low, pltpu.roll(even, cols - 2, 1), odd)
    own[...] = jnp.where(lanes(wide) % 2 == 0, pltpu.roll(right, cols - 1, 1), pltpu.roll(left, 1, 1))
    cols_a[:2 * members, :] = jnp.where(f_even, right, left).astype(BF16)
    cols_b[:2 * members, :] = jnp.where(f_even, left, right).astype(BF16)
    for k in range(2):
        to = pl.ds(k * members, members)
        rows_a[to, :] = turned[jnp.where(t_even, rows - 2, 0) + k].astype(BF16)
        rows_b[to, :] = turned[jnp.where(t_even, 0, rows - 2) + k].astype(BF16)


def corners_kernel(place, rows_a, rows_b, got_a, got_b, out_a, out_b):
    cols = got_a.shape[1]
    members = (got_a.shape[0] - TAIL) // 2
    t_even = place[0] == 0
    f_even = place[1] == 0
    side = (members, cols)
    swap = (lanes(side) % 2 == 1) == f_even
    top = jnp.where(swap, got_b[:members, :].astype(F32), got_a[:members, :].astype(F32))
    low = slice(members, 2 * members)
    bottom = jnp.where(swap, got_b[low, :].astype(F32), got_a[low, :].astype(F32))

    def to_row(pair, first):
        east = jnp.where(lanes(side) == 2 * sublanes(side), pair[:, first:first + 1], 0.0)
        west = jnp.where(lanes(side) == 2 * sublanes(side) + 1, pair[:, first + 1:first + 2], 0.0)
        return jnp.sum(east + west, axis=0, keepdims=True)

    top_row = to_row(top, 0)
    bottom_row = to_row(bottom, cols - 2)
    last = 2 * members
    second = sublanes((TAIL, cols)) == 1
    for out, ref, first, other in ((out_a, rows_a, bottom_row, top_row), (out_b, rows_b, top_row, bottom_row)):
        out[:last, :] = ref[:last, :]
        corner = jnp.where(t_even, first, other)
        out[last:, :] = jnp.where(second, corner, ref[last:, :].astype(F32)).astype(BF16)


def hubs_kernel(
    place, hub_row, dest_tile, dest_row, county, share,
    turned, weight, own, cols_a, cols_b, rows_a, rows_b,
    sent, near, halo1, beside, coef, strips, counts,
):
    rows, members, cols = turned.shape
    bands = counts.shape[0]
    t_even = place[0] == 0
    f_even = place[1] == 0
    side = (members, cols)
    lane = lanes(side)
    even_lane = lane % 2 == 0

    tail_a = rows_a[2 * members:, :].astype(F32)
    tail_b = rows_b[2 * members:, :].astype(F32)
    tail_n = jnp.where(t_even, tail_b, tail_a)
    tail_s = jnp.where(t_even, tail_a, tail_b)
    for k in range(2):
        at = slice(k * members, (k + 1) * members)
        row_a, row_b = rows_a[at, :].astype(F32), rows_b[at, :].astype(F32)
        strips[k] = jnp.where(t_even, row_b, row_a)
        strips[2 + k] = jnp.where(t_even, row_a, row_b)
    coef[0:8, :] = jnp.broadcast_to(KAPPA * (tail_n[0:1] + tail_n[2:3]), (8, cols))
    coef[8:8 + rows, :] = KAPPA * weight[...]
    coef[8 + rows:, :] = jnp.broadcast_to(KAPPA * (tail_s[0:1] + tail_s[2:3]), (8, cols))

    def corner(tail):
        row = jnp.broadcast_to(tail[1:2, :], side)
        east = jnp.sum(jnp.where(lane == 2 * sublanes(side), row, 0.0), axis=1, keepdims=True)
        west = jnp.sum(jnp.where(lane == 2 * sublanes(side) + 1, row, 0.0), axis=1, keepdims=True)
        return east, west

    east_n, west_n = corner(tail_n)
    east_s, west_s = corner(tail_s)
    halves = []
    for k in range(2):
        at = slice(k * members, (k + 1) * members)
        a, b = cols_a[at, :].astype(F32), cols_b[at, :].astype(F32)
        from_e = jnp.where(f_even, a, b)
        from_w = jnp.where(f_even, b, a)
        close = jnp.where(even_lane, from_e, from_w)
        far = jnp.where(even_lane, pltpu.roll(from_e, cols - 1, 1), pltpu.roll(from_w, 1, 1))
        near[at, :] = close
        halves.append((close, far))
    wa, wb = cols_a[2 * members:, :].astype(F32), cols_b[2 * members:, :].astype(F32)
    w_e = jnp.where(f_even, wa, wb)
    w_w = jnp.where(f_even, wb, wa)
    w_packed = jnp.where(lanes((TAIL, cols)) % 2 == 0, w_e, w_w)
    near0, near1 = halves[0][0], halves[1][0]
    down0, down1 = pltpu.roll(near0, 2, 1), pltpu.roll(near1, 2, 1)
    up0, up1 = pltpu.roll(near0, cols - 2, 1), pltpu.roll(near1, cols - 2, 1)
    n0 = jnp.where(lane < 2, jnp.where(even_lane, east_n, west_n), down0)
    n1 = jnp.where(lane < 2, down0, down1)
    s0 = jnp.where(lane >= cols - 2, up1, up0)
    s1 = jnp.where(lane >= cols - 2, jnp.where(even_lane, east_s, west_s), up1)
    for k, (n, s) in enumerate(((n0, s0), (n1, s1))):
        at = slice(k * members, (k + 1) * members)
        close, far = halves[k]
        around = (n + s) + (far + own[at, :])
        w = KAPPA * (w_packed[k:k + 1, :] + w_packed[k + 2:k + 3, :])
        halo1[at, :] = close + w * (around - 4.0 * close)
    beside[0:members, :] = jnp.where(lane == 0, west_n, east_n)
    beside[members:2 * members, :] = pltpu.roll(near1, cols - 1, 1)
    beside[2 * members:3 * members, :] = pltpu.roll(near0, 1, 1)
    beside[3 * members:, :] = jnp.where(lane == 0, west_s, east_s)

    stride = CAP * members + TAGS
    tag_lane = lanes((TAGS, cols))
    for t in range(bands):
        counts[t] = 0
        sent[t * stride + CAP * members:(t + 1) * stride, :] = jnp.full((TAGS, cols), -1.0, BF16)
    half = rows // 2
    first, last = lane == 0, lane == cols - 1

    def field_row(r):
        inside = turned[jnp.clip(r, 0, rows - 1)]
        outside = strips[jnp.clip(jnp.where(r < 0, r + 2, r - rows + 2), 0, 3)]
        return jnp.where(jnp.logical_and(r >= 0, r < rows), inside, outside)

    def halo_row(ref, r):
        k = jnp.where(r >= half, 1, 0)
        at = pl.ds(pl.multiple_of(k * members, 8), members)
        return pltpu.roll(ref[at, :], cols - 1 - 2 * (r - k * half), 1)

    def side_row(r):
        edge = jnp.where(r < 0, beside[0:members, :], beside[3 * members:, :])
        inside = halo_row(near, jnp.clip(r, 0, rows - 1))
        return jnp.where(jnp.logical_and(r >= 0, r < rows), inside, edge)

    edge = jnp.logical_or(first, last)
    band = (cols, cols)
    mask = (jnp.abs(lanes(band) - sublanes(band)) == 1).astype(BF16)
    mask = jnp.concatenate([mask, mask], axis=0)

    def lateral(rows_in):
        flat = jnp.concatenate(rows_in, axis=0)
        high = flat.astype(BF16)
        low = (flat - high.astype(F32)).astype(BF16)
        both = jnp.dot(jnp.concatenate([high, low], axis=1), mask, preferred_element_type=F32)
        return [both[k * members:(k + 1) * members] for k in range(len(rows_in))]

    def relax(c, n, s, h, w, across):
        return c + w * ((n + s) + (across + jnp.where(edge, h, 0.0)) - 4.0 * c)

    def coef_row(r):
        at = jnp.where(r < 0, 0, r + 8)
        return coef[pl.ds(at, 1), :]

    def several(i, carry):
        chosen = [i * UNROLL + k for k in range(UNROLL)]
        spot = [hub_row[h] for h in chosen]
        u = [[field_row(r + k) for k in range(-2, 3)] for r in spot]
        across = lateral([u[k][c] for k in range(UNROLL) for c in (1, 2, 3)])
        v = []
        for k, r in enumerate(spot):
            v.append([
                relax(u[k][c + 2], u[k][c + 1], u[k][c + 3], side_row(r + c), coef_row(r + c), across[3 * k + c + 1])
                for c in range(-1, 2)])
        across = lateral([x[1] for x in v])
        for k, (h, r) in enumerate(zip(chosen, spot)):
            moved = share[h] * relax(v[k][1], v[k][0], v[k][2], halo_row(halo1, r), coef_row(r), across[k])
            to = dest_tile[h]
            n = counts[to]
            counts[to] = n + 1
            base = pl.multiple_of(to * stride, 16)
            sent[pl.ds(pl.multiple_of(base + n * members, 16), members), :] = moved.astype(BF16)
            at = pl.ds(pl.multiple_of(base + CAP * members, 16), TAGS)
            tags = sent[at, :].astype(F32)
            tags = jnp.where(tag_lane == n, dest_row[h].astype(F32), tags)
            tags = jnp.where(tag_lane == CAP + n, county[h].astype(F32), tags)
            sent[at, :] = tags.astype(BF16)
        return carry

    lax.fori_loop(0, hub_row.shape[0] // UNROLL, several, 0)


def grow_kernel(draw, threshold, grow, draw_v, grow_v, limit_v, in_sem, out_sem, sem):
    chunk = draw.shape[0] // GROW
    limit = pltpu.make_async_copy(threshold, limit_v, sem)
    limit.start()

    def fetch(i, carry):
        at = pl.ds(i * chunk, chunk)
        pltpu.make_async_copy(draw.at[at], draw_v.at[at], in_sem.at[i]).start()
        return carry

    lax.fori_loop(0, GROW, fetch, 0)
    limit.wait()

    def work(i, carry):
        at = pl.ds(i * chunk, chunk)
        pltpu.make_async_copy(draw.at[at], draw_v.at[at], in_sem.at[i]).wait()
        for k in range(chunk):
            x = 0.5 * SHARPNESS * (draw_v[i * chunk + k].astype(F32) - limit_v[...])
            grow_v[i * chunk + k] = 0.5 * jnp.tanh(x) + 0.5
        pltpu.make_async_copy(grow_v.at[at], grow.at[at], out_sem).start()
        return carry

    lax.fori_loop(0, GROW, work, 0)
    pltpu.make_async_copy(grow_v, grow, out_sem).wait()


def bulk_kernel(
    hub_row, share, density, grow, coef, strips, near, halo1, beside,
    kept, field, inner, gate, factor, in_sem, gate_sem, out_sem,
):
    members, rows, cols = density.shape
    half = rows // 2
    step = STEP
    blocks = rows // step

    def fetch(i, carry):
        for k in range(step):
            r = i * step + k
            pltpu.make_async_copy(density.at[:, r, :], field.at[r + 2], in_sem.at[i]).start()
        return carry

    def fetch_gate(i, carry):
        for k in range(step):
            r = i * step + k
            pltpu.make_async_copy(grow.at[:, r, :], gate.at[r], gate_sem.at[i]).start()
        return carry

    lax.fori_loop(0, blocks, fetch, 0)
    lax.fori_loop(0, blocks, fetch_gate, 0)
    for k in range(2):
        field[k] = strips[k]
        field[rows + 2 + k] = strips[2 + k]

    def clear(i, carry):
        for k in range(8):
            factor[i * 8 + k] = 1.0
        return carry

    lax.fori_loop(0, rows // 8, clear, 0)

    def leave(h, carry):
        r = hub_row[h]
        factor[r] = factor[r] - share[h]
        return carry

    lax.fori_loop(0, hub_row.shape[0], leave, 0)

    side = (members, cols)
    lane = lanes(side)
    first, last = lane == 0, lane == cols - 1

    edge = jnp.logical_or(first, last)
    band = (cols, cols)
    beside_mask = (jnp.abs(lanes(band) - sublanes(band)) == 1).astype(BF16)
    beside_mask = jnp.concatenate([beside_mask, beside_mask], axis=0)

    def lateral(c):
        flat = c.reshape(-1, cols)
        high = flat.astype(BF16)
        low = (flat - high.astype(F32)).astype(BF16)
        parts = jnp.concatenate([high, low], axis=1)
        return jnp.dot(parts, beside_mask, preferred_element_type=F32).reshape(c.shape)

    def relax(c, n, s, h, w, across):
        return c + w * ((n + s) + (across + jnp.where(edge, h, 0.0)) - 4.0 * c)

    def halo_row(ref, part, r):
        at = pl.ds(pl.multiple_of(part * members, 8), members)
        return pltpu.roll(ref[at, :], cols - 1 - 2 * (r - part * half), 1)

    def landed(i):
        ready = field.at[pl.ds(i * step + 2, step)]
        pltpu.make_async_copy(ready, ready, in_sem.at[i]).wait()

    landed(0)
    inner[0] = relax(field[1], field[0], field[2], beside[:members, :], coef[0:1, :], lateral(field[1]))

    def early(i, carry):
        @pl.when(i < blocks - 1)
        def _():
            landed(i + 1)

        part = i // (half // step)
        across = lateral(field[pl.ds(i * step + 2, step)])
        for k in range(step):
            r = i * step + k
            inner[r + 1] = relax(
                field[r + 2], field[r + 1], field[r + 3], halo_row(near, part, r), coef[pl.ds(r + 8, 1), :], across[k])
        return carry

    lax.fori_loop(0, blocks, early, 0)
    inner[rows + 1] = relax(
        field[rows + 2], field[rows + 1], field[rows + 3], beside[3 * members:, :], coef[rows + 8:rows + 9, :],
        lateral(field[rows + 2]))

    def late(i, carry):
        ready = gate.at[pl.ds(i * step, step)]
        pltpu.make_async_copy(ready, ready, gate_sem.at[i]).wait()
        part = i // (half // step)
        across = lateral(inner[pl.ds(i * step + 1, step)])
        for k in range(step):
            r = i * step + k
            d = relax(
                inner[r + 1], inner[r], inner[r + 2], halo_row(halo1, part, r), coef[pl.ds(r + 8, 1), :], across[k])
            gate[r] = d * factor[r] * gate[r]
        for k in range(step):
            r = i * step + k
            pltpu.make_async_copy(gate.at[r], kept.at[:, r, :], out_sem).start()
        return carry

    lax.fori_loop(0, blocks, late, 0)
    pltpu.make_async_copy(gate, gate, out_sem).wait()


def land_kernel(place, landed, kept, grow, *rest):
    blocks, rest = rest[:-13], rest[-13:]
    out, table, base, gate, carried, tags_v, tags_s, owner, lead, final, tag_sem, row_sem, out_sem = rest
    per = blocks[0].shape[0]
    bands, cols = tags_v.shape
    stride = landed.shape[0] // bands
    members, rows, _ = kept.shape
    depth = table.shape[1] - TAGS
    slots = bands * CAP
    for t in range(bands):
        tags = landed[t * stride + CAP * members:(t + 1) * stride, :].astype(F32)
        tags_v[t:t + 1, :] = tags[:1].astype(jnp.int32)
    copy = pltpu.make_async_copy(tags_v, tags_s, tag_sem)
    copy.start()
    for d, ref in enumerate(blocks):
        at = jnp.bitwise_xor(place[3], d) * per
        for c in range(per):
            table[at + c] = ref[c]

    def clear(r, carry):
        for k in range(8):
            owner[r * 8 + k] = -1
        return carry

    lax.fori_loop(0, rows // 8, clear, 0)
    copy.wait()

    def fetch(row, s):
        return (pltpu.make_async_copy(out.at[:, row, :], base.at[s], row_sem),
                pltpu.make_async_copy(grow.at[:, row, :], gate.at[s], row_sem))

    def store(row, s):
        return pltpu.make_async_copy(base.at[s], out.at[:, row, :], out_sem)

    def claim(s, count):
        row = tags_s[s // CAP, s % CAP]
        at = jnp.maximum(row, 0)
        mine = owner[at]
        fresh = jnp.logical_and(row >= 0, mine < 0)
        leader = jnp.where(row < 0, slots, jnp.where(mine < 0, s, mine))
        lead[s] = leader
        final[leader] = s

        @pl.when(fresh)
        def _():
            owner[at] = s
            for c in fetch(at, s):
                c.start()

        return count + jnp.where(fresh, 1, 0)

    count = lax.fori_loop(0, slots, claim, 0)
    final[slots] = -1

    def product(t, carry):
        for n in range(CAP):
            c = jnp.maximum(tags_s[t, CAP + n], 0)
            at = pl.ds(pl.multiple_of(t * stride + n * members, 16), members)
            x = jnp.dot(landed[at, :], table[c, :depth, :], preferred_element_type=F32)
            scale = table[c, depth:, :].astype(F32)[:1]
            carried[t * CAP + n] = (x * scale).astype(BF16).astype(F32)
        return carry

    lax.fori_loop(0, bands, product, 0, unroll=8)

    def arrive(s, carry):
        for c in fetch(0, 0):
            c.wait()
        return carry

    lax.fori_loop(0, count, arrive, 0)

    def add(t, carry):
        for n in range(CAP):
            to = lead[t * CAP + n]
            base[to] = base[to] + carried[t * CAP + n] * gate[to]
        for n in range(CAP):
            to = lead[t * CAP + n]

            @pl.when(final[to] == t * CAP + n)
            def _():
                store(tags_s[t, n], to).start()

        return carry

    lax.fori_loop(0, bands, add, 0)

    def finish(s, carry):
        store(0, 0).wait()
        return carry

    lax.fori_loop(0, count, finish, 0)


def smem():
    return pl.BlockSpec(memory_space=pltpu.SMEM)


def vmem():
    return pl.BlockSpec(memory_space=pltpu.VMEM)


def anywhere():
    return pl.BlockSpec(memory_space=pl.ANY)


def hbm():
    return pl.BlockSpec(memory_space=pltpu.HBM)


def params(mib):
    return pltpu.CompilerParams(vmem_limit_bytes=int(mib * MIB))


def near_pairs(count):
    return [(i, i ^ 1) for i in range(count)]


def far_pairs(count):
    return [(i, j) for k in range(1, count - 1, 2) for i, j in ((k, k + 1), (k + 1, k))]


def local(
    density,
    habitat_class,
    suitability,
    dispersal_draw,
    threshold,
    hub_row,
    dest_tile,
    dest_row,
    county_id,
    jump_share,
    flow_tiles,
    flow_scale,
):
    members, rows, cols = density.shape
    bands, flows = lax.axis_size("tile"), lax.axis_size("flow")
    flow_scale = flow_scale.reshape(1, -1)
    density, dispersal_draw, habitat_class, flow_tiles, suitability, flow_scale, threshold = (
        pltpu.with_memory_space_constraint(x, pltpu.HBM)
        for x in (density, dispersal_draw, habitat_class, flow_tiles, suitability, flow_scale, threshold))
    t, f = lax.axis_index("tile"), lax.axis_index("flow")
    place = jnp.stack([t % 2, f % 2, t, f]).astype(jnp.int32)
    hubs, share = hub_row.reshape(-1), jump_share.reshape(-1)
    sds = jax.ShapeDtypeStruct
    per, depth = flow_tiles.shape[:2]
    message = sds((2 * members + TAIL, cols), BF16)
    pack = sds((2 * members, cols), F32)
    cols_a, cols_b, rows_a, rows_b, own, weight, tiles, turned = pl.pallas_call(
        edges_kernel,
        out_shape=(message, message, message, message, pack, sds((rows, cols), F32),
                   sds((per, depth + TAGS, cols), BF16), sds((rows, members, cols), F32)),
        in_specs=[smem()] + [hbm()] * 5,
        out_specs=(vmem(),) * 8,
        scratch_shapes=[
            pltpu.VMEM(pack.shape, F32),
            pltpu.VMEM(pack.shape, F32),
            pltpu.VMEM((rows, cols), jnp.int32),
            pltpu.SMEM(suitability.shape, F32),
            pltpu.VMEM((1, per), BF16),
            pltpu.SemaphoreType.DMA((rows // CHUNK,)),
            pltpu.SemaphoreType.DMA((4,)),
        ],
        compiler_params=params(24),
        name="edges",
    )(place, density, habitat_class, suitability, flow_tiles, flow_scale)

    got_a = lax.ppermute(cols_a, "flow", near_pairs(flows))
    got_b = lax.ppermute(cols_b, "flow", far_pairs(flows))
    rows_a, rows_b = pl.pallas_call(
        corners_kernel,
        out_shape=(message, message),
        in_specs=[smem()] + [vmem()] * 4,
        out_specs=(vmem(), vmem()),
        compiler_params=params(24),
        name="corners",
    )(place, rows_a, rows_b, got_a, got_b)
    rows_a, rows_b, dispersal_draw = lax.optimization_barrier((rows_a, rows_b, dispersal_draw))
    strip_a = lax.ppermute(rows_a, "tile", near_pairs(bands))
    strip_b = lax.ppermute(rows_b, "tile", far_pairs(bands))

    def swap(x, bit):
        return lax.ppermute(x, "flow", [(i, i ^ bit) for i in range(flows)])

    grow = pl.pallas_call(
        grow_kernel,
        out_shape=pltpu.HBM(density.shape, F32),
        in_specs=[hbm(), hbm()],
        out_specs=hbm(),
        scratch_shapes=[
            pltpu.VMEM(density.shape, BF16),
            pltpu.VMEM(density.shape, F32),
            pltpu.VMEM((rows, cols), F32),
            pltpu.SemaphoreType.DMA((GROW,)),
            pltpu.SemaphoreType.DMA,
            pltpu.SemaphoreType.DMA,
        ],
        compiler_params=params(24),
        name="grow",
    )(dispersal_draw, threshold)
    grow = pltpu.with_memory_space_constraint(grow, pltpu.HBM)

    blocks = [tiles] + [swap(tiles, d) for d in range(1, flows)]
    turned, grow = lax.optimization_barrier((turned, grow))

    stride = CAP * members + TAGS
    sent, near, halo1, beside, coef, strips = pl.pallas_call(
        hubs_kernel,
        out_shape=(sds((bands * stride, cols), BF16), pack, pack, sds((4 * members, cols), F32),
                   sds((rows + 16, cols), F32), sds((4, members, cols), F32)),
        in_specs=[smem()] * 6 + [vmem()] * 7,
        out_specs=(vmem(),) * 6,
        scratch_shapes=[pltpu.SMEM((bands,), jnp.int32)],
        compiler_params=params(24),
        name="hubs",
    )(place, hubs, dest_tile.reshape(-1), dest_row.reshape(-1), county_id.reshape(-1), share,
      turned, weight, own, got_a, got_b, strip_a, strip_b)

    landed = lax.all_to_all(sent, "tile", split_axis=0, concat_axis=0, tiled=True)
    kept = pl.pallas_call(
        bulk_kernel,
        out_shape=sds(density.shape, F32),
        in_specs=[smem(), smem(), hbm(), hbm()] + [vmem()] * 5,
        out_specs=hbm(),
        scratch_shapes=[
            pltpu.VMEM((rows + 4, members, cols), F32),
            pltpu.VMEM((rows + 2, members, cols), F32),
            pltpu.VMEM((rows, members, cols), F32),
            pltpu.SMEM((rows,), F32),
            pltpu.SemaphoreType.DMA((rows // STEP,)),
            pltpu.SemaphoreType.DMA((rows // STEP,)),
            pltpu.SemaphoreType.DMA,
        ],
        compiler_params=params(24),
        name="bulk",
    )(hubs, share, density, grow, coef, strips, near, halo1, beside)

    slots = bands * CAP
    out = pl.pallas_call(
        land_kernel,
        out_shape=sds(density.shape, F32),
        in_specs=[smem(), vmem(), hbm(), hbm()] + [vmem()] * flows,
        out_specs=hbm(),
        input_output_aliases={2: 0},
        scratch_shapes=[
            pltpu.VMEM((flows * per, depth + TAGS, cols), BF16),
            pltpu.VMEM((slots + 1, members, cols), F32),
            pltpu.VMEM((slots + 1, members, cols), F32),
            pltpu.VMEM((slots, members, cols), F32),
            pltpu.VMEM((bands, cols), jnp.int32),
            pltpu.SMEM((bands, cols), jnp.int32),
            pltpu.SMEM((rows,), jnp.int32),
            pltpu.SMEM((slots,), jnp.int32),
            pltpu.SMEM((slots + 1,), jnp.int32),
            pltpu.SemaphoreType.DMA,
            pltpu.SemaphoreType.DMA,
            pltpu.SemaphoreType.DMA,
        ],
        compiler_params=params(24),
        name="land",
    )(place, landed, kept, grow, *blocks)
    return out


def solution(mesh):
    in_specs = (
        P(None, "tile", "flow"),
        P("tile", "flow"),
        P(),
        P(None, "tile", "flow"),
        P("tile", "flow"),
        P("flow", "tile"),
        P("flow", "tile", None),
        P("flow", "tile"),
        P("flow", "tile"),
        P("flow", "tile"),
        P("flow", None, None),
        P("flow"),
    )
    out_specs = P(None, "tile", "flow")
    return jax.shard_map(local, mesh=mesh, in_specs=in_specs, out_specs=out_specs, check_vma=False)
```

```python
import jax
import jax.numpy as jnp
from jax import lax
from jax.experimental import pallas as pl
from jax.experimental.pallas import tpu as pltpu
from jax.sharding import PartitionSpec as P

CAP = 4
KAPPA = 0.24
SHARPNESS = 8.0
TAIL = 16
TAGS = 16
CHUNK = 16
UNROLL = 16
STEP = 16
GROW = 16
MIB = 1024 * 1024
F32 = jnp.float32
BF16 = jnp.bfloat16


def lanes(shape):
    return lax.broadcasted_iota(jnp.int32, shape, 1)


def sublanes(shape):
    return lax.broadcasted_iota(jnp.int32, shape, 0)


def edges_kernel(
    place, density, habitat, suit, tiles, scale,
    cols_a, cols_b, rows_a, rows_b, own, weight_out, tiles_out, turned,
    acc_e, acc_o, label_v, suit_v, scale_v, row_sems, sems,
):
    rows, members, cols = turned.shape
    half = rows // 2
    chunk = CHUNK
    t_even = place[0] == 0
    f_even = place[1] == 0
    depth = tiles.shape[1]
    small = [
        pltpu.make_async_copy(suit, suit_v, sems.at[0]),
        pltpu.make_async_copy(habitat, label_v, sems.at[1]),
        pltpu.make_async_copy(scale, scale_v, sems.at[2]),
        pltpu.make_async_copy(tiles, tiles_out.at[:, :depth, :], sems.at[3]),
    ]
    for copy in small:
        copy.start()

    def fetch(i, carry):
        for k in range(8):
            r = i * 8 + k
            pltpu.make_async_copy(density.at[:, r, :], turned.at[r], row_sems.at[i * 8 // chunk]).start()
        return carry

    lax.fori_loop(0, rows // 8, fetch, 0)
    for copy in small:
        copy.wait()

    shape = (rows, cols)
    label = label_v[...]
    weight = jnp.zeros(shape, F32)
    for c in range(suit_v.shape[0]):
        weight = jnp.where(label == c, suit_v[c], weight)
    weight_out[...] = weight
    pair_lane = lanes((half, cols)) // 2 == sublanes((half, cols))

    def spread(column):
        return jnp.sum(jnp.where(pair_lane, column, 0.0), axis=0, keepdims=True)

    row8 = sublanes((TAIL, cols))

    def split(value):
        high = value.astype(BF16).astype(F32)
        return high, value - high

    def side_weight(column):
        high0, low0 = split(spread(column[:half]))
        high1, low1 = split(spread(column[half:]))
        lows = jnp.where(row8 == 2, low0, low1)
        return jnp.where(row8 == 0, high0, jnp.where(row8 == 1, high1, lows))

    w_right = side_weight(weight[:, cols - 1:])
    w_left = side_weight(weight[:, :1])
    cols_a[2 * members:, :] = jnp.where(f_even, w_right, w_left).astype(BF16)
    cols_b[2 * members:, :] = jnp.where(f_even, w_left, w_right).astype(BF16)

    def rim_weight(row):
        high, low = split(row)
        return jnp.where(row8 == 0, high, low)

    w_top = rim_weight(weight[:1, :])
    w_bottom = rim_weight(weight[rows - 1:, :])
    rows_a[2 * members:, :] = jnp.where(t_even, w_bottom, w_top).astype(BF16)
    rows_b[2 * members:, :] = jnp.where(t_even, w_top, w_bottom).astype(BF16)
    for c in range(tiles.shape[0]):
        value = scale_v[:, c:c + 1].astype(F32)
        tiles_out[c, depth:, :] = jnp.broadcast_to(value, (TAGS, cols)).astype(BF16)

    quad = lanes((8, cols)) // 4

    def pack(i, carry):
        ready = turned.at[pl.ds(i * chunk, chunk)]
        pltpu.make_async_copy(ready, ready, row_sems.at[i]).wait()
        part = i // (half // chunk)
        first = (i - part * (half // chunk)) * (chunk // 2)
        for g in range(members // 8):
            to = pl.ds(pl.multiple_of(part * members + 8 * g, 8), 8)
            even, odd = acc_e[to, :], acc_o[to, :]
            for j in range(chunk // 2):
                r = i * chunk + 2 * j
                q = first + j
                shift = 4 * q + 2
                hit = quad == q
                even = jnp.where(hit, pltpu.roll(turned[r, 8 * g:8 * g + 8, :], shift, 1), even)
                odd = jnp.where(hit, pltpu.roll(turned[r + 1, 8 * g:8 * g + 8, :], shift, 1), odd)
            acc_e[to, :] = even
            acc_o[to, :] = odd
        return carry

    lax.fori_loop(0, rows // chunk, pack, 0)

    wide = (2 * members, cols)
    low = lanes(wide) % 4 < 2
    even, odd = acc_e[...], acc_o[...]
    right = jnp.where(low, even, pltpu.roll(odd, 2, 1))
    left = jnp.where(low, pltpu.roll(even, cols - 2, 1), odd)
    own[...] = jnp.where(lanes(wide) % 2 == 0, pltpu.roll(right, cols - 1, 1), pltpu.roll(left, 1, 1))
    cols_a[:2 * members, :] = jnp.where(f_even, right, left).astype(BF16)
    cols_b[:2 * members, :] = jnp.where(f_even, left, right).astype(BF16)
    for k in range(2):
        to = pl.ds(k * members, members)
        rows_a[to, :] = turned[jnp.where(t_even, rows - 2, 0) + k].astype(BF16)
        rows_b[to, :] = turned[jnp.where(t_even, 0, rows - 2) + k].astype(BF16)


def corners_kernel(place, rows_a, rows_b, got_a, got_b, out_a, out_b):
    cols = got_a.shape[1]
    members = (got_a.shape[0] - TAIL) // 2
    t_even = place[0] == 0
    f_even = place[1] == 0
    side = (members, cols)
    swap = (lanes(side) % 2 == 1) == f_even
    top = jnp.where(swap, got_b[:members, :].astype(F32), got_a[:members, :].astype(F32))
    low = slice(members, 2 * members)
    bottom = jnp.where(swap, got_b[low, :].astype(F32), got_a[low, :].astype(F32))

    def to_row(pair, first):
        east = jnp.where(lanes(side) == 2 * sublanes(side), pair[:, first:first + 1], 0.0)
        west = jnp.where(lanes(side) == 2 * sublanes(side) + 1, pair[:, first + 1:first + 2], 0.0)
        return jnp.sum(east + west, axis=0, keepdims=True)

    top_row = to_row(top, 0)
    bottom_row = to_row(bottom, cols - 2)
    last = 2 * members
    second = sublanes((TAIL, cols)) == 1
    for out, ref, first, other in ((out_a, rows_a, bottom_row, top_row), (out_b, rows_b, top_row, bottom_row)):
        out[:last, :] = ref[:last, :]
        corner = jnp.where(t_even, first, other)
        out[last:, :] = jnp.where(second, corner, ref[last:, :].astype(F32)).astype(BF16)


def hubs_kernel(
    place, hub_row, dest_tile, dest_row, county, share,
    turned, weight, own, cols_a, cols_b, rows_a, rows_b,
    sent, near, halo1, beside, coef, strips, counts,
):
    rows, members, cols = turned.shape
    bands = counts.shape[0]
    t_even = place[0] == 0
    f_even = place[1] == 0
    side = (members, cols)
    lane = lanes(side)
    even_lane = lane % 2 == 0

    tail_a = rows_a[2 * members:, :].astype(F32)
    tail_b = rows_b[2 * members:, :].astype(F32)
    tail_n = jnp.where(t_even, tail_b, tail_a)
    tail_s = jnp.where(t_even, tail_a, tail_b)
    for k in range(2):
        at = slice(k * members, (k + 1) * members)
        row_a, row_b = rows_a[at, :].astype(F32), rows_b[at, :].astype(F32)
        strips[k] = jnp.where(t_even, row_b, row_a)
        strips[2 + k] = jnp.where(t_even, row_a, row_b)
    coef[0:8, :] = jnp.broadcast_to(KAPPA * (tail_n[0:1] + tail_n[2:3]), (8, cols))
    coef[8:8 + rows, :] = KAPPA * weight[...]
    coef[8 + rows:, :] = jnp.broadcast_to(KAPPA * (tail_s[0:1] + tail_s[2:3]), (8, cols))

    def corner(tail):
        row = jnp.broadcast_to(tail[1:2, :], side)
        east = jnp.sum(jnp.where(lane == 2 * sublanes(side), row, 0.0), axis=1, keepdims=True)
        west = jnp.sum(jnp.where(lane == 2 * sublanes(side) + 1, row, 0.0), axis=1, keepdims=True)
        return east, west

    east_n, west_n = corner(tail_n)
    east_s, west_s = corner(tail_s)
    halves = []
    for k in range(2):
        at = slice(k * members, (k + 1) * members)
        a, b = cols_a[at, :].astype(F32), cols_b[at, :].astype(F32)
        from_e = jnp.where(f_even, a, b)
        from_w = jnp.where(f_even, b, a)
        close = jnp.where(even_lane, from_e, from_w)
        far = jnp.where(even_lane, pltpu.roll(from_e, cols - 1, 1), pltpu.roll(from_w, 1, 1))
        near[at, :] = close
        halves.append((close, far))
    wa, wb = cols_a[2 * members:, :].astype(F32), cols_b[2 * members:, :].astype(F32)
    w_e = jnp.where(f_even, wa, wb)
    w_w = jnp.where(f_even, wb, wa)
    w_packed = jnp.where(lanes((TAIL, cols)) % 2 == 0, w_e, w_w)
    near0, near1 = halves[0][0], halves[1][0]
    down0, down1 = pltpu.roll(near0, 2, 1), pltpu.roll(near1, 2, 1)
    up0, up1 = pltpu.roll(near0, cols - 2, 1), pltpu.roll(near1, cols - 2, 1)
    n0 = jnp.where(lane < 2, jnp.where(even_lane, east_n, west_n), down0)
    n1 = jnp.where(lane < 2, down0, down1)
    s0 = jnp.where(lane >= cols - 2, up1, up0)
    s1 = jnp.where(lane >= cols - 2, jnp.where(even_lane, east_s, west_s), up1)
    for k, (n, s) in enumerate(((n0, s0), (n1, s1))):
        at = slice(k * members, (k + 1) * members)
        close, far = halves[k]
        around = (n + s) + (far + own[at, :])
        w = KAPPA * (w_packed[k:k + 1, :] + w_packed[k + 2:k + 3, :])
        halo1[at, :] = close + w * (around - 4.0 * close)
    beside[0:members, :] = jnp.where(lane == 0, west_n, east_n)
    beside[members:2 * members, :] = pltpu.roll(near1, cols - 1, 1)
    beside[2 * members:3 * members, :] = pltpu.roll(near0, 1, 1)
    beside[3 * members:, :] = jnp.where(lane == 0, west_s, east_s)

    stride = CAP * members + TAGS
    tag_lane = lanes((TAGS, cols))
    for t in range(bands):
        counts[t] = 0
        sent[t * stride + CAP * members:(t + 1) * stride, :] = jnp.full((TAGS, cols), -1.0, BF16)
    half = rows // 2
    first, last = lane == 0, lane == cols - 1

    def field_row(r):
        inside = turned[jnp.clip(r, 0, rows - 1)]
        outside = strips[jnp.clip(jnp.where(r < 0, r + 2, r - rows + 2), 0, 3)]
        return jnp.where(jnp.logical_and(r >= 0, r < rows), inside, outside)

    def halo_row(ref, r):
        k = jnp.where(r >= half, 1, 0)
        at = pl.ds(pl.multiple_of(k * members, 8), members)
        return pltpu.roll(ref[at, :], cols - 1 - 2 * (r - k * half), 1)

    def side_row(r):
        edge = jnp.where(r < 0, beside[0:members, :], beside[3 * members:, :])
        inside = halo_row(near, jnp.clip(r, 0, rows - 1))
        return jnp.where(jnp.logical_and(r >= 0, r < rows), inside, edge)

    edge = jnp.logical_or(first, last)
    band = (cols, cols)
    mask = (jnp.abs(lanes(band) - sublanes(band)) == 1).astype(BF16)
    mask = jnp.concatenate([mask, mask], axis=0)

    def lateral(rows_in):
        flat = jnp.concatenate(rows_in, axis=0)
        high = flat.astype(BF16)
        low = (flat - high.astype(F32)).astype(BF16)
        both = jnp.dot(jnp.concatenate([high, low], axis=1), mask, preferred_element_type=F32)
        return [both[k * members:(k + 1) * members] for k in range(len(rows_in))]

    def relax(c, n, s, h, w, across):
        return c + w * ((n + s) + (across + jnp.where(edge, h, 0.0)) - 4.0 * c)

    def coef_row(r):
        at = jnp.where(r < 0, 0, r + 8)
        return coef[pl.ds(at, 1), :]

    def several(i, carry):
        chosen = [i * UNROLL + k for k in range(UNROLL)]
        spot = [hub_row[h] for h in chosen]
        u = [[field_row(r + k) for k in range(-2, 3)] for r in spot]
        across = lateral([u[k][c] for k in range(UNROLL) for c in (1, 2, 3)])
        v = []
        for k, r in enumerate(spot):
            v.append([
                relax(u[k][c + 2], u[k][c + 1], u[k][c + 3], side_row(r + c), coef_row(r + c), across[3 * k + c + 1])
                for c in range(-1, 2)])
        across = lateral([x[1] for x in v])
        for k, (h, r) in enumerate(zip(chosen, spot)):
            moved = share[h] * relax(v[k][1], v[k][0], v[k][2], halo_row(halo1, r), coef_row(r), across[k])
            to = dest_tile[h]
            n = counts[to]
            counts[to] = n + 1
            base = pl.multiple_of(to * stride, 16)
            sent[pl.ds(pl.multiple_of(base + n * members, 16), members), :] = moved.astype(BF16)
            at = pl.ds(pl.multiple_of(base + CAP * members, 16), TAGS)
            tags = sent[at, :].astype(F32)
            tags = jnp.where(tag_lane == n, dest_row[h].astype(F32), tags)
            tags = jnp.where(tag_lane == CAP + n, county[h].astype(F32), tags)
            sent[at, :] = tags.astype(BF16)
        return carry

    lax.fori_loop(0, hub_row.shape[0] // UNROLL, several, 0)


def grow_kernel(draw, threshold, grow, draw_v, grow_v, limit_v, in_sem, out_sem, sem):
    chunk = draw.shape[0] // GROW
    limit = pltpu.make_async_copy(threshold, limit_v, sem)
    limit.start()

    def fetch(i, carry):
        at = pl.ds(i * chunk, chunk)
        pltpu.make_async_copy(draw.at[at], draw_v.at[at], in_sem.at[i]).start()
        return carry

    lax.fori_loop(0, GROW, fetch, 0)
    limit.wait()

    def work(i, carry):
        at = pl.ds(i * chunk, chunk)
        pltpu.make_async_copy(draw.at[at], draw_v.at[at], in_sem.at[i]).wait()
        for k in range(chunk):
            x = 0.5 * SHARPNESS * (draw_v[i * chunk + k].astype(F32) - limit_v[...])
            grow_v[i * chunk + k] = 0.5 * jnp.tanh(x) + 0.5
        pltpu.make_async_copy(grow_v.at[at], grow.at[at], out_sem).start()
        return carry

    lax.fori_loop(0, GROW, work, 0)
    pltpu.make_async_copy(grow_v, grow, out_sem).wait()


def bulk_kernel(
    hub_row, share, density, grow, coef, strips, near, halo1, beside,
    kept, field, inner, gate, factor, in_sem, gate_sem, out_sem,
):
    members, rows, cols = density.shape
    half = rows // 2
    step = STEP
    blocks = rows // step

    def fetch(i, carry):
        for k in range(step):
            r = i * step + k
            pltpu.make_async_copy(density.at[:, r, :], field.at[r + 2], in_sem.at[i]).start()
        return carry

    def fetch_gate(i, carry):
        for k in range(step):
            r = i * step + k
            pltpu.make_async_copy(grow.at[:, r, :], gate.at[r], gate_sem.at[i]).start()
        return carry

    lax.fori_loop(0, blocks, fetch, 0)
    lax.fori_loop(0, blocks, fetch_gate, 0)
    for k in range(2):
        field[k] = strips[k]
        field[rows + 2 + k] = strips[2 + k]

    def clear(i, carry):
        for k in range(8):
            factor[i * 8 + k] = 1.0
        return carry

    lax.fori_loop(0, rows // 8, clear, 0)

    def leave(h, carry):
        r = hub_row[h]
        factor[r] = factor[r] - share[h]
        return carry

    lax.fori_loop(0, hub_row.shape[0], leave, 0)

    side = (members, cols)
    lane = lanes(side)
    first, last = lane == 0, lane == cols - 1

    edge = jnp.logical_or(first, last)
    band = (cols, cols)
    beside_mask = (jnp.abs(lanes(band) - sublanes(band)) == 1).astype(BF16)
    beside_mask = jnp.concatenate([beside_mask, beside_mask], axis=0)

    def lateral(c):
        flat = c.reshape(-1, cols)
        high = flat.astype(BF16)
        low = (flat - high.astype(F32)).astype(BF16)
        parts = jnp.concatenate([high, low], axis=1)
        return jnp.dot(parts, beside_mask, preferred_element_type=F32).reshape(c.shape)

    def relax(c, n, s, h, w, across):
        return c + w * ((n + s) + (across + jnp.where(edge, h, 0.0)) - 4.0 * c)

    def halo_row(ref, part, r):
        at = pl.ds(pl.multiple_of(part * members, 8), members)
        return pltpu.roll(ref[at, :], cols - 1 - 2 * (r - part * half), 1)

    def landed(i):
        ready = field.at[pl.ds(i * step + 2, step)]
        pltpu.make_async_copy(ready, ready, in_sem.at[i]).wait()

    landed(0)
    inner[0] = relax(field[1], field[0], field[2], beside[:members, :], coef[0:1, :], lateral(field[1]))

    def early(i, carry):
        @pl.when(i < blocks - 1)
        def _():
            landed(i + 1)

        part = i // (half // step)
        across = lateral(field[pl.ds(i * step + 2, step)])
        for k in range(step):
            r = i * step + k
            inner[r + 1] = relax(
                field[r + 2], field[r + 1], field[r + 3], halo_row(near, part, r), coef[pl.ds(r + 8, 1), :], across[k])
        return carry

    lax.fori_loop(0, blocks, early, 0)
    inner[rows + 1] = relax(
        field[rows + 2], field[rows + 1], field[rows + 3], beside[3 * members:, :], coef[rows + 8:rows + 9, :],
        lateral(field[rows + 2]))

    def late(i, carry):
        ready = gate.at[pl.ds(i * step, step)]
        pltpu.make_async_copy(ready, ready, gate_sem.at[i]).wait()
        part = i // (half // step)
        across = lateral(inner[pl.ds(i * step + 1, step)])
        for k in range(step):
            r = i * step + k
            d = relax(
                inner[r + 1], inner[r], inner[r + 2], halo_row(halo1, part, r), coef[pl.ds(r + 8, 1), :], across[k])
            gate[r] = d * factor[r] * gate[r]
        for k in range(step):
            r = i * step + k
            pltpu.make_async_copy(gate.at[r], kept.at[:, r, :], out_sem).start()
        return carry

    lax.fori_loop(0, blocks, late, 0)
    pltpu.make_async_copy(gate, gate, out_sem).wait()


def land_kernel(place, landed, kept, grow, *rest):
    blocks, rest = rest[:-13], rest[-13:]
    out, table, base, gate, carried, tags_v, tags_s, owner, lead, final, tag_sem, row_sem, out_sem = rest
    per = blocks[0].shape[0]
    bands, cols = tags_v.shape
    stride = landed.shape[0] // bands
    members, rows, _ = kept.shape
    depth = table.shape[1] - TAGS
    slots = bands * CAP
    for t in range(bands):
        tags = landed[t * stride + CAP * members:(t + 1) * stride, :].astype(F32)
        tags_v[t:t + 1, :] = tags[:1].astype(jnp.int32)
    copy = pltpu.make_async_copy(tags_v, tags_s, tag_sem)
    copy.start()
    for d, ref in enumerate(blocks):
        at = jnp.bitwise_xor(place[3], d) * per
        for c in range(per):
            table[at + c] = ref[c]

    def clear(r, carry):
        for k in range(8):
            owner[r * 8 + k] = -1
        return carry

    lax.fori_loop(0, rows // 8, clear, 0)
    copy.wait()

    def fetch(row, s):
        return (pltpu.make_async_copy(out.at[:, row, :], base.at[s], row_sem),
                pltpu.make_async_copy(grow.at[:, row, :], gate.at[s], row_sem))

    def store(row, s):
        return pltpu.make_async_copy(base.at[s], out.at[:, row, :], out_sem)

    def claim(s, count):
        row = tags_s[s // CAP, s % CAP]
        at = jnp.maximum(row, 0)
        mine = owner[at]
        fresh = jnp.logical_and(row >= 0, mine < 0)
        leader = jnp.where(row < 0, slots, jnp.where(mine < 0, s, mine))
        lead[s] = leader
        final[leader] = s

        @pl.when(fresh)
        def _():
            owner[at] = s
            for c in fetch(at, s):
                c.start()

        return count + jnp.where(fresh, 1, 0)

    count = lax.fori_loop(0, slots, claim, 0)
    final[slots] = -1

    def product(t, carry):
        for n in range(CAP):
            c = jnp.maximum(tags_s[t, CAP + n], 0)
            at = pl.ds(pl.multiple_of(t * stride + n * members, 16), members)
            x = jnp.dot(landed[at, :], table[c, :depth, :], preferred_element_type=F32)
            scale = table[c, depth:, :].astype(F32)[:1]
            carried[t * CAP + n] = (x * scale).astype(BF16).astype(F32)
        return carry

    lax.fori_loop(0, bands, product, 0, unroll=8)

    def arrive(s, carry):
        for c in fetch(0, 0):
            c.wait()
        return carry

    lax.fori_loop(0, count, arrive, 0)

    def add(t, carry):
        for n in range(CAP):
            to = lead[t * CAP + n]
            base[to] = base[to] + carried[t * CAP + n] * gate[to]
        for n in range(CAP):
            to = lead[t * CAP + n]

            @pl.when(final[to] == t * CAP + n)
            def _():
                store(tags_s[t, n], to).start()

        return carry

    lax.fori_loop(0, bands, add, 0)

    def finish(s, carry):
        store(0, 0).wait()
        return carry

    lax.fori_loop(0, count, finish, 0)


def smem():
    return pl.BlockSpec(memory_space=pltpu.SMEM)


def vmem():
    return pl.BlockSpec(memory_space=pltpu.VMEM)


def anywhere():
    return pl.BlockSpec(memory_space=pl.ANY)


def hbm():
    return pl.BlockSpec(memory_space=pltpu.HBM)


def params(mib):
    return pltpu.CompilerParams(vmem_limit_bytes=int(mib * MIB))


def near_pairs(count):
    return [(i, i ^ 1) for i in range(count)]


def far_pairs(count):
    return [(i, j) for k in range(1, count - 1, 2) for i, j in ((k, k + 1), (k + 1, k))]


def local(
    density,
    habitat_class,
    suitability,
    dispersal_draw,
    threshold,
    hub_row,
    dest_tile,
    dest_row,
    county_id,
    jump_share,
    flow_tiles,
    flow_scale,
):
    members, rows, cols = density.shape
    bands, flows = lax.axis_size("tile"), lax.axis_size("flow")
    flow_scale = flow_scale.reshape(1, -1)
    density, dispersal_draw, habitat_class, flow_tiles, suitability, flow_scale, threshold = (
        pltpu.with_memory_space_constraint(x, pltpu.HBM)
        for x in (density, dispersal_draw, habitat_class, flow_tiles, suitability, flow_scale, threshold))
    t, f = lax.axis_index("tile"), lax.axis_index("flow")
    place = jnp.stack([t % 2, f % 2, t, f]).astype(jnp.int32)
    hubs, share = hub_row.reshape(-1), jump_share.reshape(-1)
    sds = jax.ShapeDtypeStruct
    per, depth = flow_tiles.shape[:2]
    message = sds((2 * members + TAIL, cols), BF16)
    pack = sds((2 * members, cols), F32)
    cols_a, cols_b, rows_a, rows_b, own, weight, tiles, turned = pl.pallas_call(
        edges_kernel,
        out_shape=(message, message, message, message, pack, sds((rows, cols), F32),
                   sds((per, depth + TAGS, cols), BF16), sds((rows, members, cols), F32)),
        in_specs=[smem()] + [hbm()] * 5,
        out_specs=(vmem(),) * 8,
        scratch_shapes=[
            pltpu.VMEM(pack.shape, F32),
            pltpu.VMEM(pack.shape, F32),
            pltpu.VMEM((rows, cols), jnp.int32),
            pltpu.SMEM(suitability.shape, F32),
            pltpu.VMEM((1, per), BF16),
            pltpu.SemaphoreType.DMA((rows // CHUNK,)),
            pltpu.SemaphoreType.DMA((4,)),
        ],
        compiler_params=params(24),
        name="edges",
    )(place, density, habitat_class, suitability, flow_tiles, flow_scale)

    got_a = lax.ppermute(cols_a, "flow", near_pairs(flows))
    got_b = lax.ppermute(cols_b, "flow", far_pairs(flows))
    rows_a, rows_b = pl.pallas_call(
        corners_kernel,
        out_shape=(message, message),
        in_specs=[smem()] + [vmem()] * 4,
        out_specs=(vmem(), vmem()),
        compiler_params=params(24),
        name="corners",
    )(place, rows_a, rows_b, got_a, got_b)
    rows_a, rows_b, dispersal_draw = lax.optimization_barrier((rows_a, rows_b, dispersal_draw))
    strip_a = lax.ppermute(rows_a, "tile", near_pairs(bands))
    strip_b = lax.ppermute(rows_b, "tile", far_pairs(bands))

    def swap(x, bit):
        return lax.ppermute(x, "flow", [(i, i ^ bit) for i in range(flows)])

    grow = pl.pallas_call(
        grow_kernel,
        out_shape=pltpu.HBM(density.shape, F32),
        in_specs=[hbm(), hbm()],
        out_specs=hbm(),
        scratch_shapes=[
            pltpu.VMEM(density.shape, BF16),
            pltpu.VMEM(density.shape, F32),
            pltpu.VMEM((rows, cols), F32),
            pltpu.SemaphoreType.DMA((GROW,)),
            pltpu.SemaphoreType.DMA,
            pltpu.SemaphoreType.DMA,
        ],
        compiler_params=params(24),
        name="grow",
    )(dispersal_draw, threshold)
    grow = pltpu.with_memory_space_constraint(grow, pltpu.HBM)

    blocks = [tiles] + [swap(tiles, d) for d in range(1, flows)]
    turned, grow = lax.optimization_barrier((turned, grow))

    stride = CAP * members + TAGS
    sent, near, halo1, beside, coef, strips = pl.pallas_call(
        hubs_kernel,
        out_shape=(sds((bands * stride, cols), BF16), pack, pack, sds((4 * members, cols), F32),
                   sds((rows + 16, cols), F32), sds((4, members, cols), F32)),
        in_specs=[smem()] * 6 + [vmem()] * 7,
        out_specs=(vmem(),) * 6,
        scratch_shapes=[pltpu.SMEM((bands,), jnp.int32)],
        compiler_params=params(24),
        name="hubs",
    )(place, hubs, dest_tile.reshape(-1), dest_row.reshape(-1), county_id.reshape(-1), share,
      turned, weight, own, got_a, got_b, strip_a, strip_b)

    landed = lax.all_to_all(sent, "tile", split_axis=0, concat_axis=0, tiled=True)
    kept = pl.pallas_call(
        bulk_kernel,
        out_shape=sds(density.shape, F32),
        in_specs=[smem(), smem(), hbm(), hbm()] + [vmem()] * 5,
        out_specs=hbm(),
        scratch_shapes=[
            pltpu.VMEM((rows + 4, members, cols), F32),
            pltpu.VMEM((rows + 2, members, cols), F32),
            pltpu.VMEM((rows, members, cols), F32),
            pltpu.SMEM((rows,), F32),
            pltpu.SemaphoreType.DMA((rows // STEP,)),
            pltpu.SemaphoreType.DMA((rows // STEP,)),
            pltpu.SemaphoreType.DMA,
        ],
        compiler_params=params(24),
        name="bulk",
    )(hubs, share, density, grow, coef, strips, near, halo1, beside)

    slots = bands * CAP
    out = pl.pallas_call(
        land_kernel,
        out_shape=sds(density.shape, F32),
        in_specs=[smem(), vmem(), hbm(), hbm()] + [vmem()] * flows,
        out_specs=hbm(),
        input_output_aliases={2: 0},
        scratch_shapes=[
            pltpu.VMEM((flows * per, depth + TAGS, cols), BF16),
            pltpu.VMEM((slots + 1, members, cols), F32),
            pltpu.VMEM((slots + 1, members, cols), F32),
            pltpu.VMEM((slots, members, cols), F32),
            pltpu.VMEM((bands, cols), jnp.int32),
            pltpu.SMEM((bands, cols), jnp.int32),
            pltpu.SMEM((rows,), jnp.int32),
            pltpu.SMEM((slots,), jnp.int32),
            pltpu.SMEM((slots + 1,), jnp.int32),
            pltpu.SemaphoreType.DMA,
            pltpu.SemaphoreType.DMA,
            pltpu.SemaphoreType.DMA,
        ],
        compiler_params=params(24),
        name="land",
    )(place, landed, kept, grow, *blocks)
    return out


def solution(mesh):
    in_specs = (
        P(None, "tile", "flow"),
        P("tile", "flow"),
        P(),
        P(None, "tile", "flow"),
        P("tile", "flow"),
        P("flow", "tile"),
        P("flow", "tile", None),
        P("flow", "tile"),
        P("flow", "tile"),
        P("flow", "tile"),
        P("flow", None, None),
        P("flow"),
    )
    out_specs = P(None, "tile", "flow")
    return jax.shard_map(local, mesh=mesh, in_specs=in_specs, out_specs=out_specs, check_vma=False)
```

```python
import jax
import jax.numpy as jnp
from jax import lax
from jax.experimental import pallas as pl
from jax.experimental.pallas import tpu as pltpu
from jax.sharding import PartitionSpec as P

CAP = 4
KAPPA = 0.24
SHARPNESS = 8.0
TAIL = 16
TAGS = 16
CHUNK = 16
UNROLL = 16
STEP = 16
GROW = 8
MIB = 1024 * 1024
F32 = jnp.float32
BF16 = jnp.bfloat16


def lanes(shape):
    return lax.broadcasted_iota(jnp.int32, shape, 1)


def sublanes(shape):
    return lax.broadcasted_iota(jnp.int32, shape, 0)


def edges_kernel(
    place, density, habitat, suit, tiles, scale,
    cols_a, cols_b, rows_a, rows_b, own, weight_out, tiles_out, turned,
    acc_e, acc_o, label_v, suit_v, scale_v, row_sems, sems,
):
    rows, members, cols = turned.shape
    half = rows // 2
    chunk = CHUNK
    t_even = place[0] == 0
    f_even = place[1] == 0
    depth = tiles.shape[1]
    small = [
        pltpu.make_async_copy(suit, suit_v, sems.at[0]),
        pltpu.make_async_copy(habitat, label_v, sems.at[1]),
        pltpu.make_async_copy(scale, scale_v, sems.at[2]),
        pltpu.make_async_copy(tiles, tiles_out.at[:, :depth, :], sems.at[3]),
    ]
    for copy in small:
        copy.start()

    def fetch(i, carry):
        for k in range(8):
            r = i * 8 + k
            pltpu.make_async_copy(density.at[:, r, :], turned.at[r], row_sems.at[i * 8 // chunk]).start()
        return carry

    lax.fori_loop(0, rows // 8, fetch, 0)
    for copy in small:
        copy.wait()

    shape = (rows, cols)
    label = label_v[...]
    weight = jnp.zeros(shape, F32)
    for c in range(suit_v.shape[0]):
        weight = jnp.where(label == c, suit_v[c], weight)
    weight_out[...] = weight
    pair_lane = lanes((half, cols)) // 2 == sublanes((half, cols))

    def spread(column):
        return jnp.sum(jnp.where(pair_lane, column, 0.0), axis=0, keepdims=True)

    row8 = sublanes((TAIL, cols))

    def split(value):
        high = value.astype(BF16).astype(F32)
        return high, value - high

    def side_weight(column):
        high0, low0 = split(spread(column[:half]))
        high1, low1 = split(spread(column[half:]))
        lows = jnp.where(row8 == 2, low0, low1)
        return jnp.where(row8 == 0, high0, jnp.where(row8 == 1, high1, lows))

    w_right = side_weight(weight[:, cols - 1:])
    w_left = side_weight(weight[:, :1])
    cols_a[2 * members:, :] = jnp.where(f_even, w_right, w_left).astype(BF16)
    cols_b[2 * members:, :] = jnp.where(f_even, w_left, w_right).astype(BF16)

    def rim_weight(row):
        high, low = split(row)
        return jnp.where(row8 == 0, high, low)

    w_top = rim_weight(weight[:1, :])
    w_bottom = rim_weight(weight[rows - 1:, :])
    rows_a[2 * members:, :] = jnp.where(t_even, w_bottom, w_top).astype(BF16)
    rows_b[2 * members:, :] = jnp.where(t_even, w_top, w_bottom).astype(BF16)
    for c in range(tiles.shape[0]):
        value = scale_v[:, c:c + 1].astype(F32)
        tiles_out[c, depth:, :] = jnp.broadcast_to(value, (TAGS, cols)).astype(BF16)

    quad = lanes((8, cols)) // 4

    def pack(i, carry):
        ready = turned.at[pl.ds(i * chunk, chunk)]
        pltpu.make_async_copy(ready, ready, row_sems.at[i]).wait()
        part = i // (half // chunk)
        first = (i - part * (half // chunk)) * (chunk // 2)
        for g in range(members // 8):
            to = pl.ds(pl.multiple_of(part * members + 8 * g, 8), 8)
            even, odd = acc_e[to, :], acc_o[to, :]
            for j in range(chunk // 2):
                r = i * chunk + 2 * j
                q = first + j
                shift = 4 * q + 2
                hit = quad == q
                even = jnp.where(hit, pltpu.roll(turned[r, 8 * g:8 * g + 8, :], shift, 1), even)
                odd = jnp.where(hit, pltpu.roll(turned[r + 1, 8 * g:8 * g + 8, :], shift, 1), odd)
            acc_e[to, :] = even
            acc_o[to, :] = odd
        return carry

    lax.fori_loop(0, rows // chunk, pack, 0)

    wide = (2 * members, cols)
    low = lanes(wide) % 4 < 2
    even, odd = acc_e[...], acc_o[...]
    right = jnp.where(low, even, pltpu.roll(odd, 2, 1))
    left = jnp.where(low, pltpu.roll(even, cols - 2, 1), odd)
    own[...] = jnp.where(lanes(wide) % 2 == 0, pltpu.roll(right, cols - 1, 1), pltpu.roll(left, 1, 1))
    cols_a[:2 * members, :] = jnp.where(f_even, right, left).astype(BF16)
    cols_b[:2 * members, :] = jnp.where(f_even, left, right).astype(BF16)
    for k in range(2):
        to = pl.ds(k * members, members)
        rows_a[to, :] = turned[jnp.where(t_even, rows - 2, 0) + k].astype(BF16)
        rows_b[to, :] = turned[jnp.where(t_even, 0, rows - 2) + k].astype(BF16)


def corners_kernel(place, rows_a, rows_b, got_a, got_b, out_a, out_b):
    cols = got_a.shape[1]
    members = (got_a.shape[0] - TAIL) // 2
    t_even = place[0] == 0
    f_even = place[1] == 0
    side = (members, cols)
    swap = (lanes(side) % 2 == 1) == f_even
    top = jnp.where(swap, got_b[:members, :].astype(F32), got_a[:members, :].astype(F32))
    low = slice(members, 2 * members)
    bottom = jnp.where(swap, got_b[low, :].astype(F32), got_a[low, :].astype(F32))

    def to_row(pair, first):
        east = jnp.where(lanes(side) == 2 * sublanes(side), pair[:, first:first + 1], 0.0)
        west = jnp.where(lanes(side) == 2 * sublanes(side) + 1, pair[:, first + 1:first + 2], 0.0)
        return jnp.sum(east + west, axis=0, keepdims=True)

    top_row = to_row(top, 0)
    bottom_row = to_row(bottom, cols - 2)
    last = 2 * members
    second = sublanes((TAIL, cols)) == 1
    for out, ref, first, other in ((out_a, rows_a, bottom_row, top_row), (out_b, rows_b, top_row, bottom_row)):
        out[:last, :] = ref[:last, :]
        corner = jnp.where(t_even, first, other)
        out[last:, :] = jnp.where(second, corner, ref[last:, :].astype(F32)).astype(BF16)


def hubs_kernel(
    place, hub_row, dest_tile, dest_row, county, share,
    turned, weight, own, cols_a, cols_b, rows_a, rows_b,
    sent, near, halo1, beside, coef, strips, counts,
):
    rows, members, cols = turned.shape
    bands = counts.shape[0]
    t_even = place[0] == 0
    f_even = place[1] == 0
    side = (members, cols)
    lane = lanes(side)
    even_lane = lane % 2 == 0

    tail_a = rows_a[2 * members:, :].astype(F32)
    tail_b = rows_b[2 * members:, :].astype(F32)
    tail_n = jnp.where(t_even, tail_b, tail_a)
    tail_s = jnp.where(t_even, tail_a, tail_b)
    for k in range(2):
        at = slice(k * members, (k + 1) * members)
        row_a, row_b = rows_a[at, :].astype(F32), rows_b[at, :].astype(F32)
        strips[k] = jnp.where(t_even, row_b, row_a)
        strips[2 + k] = jnp.where(t_even, row_a, row_b)
    coef[0:8, :] = jnp.broadcast_to(KAPPA * (tail_n[0:1] + tail_n[2:3]), (8, cols))
    coef[8:8 + rows, :] = KAPPA * weight[...]
    coef[8 + rows:, :] = jnp.broadcast_to(KAPPA * (tail_s[0:1] + tail_s[2:3]), (8, cols))

    def corner(tail):
        row = jnp.broadcast_to(tail[1:2, :], side)
        east = jnp.sum(jnp.where(lane == 2 * sublanes(side), row, 0.0), axis=1, keepdims=True)
        west = jnp.sum(jnp.where(lane == 2 * sublanes(side) + 1, row, 0.0), axis=1, keepdims=True)
        return east, west

    east_n, west_n = corner(tail_n)
    east_s, west_s = corner(tail_s)
    halves = []
    for k in range(2):
        at = slice(k * members, (k + 1) * members)
        a, b = cols_a[at, :].astype(F32), cols_b[at, :].astype(F32)
        from_e = jnp.where(f_even, a, b)
        from_w = jnp.where(f_even, b, a)
        close = jnp.where(even_lane, from_e, from_w)
        far = jnp.where(even_lane, pltpu.roll(from_e, cols - 1, 1), pltpu.roll(from_w, 1, 1))
        near[at, :] = close
        halves.append((close, far))
    wa, wb = cols_a[2 * members:, :].astype(F32), cols_b[2 * members:, :].astype(F32)
    w_e = jnp.where(f_even, wa, wb)
    w_w = jnp.where(f_even, wb, wa)
    w_packed = jnp.where(lanes((TAIL, cols)) % 2 == 0, w_e, w_w)
    near0, near1 = halves[0][0], halves[1][0]
    down0, down1 = pltpu.roll(near0, 2, 1), pltpu.roll(near1, 2, 1)
    up0, up1 = pltpu.roll(near0, cols - 2, 1), pltpu.roll(near1, cols - 2, 1)
    n0 = jnp.where(lane < 2, jnp.where(even_lane, east_n, west_n), down0)
    n1 = jnp.where(lane < 2, down0, down1)
    s0 = jnp.where(lane >= cols - 2, up1, up0)
    s1 = jnp.where(lane >= cols - 2, jnp.where(even_lane, east_s, west_s), up1)
    for k, (n, s) in enumerate(((n0, s0), (n1, s1))):
        at = slice(k * members, (k + 1) * members)
        close, far = halves[k]
        around = (n + s) + (far + own[at, :])
        w = KAPPA * (w_packed[k:k + 1, :] + w_packed[k + 2:k + 3, :])
        halo1[at, :] = close + w * (around - 4.0 * close)
    beside[0:members, :] = jnp.where(lane == 0, west_n, east_n)
    beside[members:2 * members, :] = pltpu.roll(near1, cols - 1, 1)
    beside[2 * members:3 * members, :] = pltpu.roll(near0, 1, 1)
    beside[3 * members:, :] = jnp.where(lane == 0, west_s, east_s)

    stride = CAP * members + TAGS
    tag_lane = lanes((TAGS, cols))
    for t in range(bands):
        counts[t] = 0
        sent[t * stride + CAP * members:(t + 1) * stride, :] = jnp.full((TAGS, cols), -1.0, BF16)
    half = rows // 2
    first, last = lane == 0, lane == cols - 1

    def field_row(r):
        inside = turned[jnp.clip(r, 0, rows - 1)]
        outside = strips[jnp.clip(jnp.where(r < 0, r + 2, r - rows + 2), 0, 3)]
        return jnp.where(jnp.logical_and(r >= 0, r < rows), inside, outside)

    def halo_row(ref, r):
        k = jnp.where(r >= half, 1, 0)
        at = pl.ds(pl.multiple_of(k * members, 8), members)
        return pltpu.roll(ref[at, :], cols - 1 - 2 * (r - k * half), 1)

    def side_row(r):
        edge = jnp.where(r < 0, beside[0:members, :], beside[3 * members:, :])
        inside = halo_row(near, jnp.clip(r, 0, rows - 1))
        return jnp.where(jnp.logical_and(r >= 0, r < rows), inside, edge)

    edge = jnp.logical_or(first, last)
    band = (cols, cols)
    mask = (jnp.abs(lanes(band) - sublanes(band)) == 1).astype(BF16)
    mask = jnp.concatenate([mask, mask], axis=0)

    def lateral(rows_in):
        flat = jnp.concatenate(rows_in, axis=0)
        high = flat.astype(BF16)
        low = (flat - high.astype(F32)).astype(BF16)
        both = jnp.dot(jnp.concatenate([high, low], axis=1), mask, preferred_element_type=F32)
        return [both[k * members:(k + 1) * members] for k in range(len(rows_in))]

    def relax(c, n, s, h, w, across):
        return c + w * ((n + s) + (across + jnp.where(edge, h, 0.0)) - 4.0 * c)

    def coef_row(r):
        at = jnp.where(r < 0, 0, r + 8)
        return coef[pl.ds(at, 1), :]

    def several(i, carry):
        chosen = [i * UNROLL + k for k in range(UNROLL)]
        spot = [hub_row[h] for h in chosen]
        u = [[field_row(r + k) for k in range(-2, 3)] for r in spot]
        across = lateral([u[k][c] for k in range(UNROLL) for c in (1, 2, 3)])
        v = []
        for k, r in enumerate(spot):
            v.append([
                relax(u[k][c + 2], u[k][c + 1], u[k][c + 3], side_row(r + c), coef_row(r + c), across[3 * k + c + 1])
                for c in range(-1, 2)])
        across = lateral([x[1] for x in v])
        for k, (h, r) in enumerate(zip(chosen, spot)):
            moved = share[h] * relax(v[k][1], v[k][0], v[k][2], halo_row(halo1, r), coef_row(r), across[k])
            to = dest_tile[h]
            n = counts[to]
            counts[to] = n + 1
            base = pl.multiple_of(to * stride, 16)
            sent[pl.ds(pl.multiple_of(base + n * members, 16), members), :] = moved.astype(BF16)
            at = pl.ds(pl.multiple_of(base + CAP * members, 16), TAGS)
            tags = sent[at, :].astype(F32)
            tags = jnp.where(tag_lane == n, dest_row[h].astype(F32), tags)
            tags = jnp.where(tag_lane == CAP + n, county[h].astype(F32), tags)
            sent[at, :] = tags.astype(BF16)
        return carry

    lax.fori_loop(0, hub_row.shape[0] // UNROLL, several, 0)


def grow_kernel(draw, threshold, grow, draw_v, grow_v, limit_v, in_sem, out_sem, sem):
    chunk = draw.shape[0] // GROW
    limit = pltpu.make_async_copy(threshold, limit_v, sem)
    limit.start()

    def fetch(i, carry):
        at = pl.ds(i * chunk, chunk)
        pltpu.make_async_copy(draw.at[at], draw_v.at[at], in_sem.at[i]).start()
        return carry

    lax.fori_loop(0, GROW, fetch, 0)
    limit.wait()

    def work(i, carry):
        at = pl.ds(i * chunk, chunk)
        pltpu.make_async_copy(draw.at[at], draw_v.at[at], in_sem.at[i]).wait()
        for k in range(chunk):
            x = 0.5 * SHARPNESS * (draw_v[i * chunk + k].astype(F32) - limit_v[...])
            grow_v[i * chunk + k] = 0.5 * jnp.tanh(x) + 0.5
        pltpu.make_async_copy(grow_v.at[at], grow.at[at], out_sem).start()
        return carry

    lax.fori_loop(0, GROW, work, 0)
    pltpu.make_async_copy(grow_v, grow, out_sem).wait()


def bulk_kernel(
    hub_row, share, density, grow, coef, strips, near, halo1, beside,
    kept, field, inner, gate, factor, in_sem, gate_sem, out_sem,
):
    members, rows, cols = density.shape
    half = rows // 2
    step = STEP
    blocks = rows // step

    def fetch(i, carry):
        for k in range(step):
            r = i * step + k
            pltpu.make_async_copy(density.at[:, r, :], field.at[r + 2], in_sem.at[i]).start()
        return carry

    def fetch_gate(i, carry):
        for k in range(step):
            r = i * step + k
            pltpu.make_async_copy(grow.at[:, r, :], gate.at[r], gate_sem.at[i]).start()
        return carry

    lax.fori_loop(0, blocks, fetch, 0)
    lax.fori_loop(0, blocks, fetch_gate, 0)
    for k in range(2):
        field[k] = strips[k]
        field[rows + 2 + k] = strips[2 + k]

    def clear(i, carry):
        for k in range(8):
            factor[i * 8 + k] = 1.0
        return carry

    lax.fori_loop(0, rows // 8, clear, 0)

    def leave(h, carry):
        r = hub_row[h]
        factor[r] = factor[r] - share[h]
        return carry

    lax.fori_loop(0, hub_row.shape[0], leave, 0)

    side = (members, cols)
    lane = lanes(side)
    first, last = lane == 0, lane == cols - 1

    edge = jnp.logical_or(first, last)
    band = (cols, cols)
    beside_mask = (jnp.abs(lanes(band) - sublanes(band)) == 1).astype(BF16)
    beside_mask = jnp.concatenate([beside_mask, beside_mask], axis=0)

    def lateral(c):
        flat = c.reshape(-1, cols)
        high = flat.astype(BF16)
        low = (flat - high.astype(F32)).astype(BF16)
        parts = jnp.concatenate([high, low], axis=1)
        return jnp.dot(parts, beside_mask, preferred_element_type=F32).reshape(c.shape)

    def relax(c, n, s, h, w, across):
        return c + w * ((n + s) + (across + jnp.where(edge, h, 0.0)) - 4.0 * c)

    def halo_row(ref, part, r):
        at = pl.ds(pl.multiple_of(part * members, 8), members)
        return pltpu.roll(ref[at, :], cols - 1 - 2 * (r - part * half), 1)

    def landed(i):
        ready = field.at[pl.ds(i * step + 2, step)]
        pltpu.make_async_copy(ready, ready, in_sem.at[i]).wait()

    landed(0)
    inner[0] = relax(field[1], field[0], field[2], beside[:members, :], coef[0:1, :], lateral(field[1]))

    def early(i, carry):
        @pl.when(i < blocks - 1)
        def _():
            landed(i + 1)

        part = i // (half // step)
        across = lateral(field[pl.ds(i * step + 2, step)])
        for k in range(step):
            r = i * step + k
            inner[r + 1] = relax(
                field[r + 2], field[r + 1], field[r + 3], halo_row(near, part, r), coef[pl.ds(r + 8, 1), :], across[k])
        return carry

    lax.fori_loop(0, blocks, early, 0)
    inner[rows + 1] = relax(
        field[rows + 2], field[rows + 1], field[rows + 3], beside[3 * members:, :], coef[rows + 8:rows + 9, :],
        lateral(field[rows + 2]))

    def late(i, carry):
        ready = gate.at[pl.ds(i * step, step)]
        pltpu.make_async_copy(ready, ready, gate_sem.at[i]).wait()
        part = i // (half // step)
        across = lateral(inner[pl.ds(i * step + 1, step)])
        for k in range(step):
            r = i * step + k
            d = relax(
                inner[r + 1], inner[r], inner[r + 2], halo_row(halo1, part, r), coef[pl.ds(r + 8, 1), :], across[k])
            gate[r] = d * factor[r] * gate[r]
        for k in range(step):
            r = i * step + k
            pltpu.make_async_copy(gate.at[r], kept.at[:, r, :], out_sem).start()
        return carry

    lax.fori_loop(0, blocks, late, 0)
    pltpu.make_async_copy(gate, gate, out_sem).wait()


def land_kernel(place, landed, kept, grow, *rest):
    blocks, rest = rest[:-13], rest[-13:]
    out, table, base, gate, carried, tags_v, tags_s, owner, lead, final, tag_sem, row_sem, out_sem = rest
    per = blocks[0].shape[0]
    bands, cols = tags_v.shape
    stride = landed.shape[0] // bands
    members, rows, _ = kept.shape
    depth = table.shape[1] - TAGS
    slots = bands * CAP
    for t in range(bands):
        tags = landed[t * stride + CAP * members:(t + 1) * stride, :].astype(F32)
        tags_v[t:t + 1, :] = tags[:1].astype(jnp.int32)
    copy = pltpu.make_async_copy(tags_v, tags_s, tag_sem)
    copy.start()
    for d, ref in enumerate(blocks):
        at = jnp.bitwise_xor(place[3], d) * per
        for c in range(per):
            table[at + c] = ref[c]

    def clear(r, carry):
        for k in range(8):
            owner[r * 8 + k] = -1
        return carry

    lax.fori_loop(0, rows // 8, clear, 0)
    copy.wait()

    def fetch(row, s):
        return (pltpu.make_async_copy(out.at[:, row, :], base.at[s], row_sem),
                pltpu.make_async_copy(grow.at[:, row, :], gate.at[s], row_sem))

    def store(row, s):
        return pltpu.make_async_copy(base.at[s], out.at[:, row, :], out_sem)

    def claim(s, count):
        row = tags_s[s // CAP, s % CAP]
        at = jnp.maximum(row, 0)
        mine = owner[at]
        fresh = jnp.logical_and(row >= 0, mine < 0)
        leader = jnp.where(row < 0, slots, jnp.where(mine < 0, s, mine))
        lead[s] = leader
        final[leader] = s

        @pl.when(fresh)
        def _():
            owner[at] = s
            for c in fetch(at, s):
                c.start()

        return count + jnp.where(fresh, 1, 0)

    count = lax.fori_loop(0, slots, claim, 0)
    final[slots] = -1

    def product(t, carry):
        for n in range(CAP):
            c = jnp.maximum(tags_s[t, CAP + n], 0)
            at = pl.ds(pl.multiple_of(t * stride + n * members, 16), members)
            x = jnp.dot(landed[at, :], table[c, :depth, :], preferred_element_type=F32)
            scale = table[c, depth:, :].astype(F32)[:1]
            carried[t * CAP + n] = (x * scale).astype(BF16).astype(F32)
        return carry

    lax.fori_loop(0, bands, product, 0, unroll=8)

    def arrive(s, carry):
        for c in fetch(0, 0):
            c.wait()
        return carry

    lax.fori_loop(0, count, arrive, 0)

    def add(t, carry):
        for n in range(CAP):
            to = lead[t * CAP + n]
            base[to] = base[to] + carried[t * CAP + n] * gate[to]
        for n in range(CAP):
            to = lead[t * CAP + n]

            @pl.when(final[to] == t * CAP + n)
            def _():
                store(tags_s[t, n], to).start()

        return carry

    lax.fori_loop(0, bands, add, 0)

    def finish(s, carry):
        store(0, 0).wait()
        return carry

    lax.fori_loop(0, count, finish, 0)


def smem():
    return pl.BlockSpec(memory_space=pltpu.SMEM)


def vmem():
    return pl.BlockSpec(memory_space=pltpu.VMEM)


def anywhere():
    return pl.BlockSpec(memory_space=pl.ANY)


def hbm():
    return pl.BlockSpec(memory_space=pltpu.HBM)


def params(mib):
    return pltpu.CompilerParams(vmem_limit_bytes=int(mib * MIB))


def near_pairs(count):
    return [(i, i ^ 1) for i in range(count)]


def far_pairs(count):
    return [(i, j) for k in range(1, count - 1, 2) for i, j in ((k, k + 1), (k + 1, k))]


def local(
    density,
    habitat_class,
    suitability,
    dispersal_draw,
    threshold,
    hub_row,
    dest_tile,
    dest_row,
    county_id,
    jump_share,
    flow_tiles,
    flow_scale,
):
    members, rows, cols = density.shape
    bands, flows = lax.axis_size("tile"), lax.axis_size("flow")
    flow_scale = flow_scale.reshape(1, -1)
    density, dispersal_draw, habitat_class, flow_tiles, suitability, flow_scale, threshold = (
        pltpu.with_memory_space_constraint(x, pltpu.HBM)
        for x in (density, dispersal_draw, habitat_class, flow_tiles, suitability, flow_scale, threshold))
    t, f = lax.axis_index("tile"), lax.axis_index("flow")
    place = jnp.stack([t % 2, f % 2, t, f]).astype(jnp.int32)
    hubs, share = hub_row.reshape(-1), jump_share.reshape(-1)
    sds = jax.ShapeDtypeStruct
    per, depth = flow_tiles.shape[:2]
    message = sds((2 * members + TAIL, cols), BF16)
    pack = sds((2 * members, cols), F32)
    cols_a, cols_b, rows_a, rows_b, own, weight, tiles, turned = pl.pallas_call(
        edges_kernel,
        out_shape=(message, message, message, message, pack, sds((rows, cols), F32),
                   sds((per, depth + TAGS, cols), BF16), sds((rows, members, cols), F32)),
        in_specs=[smem()] + [hbm()] * 5,
        out_specs=(vmem(),) * 8,
        scratch_shapes=[
            pltpu.VMEM(pack.shape, F32),
            pltpu.VMEM(pack.shape, F32),
            pltpu.VMEM((rows, cols), jnp.int32),
            pltpu.SMEM(suitability.shape, F32),
            pltpu.VMEM((1, per), BF16),
            pltpu.SemaphoreType.DMA((rows // CHUNK,)),
            pltpu.SemaphoreType.DMA((4,)),
        ],
        compiler_params=params(24),
        name="edges",
    )(place, density, habitat_class, suitability, flow_tiles, flow_scale)

    got_a = lax.ppermute(cols_a, "flow", near_pairs(flows))
    got_b = lax.ppermute(cols_b, "flow", far_pairs(flows))
    rows_a, rows_b = pl.pallas_call(
        corners_kernel,
        out_shape=(message, message),
        in_specs=[smem()] + [vmem()] * 4,
        out_specs=(vmem(), vmem()),
        compiler_params=params(24),
        name="corners",
    )(place, rows_a, rows_b, got_a, got_b)
    rows_a, rows_b, dispersal_draw = lax.optimization_barrier((rows_a, rows_b, dispersal_draw))
    strip_a = lax.ppermute(rows_a, "tile", near_pairs(bands))
    strip_b = lax.ppermute(rows_b, "tile", far_pairs(bands))

    def swap(x, bit):
        return lax.ppermute(x, "flow", [(i, i ^ bit) for i in range(flows)])

    grow = pl.pallas_call(
        grow_kernel,
        out_shape=pltpu.HBM(density.shape, F32),
        in_specs=[hbm(), hbm()],
        out_specs=hbm(),
        scratch_shapes=[
            pltpu.VMEM(density.shape, BF16),
            pltpu.VMEM(density.shape, F32),
            pltpu.VMEM((rows, cols), F32),
            pltpu.SemaphoreType.DMA((GROW,)),
            pltpu.SemaphoreType.DMA,
            pltpu.SemaphoreType.DMA,
        ],
        compiler_params=params(24),
        name="grow",
    )(dispersal_draw, threshold)
    grow = pltpu.with_memory_space_constraint(grow, pltpu.HBM)

    blocks = [tiles] + [swap(tiles, d) for d in range(1, flows)]
    turned, grow = lax.optimization_barrier((turned, grow))

    stride = CAP * members + TAGS
    sent, near, halo1, beside, coef, strips = pl.pallas_call(
        hubs_kernel,
        out_shape=(sds((bands * stride, cols), BF16), pack, pack, sds((4 * members, cols), F32),
                   sds((rows + 16, cols), F32), sds((4, members, cols), F32)),
        in_specs=[smem()] * 6 + [vmem()] * 7,
        out_specs=(vmem(),) * 6,
        scratch_shapes=[pltpu.SMEM((bands,), jnp.int32)],
        compiler_params=params(24),
        name="hubs",
    )(place, hubs, dest_tile.reshape(-1), dest_row.reshape(-1), county_id.reshape(-1), share,
      turned, weight, own, got_a, got_b, strip_a, strip_b)

    landed = lax.all_to_all(sent, "tile", split_axis=0, concat_axis=0, tiled=True)
    kept = pl.pallas_call(
        bulk_kernel,
        out_shape=sds(density.shape, F32),
        in_specs=[smem(), smem(), hbm(), hbm()] + [vmem()] * 5,
        out_specs=hbm(),
        scratch_shapes=[
            pltpu.VMEM((rows + 4, members, cols), F32),
            pltpu.VMEM((rows + 2, members, cols), F32),
            pltpu.VMEM((rows, members, cols), F32),
            pltpu.SMEM((rows,), F32),
            pltpu.SemaphoreType.DMA((rows // STEP,)),
            pltpu.SemaphoreType.DMA((rows // STEP,)),
            pltpu.SemaphoreType.DMA,
        ],
        compiler_params=params(24),
        name="bulk",
    )(hubs, share, density, grow, coef, strips, near, halo1, beside)

    slots = bands * CAP
    out = pl.pallas_call(
        land_kernel,
        out_shape=sds(density.shape, F32),
        in_specs=[smem(), vmem(), hbm(), hbm()] + [vmem()] * flows,
        out_specs=hbm(),
        input_output_aliases={2: 0},
        scratch_shapes=[
            pltpu.VMEM((flows * per, depth + TAGS, cols), BF16),
            pltpu.VMEM((slots + 1, members, cols), F32),
            pltpu.VMEM((slots + 1, members, cols), F32),
            pltpu.VMEM((slots, members, cols), F32),
            pltpu.VMEM((bands, cols), jnp.int32),
            pltpu.SMEM((bands, cols), jnp.int32),
            pltpu.SMEM((rows,), jnp.int32),
            pltpu.SMEM((slots,), jnp.int32),
            pltpu.SMEM((slots + 1,), jnp.int32),
            pltpu.SemaphoreType.DMA,
            pltpu.SemaphoreType.DMA,
            pltpu.SemaphoreType.DMA,
        ],
        compiler_params=params(24),
        name="land",
    )(place, landed, kept, grow, *blocks)
    return out


def solution(mesh):
    in_specs = (
        P(None, "tile", "flow"),
        P("tile", "flow"),
        P(),
        P(None, "tile", "flow"),
        P("tile", "flow"),
        P("flow", "tile"),
        P("flow", "tile", None),
        P("flow", "tile"),
        P("flow", "tile"),
        P("flow", "tile"),
        P("flow", None, None),
        P("flow"),
    )
    out_specs = P(None, "tile", "flow")
    return jax.shard_map(local, mesh=mesh, in_specs=in_specs, out_specs=out_specs, check_vma=False)
```
